256 devices in a mesh: pair: 16 (over z, x_lo), side: 2 (over core), tp: 8 (over y, x_hi).
Axes of the slice: x: 4 (x_hi: 2, x_lo: 2; x = x_hi * 2 + x_lo), y: 4, z: 8, core: 2. Of those that a mesh axis runs over, the one named last changes fastest.
Arguments:
- segment_queries: bfloat16 [16, 1024, 8192], P('pair', 'side', 'tp'), may hold values from -60 to 60
- segment_kv: bfloat16 [16, 1024, 2048], P('pair', 'side', 'tp'), may hold values from -6 to 6
- prefix_kv: bfloat16 [16, 1024, 2048], P('pair', None, 'tp'), may hold values from -8 to 8
- kv_cache: bfloat16 [16, 7, 2048, 2048], P('pair', None, ('side', 'tp')), may hold values from -8 to 8
- decode_queries: bfloat16 [16, 4, 8, 8192], P('pair'), may hold values from -60 to 60
- decode_kv: bfloat16 [16, 4, 8, 2048], P('pair'), may hold values from -6 to 6
- matching: int32 [16], replicated, may hold values from 0 to 15, each once
- segment_starts: int32 [16], replicated, may hold values from 2 to 1024, as said below
- cache_lengths: int32 [16, 7], P('pair'), may hold values from 2 to 2048, as said below
Outputs:
- prompt_out: bfloat16 [16, 1024, 8192], P('pair', 'side', 'tp')
- decode_out: bfloat16 [16, 4, 8, 8192], P('pair', None, None, ('side', 'tp'))
The draws below stay inside these ranges and needn't reach their ends.
Inputs may be any that keep to these rules, and one draw needn't show every extreme that they name: `matching`: each group index appears once. `segment_starts`: the largest entry equals 1024. `cache_lengths`: the largest entry equals 2048.
All inputs are finite; a program needn't handle non-finite values.
Results may differ from the reference program's by a relative error of at most 0.0075.
Values may be sent and summed in bfloat16 or wider, within the bound.
No kernel may reach another device: no remote copies, remote signals or barrier semaphores. Data moves between devices by JAX's collectives and lax.ppermute only.
A program may use at most 128 MiB of HBM per device.

```python
import math
import jax
import jax.numpy as jnp
from jax import lax

H = 64
KVH = 8
HD = 128
SEGMENT = 1024
PREFIX = 1024
CACHE = 2048
NR = 8
STEPS = 4
GROUPS = 16


def draw_segment_queries(key, part):
    key = jax.random.fold_in(key, 11)
    first_key = jax.random.fold_in(key, 0)
    full_shape = (GROUPS, SEGMENT, H, HD)
    values = jax.random.truncated_normal(first_key, -6.0, 6.0, full_shape, jnp.float32)
    return values.reshape(GROUPS, SEGMENT, H * HD).astype(jnp.bfloat16)


def draw_decode_queries(key, part):
    key = jax.random.fold_in(key, 19)
    first_key = jax.random.fold_in(key, 0)
    full_shape = (GROUPS, STEPS, NR, H, HD)
    values = jax.random.truncated_normal(first_key, -6.0, 6.0, full_shape, jnp.float32)
    return values.reshape(GROUPS, STEPS, NR, H * HD).astype(jnp.bfloat16)


def draw_prefix_kv(key, part):
    key = jax.random.fold_in(key, 13)
    first_key = jax.random.fold_in(key, 0)
    full_shape = (GROUPS, PREFIX, KVH, 2, HD)
    values = jax.random.truncated_normal(first_key, -6.0, 6.0, full_shape, jnp.float32)
    return values.reshape(GROUPS, PREFIX, KVH * 2 * HD).astype(jnp.bfloat16)


def draw_kv_cache(key, part):
    key = jax.random.fold_in(key, 17)
    first_key = jax.random.fold_in(key, 0)
    full_shape = (GROUPS, NR - 1, CACHE, KVH, 2, HD)
    values = jax.random.truncated_normal(first_key, -6.0, 6.0, full_shape, jnp.float32)
    return values.reshape(GROUPS, NR - 1, CACHE, KVH * 2 * HD).astype(jnp.bfloat16)


def draw_segment_starts(key, part):
    key = jax.random.fold_in(key, 23)
    first_key, second_key = jax.random.split(key, 2)
    drawn = jax.random.randint(first_key, (GROUPS,), 2, PREFIX + 1)
    target = jax.random.randint(second_key, (), 0, GROUPS)
    return jnp.where(jnp.arange(GROUPS) == target, PREFIX, drawn).astype(jnp.int32)


def draw_cache_lengths(key, part):
    key = jax.random.fold_in(key, 29)
    first_key, second_key = jax.random.split(key, 2)
    entries = GROUPS * (NR - 1)
    drawn = jax.random.randint(first_key, (entries,), 2, CACHE + 1)
    target = jax.random.randint(second_key, (), 0, entries)
    return jnp.where(jnp.arange(entries) == target, CACHE, drawn).reshape(GROUPS, NR - 1).astype(jnp.int32)


def block_levels(rng, shape, shards, least, high):
    def one(dim, parts):
        steps = jax.random.uniform(jax.random.fold_in(jax.random.fold_in(rng, 6), dim), (parts,), jnp.float32, least / len(shards), high / len(shards))
        return jnp.repeat(jnp.exp(steps), shape[dim] // parts).reshape((-1,) + (1,) * (len(shape) - dim - 1))

    loudness = one(*shards[0])
    for cut in shards[1:]:
        loudness = loudness * one(*cut)
    return loudness


def noise(stream_key, shape, width, limit, shards=(), kind=jnp.bfloat16):
    loudness = block_levels(stream_key, shape, shards, -0.22, 0.18) if shards else 1.0
    result = jax.random.normal(stream_key, shape, jnp.float32) * width * loudness
    return jnp.minimum(jnp.maximum(result, -limit), limit).astype(kind)


def setup_inputs(seed: int = 0) -> dict:
    key_of = jax.random.split(jax.random.key(seed), 10)
    return {
        "segment_queries": draw_segment_queries(jax.random.fold_in(key_of[9], 71), 0),
        "segment_kv": noise(key_of[1], (GROUPS, SEGMENT, 2 * KVH * HD), 1.0, 6.0, ((0, 16), (1, 2), (2, 8))),
        "prefix_kv": draw_prefix_kv(jax.random.fold_in(key_of[9], 71), 0),
        "kv_cache": draw_kv_cache(jax.random.fold_in(key_of[9], 71), 0),
        "decode_queries": draw_decode_queries(jax.random.fold_in(key_of[9], 71), 0),
        "decode_kv": noise(key_of[5], (GROUPS, STEPS, NR, 2 * KVH * HD), 1.0, 6.0, ((0, 16),)),
        "matching": jax.random.permutation(key_of[6], GROUPS).astype(jnp.int32),
        "segment_starts": draw_segment_starts(jax.random.fold_in(key_of[9], 71), 0),
        "cache_lengths": draw_cache_lengths(jax.random.fold_in(key_of[9], 71), 0),
    }


NEG_FILL = -1e+30

def softmax_terms(scores, allowed):
    masked = jnp.where(allowed, scores, NEG_FILL)
    highest = lax.optimization_barrier(jnp.max(masked, axis=-1, keepdims=True))
    weights = jnp.where(allowed, jnp.exp(masked - highest), 0.0)
    totals = lax.optimization_barrier(jnp.sum(weights, axis=-1))
    return (weights.astype(jnp.bfloat16), totals)

def prompt_group(operands):
    queries, segment, prefix, first_new = operands
    keys_all = jnp.concatenate([prefix, segment], axis=0).reshape(PREFIX + SEGMENT, KVH, 2, HD)
    query_pos = jnp.arange(SEGMENT, dtype=jnp.int32)
    key_pos = jnp.arange(PREFIX + SEGMENT, dtype=jnp.int32)
    allowed = jnp.where(key_pos[None, :] < PREFIX, key_pos[None, :] < first_new, key_pos[None, :] - PREFIX <= query_pos[:, None])
    grouped = queries.reshape(SEGMENT, KVH, H // KVH, HD)
    factor = 1.0 / math.sqrt(HD)

    def per_head(kv_head):
        query_block = lax.dynamic_index_in_dim(grouped, kv_head, 1, keepdims=False).astype(jnp.float32)
        pair_kv = lax.dynamic_index_in_dim(keys_all, kv_head, 1, keepdims=False).astype(jnp.float32)
        scores = jnp.einsum('qgd,kd->qgk', query_block, pair_kv[:, 0]) * factor
        weights, totals = softmax_terms(scores, allowed[:, None, :])
        mixture = jnp.einsum('qgk,kd->qgd', weights.astype(jnp.float32), pair_kv[:, 1])
        return (mixture / totals[..., None]).astype(jnp.bfloat16)
    heads_out = lax.map(per_head, jnp.arange(KVH, dtype=jnp.int32))
    return jnp.transpose(heads_out, (1, 0, 2, 3)).reshape(SEGMENT, H * HD)

def decode_row(queries, keys_kv, allowed, fresh_kv):
    key_count = keys_kv.shape[0]
    joined = jnp.concatenate([keys_kv, fresh_kv], axis=0).reshape(key_count + STEPS, KVH, 2, HD).astype(jnp.float32)
    step_ids = jnp.arange(STEPS, dtype=jnp.int32)
    causal = step_ids[None, :] <= step_ids[:, None]
    allowed_all = jnp.concatenate([jnp.broadcast_to(allowed[None, :], (STEPS, key_count)), causal], axis=1)
    grouped = queries.reshape(STEPS, KVH, H // KVH, HD).astype(jnp.float32)
    scores = jnp.einsum('scgd,jcd->scgj', grouped, joined[:, :, 0]) * (1.0 / math.sqrt(HD))
    weights, totals = softmax_terms(scores, allowed_all[:, None, None, :])
    mixture = jnp.einsum('scgj,jcd->scgd', weights.astype(jnp.float32), joined[:, :, 1])
    return (mixture / totals[..., None]).astype(jnp.bfloat16).reshape(STEPS, H * HD)

def decode_group(operands):
    queries, fresh_kv, cache_rows, lengths, prompt_kv, prompt_len = operands
    prompt_pos = jnp.arange(PREFIX + SEGMENT, dtype=jnp.int32)
    first_row = decode_row(queries[:, 0], prompt_kv, (prompt_pos >= PREFIX) | (prompt_pos < prompt_len), fresh_kv[:, 0])
    cache_pos = jnp.arange(CACHE, dtype=jnp.int32)

    def running_row(row_queries, row_cache, row_length, row_fresh):
        return decode_row(row_queries, row_cache, cache_pos < row_length, row_fresh)
    others = jax.vmap(running_row, in_axes=(1, 0, 0, 1), out_axes=1)(queries[:, 1:], cache_rows, lengths, fresh_kv[:, 1:])
    return jnp.concatenate([first_row[:, None], others], axis=1)

def reference(segment_queries, segment_kv, prefix_kv, kv_cache, decode_queries, decode_kv, matching, segment_starts, cache_lengths):
    prompt_out = lax.map(prompt_group, (segment_queries, segment_kv, prefix_kv, segment_starts))
    indices = jnp.arange(GROUPS, dtype=jnp.int32)
    inverse = lax.optimization_barrier(jnp.sum(jnp.where(matching[:, None] == indices[None, :], indices[:, None], 0), axis=0)).astype(jnp.int32)
    prompts = jnp.take(jnp.concatenate([prefix_kv, segment_kv], axis=1), inverse, axis=0)
    starts = jnp.take(segment_starts, inverse, axis=0)
    decode_out = lax.map(decode_group, (decode_queries, decode_kv, kv_cache, cache_lengths, prompts, starts))
    return (prompt_out, decode_out)
```

```python
import functools
import math

import jax
import jax.numpy as jnp
from jax import lax
from jax.experimental import pallas as pl
from jax.experimental.pallas import tpu as pltpu
from jax.sharding import PartitionSpec as P

H = 64
KVH = 8
HD = 128
STEPS = 4
ROWS = 8
GROUPS = 16
BLOCKS = 16
SEG_HALF = 512
PREFIX = 1024
CACHE_BLOCK = 128

FACTOR = 1.0 / math.sqrt(HD)
LOG2E = 1.4426950408889634
NEG_FILL = -1e30
PART_ROWS = 144

f32 = jnp.float32
bf16 = jnp.bfloat16


def params(**kw):
    return pltpu.CompilerParams(vmem_limit_bytes=60 * 1024 * 1024, **kw)


def whole(shape):
    return pl.BlockSpec(shape, lambda *_: (0,) * len(shape))


def dot_t(a, b):
    return lax.dot_general(a, b, (((1,), (1,)), ((), ())), preferred_element_type=f32)


def dot(a, b):
    return jnp.dot(a, b, preferred_element_type=f32)


def prep_kernel(q_ref, kv_ref, out_ref):
    side = lax.axis_index("side")
    tp = lax.axis_index("tp")
    q_col = pl.multiple_of((2 * tp + side) * 512, 512)
    kv_col = pl.multiple_of(tp * 256, 256)
    q = q_ref[0, :, :, pl.ds(q_col, 512)].astype(f32)
    kv = kv_ref[0, :, :, pl.ds(kv_col, 256)].astype(f32)
    rows = [q[t, 0:1, h * HD : (h + 1) * HD] for t in range(STEPS) for h in range(4)]
    pad = [jnp.zeros((4, HD), f32)]
    rows += [kv[u, 0:1, :HD] for u in range(STEPS)] + pad
    rows += [kv[u, 0:1, HD:] for u in range(STEPS)] + pad
    sent = jnp.concatenate(rows, axis=0).astype(bf16)
    for p in range(GROUPS):
        out_ref[p] = sent


def prep(decode_queries, decode_kv):
    shape = (GROUPS, 32, HD)
    return pl.pallas_call(
        prep_kernel,
        out_shape=jax.ShapeDtypeStruct(shape, bf16),
        grid=(1,),
        in_specs=[whole(decode_queries.shape), whole(decode_kv.shape)],
        out_specs=whole(shape),
        compiler_params=params(),
        cost_estimate=pl.CostEstimate(flops=10000, bytes_accessed=800000, transcendentals=0),
        name="prep",
    )(decode_queries, decode_kv)


def decode_kernel(len_ref, q_ref, cache_ref, after_ref, out_ref):
    block = lax.axis_index("side") * 8 + lax.axis_index("tp")
    sub = lax.broadcasted_iota(jnp.int32, (ROWS, HD), 0)
    lane = lax.broadcasted_iota(jnp.int32, (ROWS, HD), 1)
    lens = jnp.zeros((ROWS, HD), jnp.int32)
    for k in range(ROWS - 1):
        lens = jnp.where(sub == k + 1, len_ref[0, k], lens)
    allowed = (block * CACHE_BLOCK + lane < lens)[None]
    tiles = STEPS * 8
    small = lane % 32
    for head in range(2):
        key = slice(head * 256, head * 256 + HD)
        value = slice(head * 256 + HD, head * 256 + 256)
        q = jnp.concatenate(
            [
                q_ref[0, t, :, (head * 8 + g) * HD : (head * 8 + g + 1) * HD].astype(f32)
                for t in range(STEPS)
                for g in range(8)
            ],
            axis=0,
        ).astype(bf16)
        scores = jnp.zeros((tiles, ROWS, HD), f32)
        for k in range(0, ROWS - 1, 2):
            n = min(2, ROWS - 1 - k)
            part = dot_t(q, cache_ref[0, k : k + n, :, key].reshape(n * CACHE_BLOCK, HD))
            for e in range(n):
                one = part[:, e * HD : (e + 1) * HD].reshape(tiles, ROWS, HD)
                scores = jnp.where((sub == k + e + 1)[None], one, scores)
        scores = jnp.where(allowed, scores * FACTOR, NEG_FILL)
        peak = jnp.max(scores, axis=-1, keepdims=True)
        weights = jnp.where(allowed, jnp.exp(scores - peak), 0.0)
        totals = jnp.sum(weights, axis=-1, keepdims=True)
        wide = jnp.concatenate(
            [
                jnp.where((sub == k + 1)[None], weights, 0.0).reshape(tiles * ROWS, HD).astype(bf16)
                for k in range(ROWS - 1)
            ],
            axis=1,
        )
        values = cache_ref[0, :, :, value].reshape((ROWS - 1) * CACHE_BLOCK, HD)
        mix = dot(wide, values).reshape(STEPS, 8, ROWS, HD)
        peak = peak.reshape(STEPS, 8, ROWS, 1)
        totals = totals.reshape(STEPS, 8, ROWS, 1)
        for half in range(2):
            stats = jnp.zeros((ROWS, HD), f32)
            for t in range(STEPS):
                for h in range(4):
                    j = t * 4 + h
                    stats = jnp.where(small == j, peak[t, half * 4 + h], stats)
                    stats = jnp.where(small == 16 + j, totals[t, half * 4 + h], stats)
            high = stats.astype(bf16).astype(f32)
            rest = stats - high
            mid = rest.astype(bf16).astype(f32)
            low = rest - mid
            packed = jnp.where(lane < 32, high, jnp.where(lane < 64, mid, low))
            slot = head * 2 + half
            out_ref[slot, 0:128] = mix[:, half * 4 : half * 4 + 4].reshape(128, HD).astype(bf16)
            out_ref[slot, 128:144] = jnp.concatenate(
                [packed, jnp.zeros((ROWS, HD), f32)], axis=0
            ).astype(bf16)


def decode_parts(cache_lengths, decode_queries, kv_cache, after):
    return pl.pallas_call(
        decode_kernel,
        out_shape=jax.ShapeDtypeStruct((BLOCKS, PART_ROWS, HD), bf16),
        grid_spec=pltpu.PrefetchScalarGridSpec(
            num_scalar_prefetch=1,
            grid=(KVH // 2,),
            in_specs=[
                pl.BlockSpec((1, STEPS, ROWS, 2048), lambda c, *_: (0, 0, 0, c)),
                pl.BlockSpec((1, ROWS - 1, CACHE_BLOCK, 512), lambda c, *_: (0, 0, 0, c)),
                pl.BlockSpec(memory_space=pl.ANY),
            ],
            out_specs=pl.BlockSpec((4, PART_ROWS, HD), lambda c, *_: (c, 0, 0)),
        ),
        compiler_params=params(),
        cost_estimate=pl.CostEstimate(
            flops=2000000000, bytes_accessed=4800000, transcendentals=300000
        ),
        name="decode_parts",
    )(cache_lengths, decode_queries, kv_cache, after)


def prompt_kernel(index, heads, start_ref, q_ref, prefix_ref, own_ref, other_ref, *rest):
    out_ref, mixed, least = rest[-3:]
    side = lax.axis_index("side")
    start = start_ref[lax.axis_index("pair")]
    tokens = 256
    own_keys = (index + 1) * tokens
    scale = FACTOR * LOG2E

    pos = lax.broadcasted_iota(jnp.int32, (PREFIX, 2 * HD), 0)
    wide = jnp.concatenate([prefix_ref[0, :, HD:], jnp.ones((PREFIX, HD), bf16)], axis=1)
    mixed[SEG_HALF : SEG_HALF + PREFIX] = jnp.where(pos < start, wide.astype(f32), 0.0).astype(bf16)
    ones = jnp.ones((SEG_HALF, HD), bf16)
    mixed[:SEG_HALF] = jnp.concatenate([other_ref[0, :, HD:], ones], axis=1)
    mixed[SEG_HALF + PREFIX :] = jnp.concatenate([own_ref[0, :, HD:], ones], axis=1)
    least[...] = jnp.ones(least.shape, f32)

    def norm(ref):
        k = ref[0, :, :HD].astype(f32)
        return jnp.max(jnp.sum(k * k, axis=-1, keepdims=True), axis=0, keepdims=True)

    longest = jnp.maximum(norm(prefix_ref), jnp.maximum(norm(own_ref), norm(other_ref)))
    causal = lax.broadcasted_iota(jnp.int32, (tokens, tokens), 1) <= lax.broadcasted_iota(
        jnp.int32, (tokens, tokens), 0
    )

    def key_parts(later):
        parts = []
        if later:
            parts += [(other_ref, n) for n in range(0, SEG_HALF, 256)]
        parts += [(prefix_ref, n) for n in range(0, PREFIX, 256)]
        parts += [(own_ref, n) for n in range(0, own_keys, 256)]
        return parts

    def one_head(g, later):
        col = pl.ds(pl.multiple_of(g * HD, HD), HD)
        q = q_ref[0, :, col]
        wide_q = q.astype(f32)
        bound = jnp.sqrt(jnp.sum(wide_q * wide_q, axis=-1, keepdims=True) * longest) * scale
        parts = key_parts(later)
        weights = []
        for number, (ref, n) in enumerate(parts):
            w = jnp.exp2(dot_t(q, ref[0, n : n + 256, :HD]) * scale - bound)
            if number == len(parts) - 1:
                w = jnp.where(causal, w, 0.0)
            weights.append(w.astype(bf16))
        first = 0 if later else SEG_HALF
        total = dot(
            jnp.concatenate(weights, axis=1), mixed[first : SEG_HALF + PREFIX + own_keys]
        )
        sums = total[:, HD:]
        out_ref[0, :, col] = (total[:, :HD] / sums).astype(bf16)
        least[...] = jnp.minimum(least[...], sums)

    def one_head_exact(g, later):
        col = pl.ds(pl.multiple_of(g * HD, HD), HD)
        q = q_ref[0, :, col]
        parts = key_parts(later)
        scores = []
        for number, (ref, n) in enumerate(parts):
            s = dot_t(q, ref[0, n : n + 256, :HD])
            if ref is prefix_ref:
                at = n + lax.broadcasted_iota(jnp.int32, s.shape, 1)
                s = jnp.where(at < start, s, NEG_FILL)
            if number == len(parts) - 1:
                s = jnp.where(causal, s, NEG_FILL)
            scores.append(s)
        peak = functools.reduce(
            jnp.maximum, [jnp.max(s, axis=-1, keepdims=True) for s in scores]
        )
        weights = [jnp.exp2((s - peak) * scale).astype(bf16) for s in scores]
        first = 0 if later else SEG_HALF
        total = dot(
            jnp.concatenate(weights, axis=1), mixed[first : SEG_HALF + PREFIX + own_keys]
        )
        out_ref[0, :, col] = (total[:, :HD] / total[:, HD:]).astype(bf16)

    for later in (False, True):

        @pl.when(side == int(later))
        def _(later=later):
            @pl.loop(0, 8 // heads)
            def _(step):
                for e in range(heads):
                    one_head(step * heads + e, later)

            @pl.when(jnp.min(least[...]) < 1e-27)
            def _():
                @pl.loop(0, 8)
                def _(g):
                    one_head_exact(g, later)


def prompt_block(index, heads, starts, queries, prefix, own, other, prior, after):
    operands = [starts, queries, prefix, own, other]
    block = pl.BlockSpec((1, 256, 1024), lambda g, *_: (0, index, 0))
    in_specs = [block, whole(prefix.shape), whole(own.shape), whole(other.shape)]
    aliases = {}
    if prior is not None:
        operands += [prior, after]
        in_specs += [pl.BlockSpec(memory_space=pl.ANY)] * 2
        aliases = {5: 0}
    keys = PREFIX + SEG_HALF + (index + 1) * 256
    return pl.pallas_call(
        functools.partial(prompt_kernel, index, heads),
        out_shape=jax.ShapeDtypeStruct(queries.shape, bf16),
        grid_spec=pltpu.PrefetchScalarGridSpec(
            num_scalar_prefetch=1,
            grid=(1,),
            in_specs=in_specs,
            out_specs=block,
            scratch_shapes=[
                pltpu.VMEM((2 * SEG_HALF + PREFIX, 2 * HD), bf16),
                pltpu.VMEM((256, HD), f32),
            ],
        ),
        input_output_aliases=aliases,
        compiler_params=params(),
        cost_estimate=pl.CostEstimate(
            flops=2048 * keys * 128 * 8, bytes_accessed=2000000, transcendentals=2048 * keys
        ),
        name="prompt_block",
    )(*operands)


def first_row_kernel(match_ref, start_ref, moved_ref, prefix_ref, own_ref, other_ref, after_ref, out_ref):
    group = lax.axis_index("pair")
    target = match_ref[group]
    start = start_ref[group]
    q = moved_ref[target, 0:16]
    fresh = moved_ref[target, 16:32]
    wide = fresh.astype(f32)
    fresh_v = jnp.concatenate([wide[8:], wide[:8]], axis=0).astype(bf16)
    s0 = dot_t(q, prefix_ref[0, :, :HD])
    pos = lax.broadcasted_iota(jnp.int32, s0.shape, 1)
    s0 = jnp.where(pos < start, s0, NEG_FILL)
    s1 = dot_t(q, own_ref[0, :, :HD])
    s2 = dot_t(q, other_ref[0, :, :HD])
    s3 = dot_t(q, fresh)
    step = lax.broadcasted_iota(jnp.int32, s3.shape, 0) // 4
    pos = lax.broadcasted_iota(jnp.int32, s3.shape, 1)
    s3 = jnp.where(pos <= step, s3, NEG_FILL)
    scores = (s0, s1, s2, s3)
    values = (prefix_ref[0, :, HD:], own_ref[0, :, HD:], other_ref[0, :, HD:], fresh_v)
    peak = functools.reduce(jnp.maximum, [jnp.max(s, axis=-1, keepdims=True) for s in scores])
    mix = jnp.zeros((16, HD), f32)
    totals = jnp.zeros((16, 1), f32)
    for s, v in zip(scores, values):
        w = jnp.exp2((s - peak) * (FACTOR * LOG2E))
        totals += jnp.sum(w, axis=-1, keepdims=True)
        mix += dot(w.astype(bf16), v)
    out_ref[...] = jnp.zeros(out_ref.shape, bf16)
    out_ref[target] = (mix / totals).astype(bf16)


def first_row(matching, starts, moved, prefix, own, other, after):
    return pl.pallas_call(
        first_row_kernel,
        out_shape=jax.ShapeDtypeStruct((GROUPS, 16, HD), bf16),
        grid_spec=pltpu.PrefetchScalarGridSpec(
            num_scalar_prefetch=2,
            grid=(1,),
            in_specs=[whole(moved.shape), whole(prefix.shape), whole(own.shape), whole(other.shape)]
            + [pl.BlockSpec(memory_space=pl.ANY)],
            out_specs=whole((GROUPS, 16, HD)),
        ),
        compiler_params=params(),
        cost_estimate=pl.CostEstimate(
            flops=20000000, bytes_accessed=1300000, transcendentals=33000
        ),
        name="first_row",
    )(matching, starts, moved, prefix, own, other, after)


def merge_kernel(match_ref, parts_ref, first_ref, q_ref, kv_ref, out_ref):
    group = lax.axis_index("pair")
    block = lax.axis_index("side") * 8 + lax.axis_index("tp")
    source = jnp.int32(0)
    for p in range(GROUPS):
        source = jnp.where(match_ref[p] == group, p, source)
    q = q_ref[0, :, :, pl.ds(pl.multiple_of(block * 512, 512), 512)].astype(f32)
    kv = kv_ref[0, :, :, pl.ds(pl.multiple_of((block // 2) * 256, 256), 256)].astype(f32)
    sub = lax.broadcasted_iota(jnp.int32, (ROWS, HD), 0)
    lane = lax.broadcasted_iota(jnp.int32, (ROWS, HD), 1)

    peaks, totals = [], []
    for b in range(BLOCKS):
        x = parts_ref[b, 128:144].astype(f32)[:ROWS]
        x = x + pltpu.roll(x, HD - 32, 1) + pltpu.roll(x, HD - 64, 1)
        peaks.append(x)
        totals.append(pltpu.roll(x, HD - 16, 1))
    top = functools.reduce(jnp.maximum, peaks)
    fresh = {}
    fresh_top = jnp.full((ROWS, HD), NEG_FILL, f32)
    for t in range(STEPS):
        for h in range(4):
            j = t * 4 + h
            qt = q[t, :, h * HD : (h + 1) * HD]
            for u in range(t + 1):
                s = jnp.sum(qt * kv[u, :, :HD], axis=-1, keepdims=True) * FACTOR
                fresh[j, u] = s
                fresh_top = jnp.where(lane == j, jnp.maximum(fresh_top, s), fresh_top)
    top = jnp.maximum(top, fresh_top)
    scales = [jnp.exp(p - top) for p in peaks]
    total = functools.reduce(jnp.add, [s * t for s, t in zip(scales, totals)])
    first = first_ref[source].astype(f32)
    for t in range(STEPS):
        for h in range(4):
            j = t * 4 + h
            acc = jnp.zeros((ROWS, HD), f32)
            for b in range(0, BLOCKS):
                tile = parts_ref[b, (j // 2) * 16 : (j // 2) * 16 + 16].astype(f32)
                acc += scales[b][:, j : j + 1] * tile[(j % 2) * 8 : (j % 2) * 8 + 8]
            denom = total[:, j : j + 1]
            for u in range(t + 1):
                w = jnp.exp(fresh[j, u] - top[:, j : j + 1])
                acc += w * kv[u, :, HD:]
                denom = denom + w
            out = acc / denom
            out = jnp.where(sub == 0, first[j : j + 1], out)
            out_ref[0, t, :, h * HD : (h + 1) * HD] = out.astype(bf16)


def merge(matching, parts, first, decode_queries, decode_kv):
    shape = (1, STEPS, ROWS, 512)
    return pl.pallas_call(
        merge_kernel,
        out_shape=jax.ShapeDtypeStruct(shape, bf16),
        grid_spec=pltpu.PrefetchScalarGridSpec(
            num_scalar_prefetch=1,
            grid=(1,),
            in_specs=[
                whole(parts.shape),
                whole(first.shape),
                whole(decode_queries.shape),
                whole(decode_kv.shape),
            ],
            out_specs=whole(shape),
        ),
        compiler_params=params(),
        cost_estimate=pl.CostEstimate(flops=3000000, bytes_accessed=1300000, transcendentals=60000),
        name="merge",
    )(matching, parts, first, decode_queries, decode_kv)


def local(
    segment_queries,
    segment_kv,
    prefix_kv,
    kv_cache,
    decode_queries,
    decode_kv,
    matching,
    segment_starts,
    cache_lengths,
):
    other_kv = lax.ppermute(segment_kv, "side", [(0, 1), (1, 0)])
    moved = prep(decode_queries, decode_kv)
    moved = lax.all_to_all(moved, "pair", split_axis=0, concat_axis=0, tiled=True)
    keys = (prefix_kv, segment_kv, other_kv)
    out = prompt_block(0, 1, segment_starts, segment_queries, *keys, None, None)
    first = first_row(matching, segment_starts, moved, *keys, out)
    parts = decode_parts(cache_lengths, decode_queries, kv_cache, first)
    first = lax.all_to_all(first, "pair", split_axis=0, concat_axis=0, tiled=True)
    first = lax.ppermute(
        first, ("side", "tp"), [(s * 8 + c, 2 * c + s) for s in range(2) for c in range(8)]
    )
    out = prompt_block(1, 2, segment_starts, segment_queries, *keys, out, parts)
    parts = lax.all_to_all(parts, ("side", "tp"), split_axis=0, concat_axis=0, tiled=True)
    decode_out = merge(matching, parts, first, decode_queries, decode_kv)
    return (out, decode_out)


def solution(mesh):
    in_specs = (
        P("pair", "side", "tp"),
        P("pair", "side", "tp"),
        P("pair", None, "tp"),
        P("pair", None, ("side", "tp"), None),
        P("pair", None, None, None),
        P("pair", None, None, None),
        P(),
        P(),
        P("pair", None),
    )
    out_specs = (P("pair", "side", "tp"), P("pair", None, None, ("side", "tp")))
    return jax.shard_map(local, mesh=mesh, in_specs=in_specs, out_specs=out_specs, check_vma=False)
```

```python
import functools
import math

import jax
import jax.numpy as jnp
from jax import lax
from jax.experimental import pallas as pl
from jax.experimental.pallas import tpu as pltpu
from jax.sharding import PartitionSpec as P

H = 64
KVH = 8
HD = 128
STEPS = 4
ROWS = 8
GROUPS = 16
BLOCKS = 16
SEG_HALF = 512
PREFIX = 1024
CACHE_BLOCK = 128

FACTOR = 1.0 / math.sqrt(HD)
LOG2E = 1.4426950408889634
NEG_FILL = -1e30
PART_ROWS = 144

f32 = jnp.float32
bf16 = jnp.bfloat16


def params(mib):
    return pltpu.CompilerParams(vmem_limit_bytes=mib * 1024 * 1024)


def in_hbm(x):
    return pltpu.with_memory_space_constraint(x, pltpu.HBM)


def whole(shape):
    return pl.BlockSpec(shape, lambda *_: (0,) * len(shape))


def dot_t(a, b):
    return lax.dot_general(a, b, (((1,), (1,)), ((), ())), preferred_element_type=f32)


def dot(a, b):
    return jnp.dot(a, b, preferred_element_type=f32)


def prep_kernel(q_hbm, kv_hbm, out_ref, q_ref, kv_ref, sems):
    side = lax.axis_index("side")
    tp = lax.axis_index("tp")
    q_col = pl.multiple_of((2 * tp + side) * 512, 512)
    kv_col = pl.multiple_of(tp * 256, 256)
    copies = [
        pltpu.make_async_copy(q_hbm.at[0, :, :, pl.ds(q_col, 512)], q_ref, sems.at[0]),
        pltpu.make_async_copy(kv_hbm.at[0, :, :, pl.ds(kv_col, 256)], kv_ref, sems.at[1]),
    ]
    for copy in copies:
        copy.start()
    for copy in copies:
        copy.wait()
    q = q_ref[...].astype(f32)
    kv = kv_ref[...].astype(f32)
    rows = [q[t, 0:1, h * HD : (h + 1) * HD] for t in range(STEPS) for h in range(4)]
    pad = [jnp.zeros((4, HD), f32)]
    rows += [kv[u, 0:1, :HD] for u in range(STEPS)] + pad
    rows += [kv[u, 0:1, HD:] for u in range(STEPS)] + pad
    sent = jnp.concatenate(rows, axis=0).astype(bf16)
    for p in range(GROUPS):
        out_ref[p] = sent


def prep(decode_queries, decode_kv):
    shape = (GROUPS, 32, HD)
    return pl.pallas_call(
        prep_kernel,
        out_shape=jax.ShapeDtypeStruct(shape, bf16),
        grid=(1,),
        in_specs=[pl.BlockSpec(memory_space=pltpu.HBM)] * 2,
        out_specs=whole(shape),
        scratch_shapes=[
            pltpu.VMEM((STEPS, ROWS, 512), bf16),
            pltpu.VMEM((STEPS, ROWS, 256), bf16),
            pltpu.SemaphoreType.DMA((2,)),
        ],
        compiler_params=params(4),
        cost_estimate=pl.CostEstimate(flops=10000, bytes_accessed=200000, transcendentals=0),
        name="prep",
    )(in_hbm(decode_queries), in_hbm(decode_kv))


def decode_kernel(len_ref, q_ref, cache_ref, after_ref, out_ref):
    block = lax.axis_index("side") * 8 + lax.axis_index("tp")
    sub = lax.broadcasted_iota(jnp.int32, (ROWS, HD), 0)
    lane = lax.broadcasted_iota(jnp.int32, (ROWS, HD), 1)
    lens = jnp.zeros((ROWS, HD), jnp.int32)
    for k in range(ROWS - 1):
        lens = jnp.where(sub == k + 1, len_ref[0, k], lens)
    allowed = (block * CACHE_BLOCK + lane < lens)[None]
    tiles = STEPS * 8
    small = lane % 32
    row_of = lax.broadcasted_iota(jnp.int32, (tiles * ROWS, HD), 0) % ROWS
    keep = [jnp.where(row_of == k + 1, 1.0, 0.0).astype(bf16) for k in range(ROWS - 1)]

    def spread(x):
        return jnp.concatenate([x * k for k in keep], axis=1)

    scores = []
    for head in range(2):
        q = jnp.concatenate(
            [
                q_ref[0, t, :, (head * 8 + g) * HD : (head * 8 + g + 1) * HD].astype(f32)
                for t in range(STEPS)
                for g in range(8)
            ],
            axis=0,
        ).astype(bf16)
        keys = jnp.concatenate(
            [cache_ref[0, k, :, head * 256 : head * 256 + HD] for k in range(ROWS - 1)], axis=1
        )
        scores.append(dot_t(spread(q), keys).reshape(tiles, ROWS, HD))
    for head in range(2):
        s = jnp.where(allowed, scores[head] * FACTOR, NEG_FILL)
        peak = jnp.max(s, axis=-1, keepdims=True)
        weights = jnp.where(allowed, jnp.exp(s - peak), 0.0)
        values = cache_ref[0, :, :, head * 256 + HD : head * 256 + 256].reshape(-1, HD)
        values = jnp.concatenate([values, jnp.ones_like(values)], axis=1)
        both = dot(spread(weights.reshape(tiles * ROWS, HD).astype(bf16)), values)
        both = both.reshape(STEPS, 8, ROWS, 2 * HD)
        peak = peak.reshape(STEPS, 8, ROWS, 1)
        for half in range(2):
            stats = jnp.zeros((ROWS, HD), f32)
            for t in range(STEPS):
                for h in range(4):
                    j = t * 4 + h
                    stats = jnp.where(small == j, peak[t, half * 4 + h], stats)
                    stats = jnp.where(small == 16 + j, both[t, half * 4 + h, :, HD:], stats)
            high = stats.astype(bf16).astype(f32)
            rest = stats - high
            mid = rest.astype(bf16).astype(f32)
            low = rest - mid
            packed = jnp.where(lane < 32, high, jnp.where(lane < 64, mid, low))
            slot = head * 2 + half
            mix = both[:, half * 4 : half * 4 + 4, :, :HD].reshape(128, HD)
            out_ref[slot, 0:128] = mix.astype(bf16)
            out_ref[slot, 128:144] = jnp.concatenate(
                [packed, jnp.zeros((ROWS, HD), f32)], axis=0
            ).astype(bf16)


def decode_parts(cache_lengths, decode_queries, kv_cache, after):
    return pl.pallas_call(
        decode_kernel,
        out_shape=jax.ShapeDtypeStruct((BLOCKS, PART_ROWS, HD), bf16),
        grid_spec=pltpu.PrefetchScalarGridSpec(
            num_scalar_prefetch=1,
            grid=(KVH // 2,),
            in_specs=[
                pl.BlockSpec((1, STEPS, ROWS, 2048), lambda c, *_: (0, 0, 0, c)),
                pl.BlockSpec((1, ROWS - 1, CACHE_BLOCK, 512), lambda c, *_: (0, 0, 0, c)),
                pl.BlockSpec(memory_space=pl.ANY),
            ],
            out_specs=pl.BlockSpec((4, PART_ROWS, HD), lambda c, *_: (c, 0, 0)),
        ),
        compiler_params=params(16),
        cost_estimate=pl.CostEstimate(
            flops=2000000000, bytes_accessed=4800000, transcendentals=300000
        ),
        name="decode_parts",
    )(in_hbm(cache_lengths), in_hbm(decode_queries), in_hbm(kv_cache), after)


def prompt_kernel(start_ref, q_ref, prefix_ref, own_ref, other_ref, after_ref, out_ref, mixed, least, longest):
    side = lax.axis_index("side")
    start = start_ref[lax.axis_index("pair")]
    tokens = 256
    scale = FACTOR * LOG2E

    @pl.when(pl.program_id(0) == 0)
    def _():
        pos = lax.broadcasted_iota(jnp.int32, (PREFIX, 2 * HD), 0)
        wide = jnp.concatenate([prefix_ref[0, :, HD:], jnp.ones((PREFIX, HD), bf16)], axis=1)
        mixed[SEG_HALF : SEG_HALF + PREFIX] = jnp.where(pos < start, wide.astype(f32), 0.0).astype(
            bf16
        )
        ones = jnp.ones((SEG_HALF, HD), bf16)
        mixed[:SEG_HALF] = jnp.concatenate([other_ref[0, :, HD:], ones], axis=1)
        mixed[SEG_HALF + PREFIX :] = jnp.concatenate([own_ref[0, :, HD:], ones], axis=1)

        def norm(ref):
            k = ref[0, :, :HD].astype(f32)
            return jnp.max(jnp.sum(k * k, axis=-1, keepdims=True), axis=0, keepdims=True)

        most = jnp.maximum(norm(prefix_ref), jnp.maximum(norm(own_ref), norm(other_ref)))
        longest[...] = jnp.broadcast_to(most, longest.shape)

    causal = lax.broadcasted_iota(jnp.int32, (tokens, tokens), 1) <= lax.broadcasted_iota(
        jnp.int32, (tokens, tokens), 0
    )

    def key_parts(half, later):
        parts = []
        if later:
            parts += [(other_ref, n) for n in range(0, SEG_HALF, 256)]
        parts += [(prefix_ref, n) for n in range(0, PREFIX, 256)]
        parts += [(own_ref, n) for n in range(0, (half + 1) * tokens, 256)]
        return parts

    def mix(weights, half, later):
        first = 0 if later else SEG_HALF
        last = SEG_HALF + PREFIX + (half + 1) * tokens
        return dot(jnp.concatenate(weights, axis=1), mixed[first:last])

    def place(half, head):
        return slice(half * tokens, (half + 1) * tokens), slice(head * HD, (head + 1) * HD)

    def block(half, head, later):
        rows, cols = place(half, head)
        q = q_ref[0, rows, cols]
        wide_q = q.astype(f32)
        norms = jnp.sum(wide_q * wide_q, axis=-1, keepdims=True)
        bound = jnp.sqrt(norms * longest[0:1, 0:1]) * scale
        parts = key_parts(half, later)
        weights = []
        for number, (ref, n) in enumerate(parts):
            w = jnp.exp2(dot_t(q, ref[0, n : n + 256, :HD]) * scale - bound)
            if number == len(parts) - 1:
                w = jnp.where(causal, w, 0.0)
            weights.append(w.astype(bf16))
        total = mix(weights, half, later)
        sums = total[:, HD:]
        out_ref[0, rows, cols] = (total[:, :HD] / sums).astype(bf16)
        least[...] = jnp.minimum(least[...], sums)

    def block_exact(half, head, later):
        rows, cols = place(half, head)
        q = q_ref[0, rows, cols]
        parts = key_parts(half, later)
        scores = []
        for number, (ref, n) in enumerate(parts):
            s = dot_t(q, ref[0, n : n + 256, :HD])
            if ref is prefix_ref:
                at = n + lax.broadcasted_iota(jnp.int32, s.shape, 1)
                s = jnp.where(at < start, s, NEG_FILL)
            if number == len(parts) - 1:
                s = jnp.where(causal, s, NEG_FILL)
            scores.append(s)
        peak = functools.reduce(
            jnp.maximum, [jnp.max(s, axis=-1, keepdims=True) for s in scores]
        )
        weights = [jnp.exp2((s - peak) * scale).astype(bf16) for s in scores]
        total = mix(weights, half, later)
        out_ref[0, rows, cols] = (total[:, :HD] / total[:, HD:]).astype(bf16)

    least[...] = jnp.ones(least.shape, f32)
    for later in (False, True):

        @pl.when(side == int(later))
        def _(later=later):
            for half in range(2):
                for head in range(2):
                    block(half, head, later)

            @pl.when(jnp.min(least[...]) < 1e-27)
            def _():
                for half in range(2):
                    for head in range(2):
                        block_exact(half, head, later)


def prompt(starts, queries, prefix, own, other, after):
    block = pl.BlockSpec((1, 2 * 256, 2 * HD), lambda g, *_: (0, 0, g))
    return pl.pallas_call(
        prompt_kernel,
        out_shape=jax.ShapeDtypeStruct(queries.shape, bf16),
        grid_spec=pltpu.PrefetchScalarGridSpec(
            num_scalar_prefetch=1,
            grid=(4,),
            in_specs=[
                block,
                whole(prefix.shape),
                whole(own.shape),
                whole(other.shape),
                pl.BlockSpec(memory_space=pl.ANY),
            ],
            out_specs=block,
            scratch_shapes=[
                pltpu.VMEM((2 * SEG_HALF + PREFIX, 2 * HD), bf16),
                pltpu.VMEM((256, HD), f32),
                pltpu.VMEM((ROWS, HD), f32),
            ],
        ),
        compiler_params=params(32),
        cost_estimate=pl.CostEstimate(
            flops=4096 * 1920 * 128 * 8, bytes_accessed=3000000, transcendentals=4096 * 1920
        ),
        name="prompt",
    )(in_hbm(starts), queries, prefix, own, other, after)


def first_row_kernel(match_ref, start_ref, moved_ref, prefix_ref, own_ref, other_ref, out_ref):
    group = lax.axis_index("pair")
    target = match_ref[group]
    start = start_ref[group]
    q = moved_ref[target, 0:16]
    fresh = moved_ref[target, 16:32]
    wide = fresh.astype(f32)
    fresh_v = jnp.concatenate([wide[8:], wide[:8]], axis=0).astype(bf16)
    s0 = dot_t(q, prefix_ref[0, :, :HD])
    pos = lax.broadcasted_iota(jnp.int32, s0.shape, 1)
    s0 = jnp.where(pos < start, s0, NEG_FILL)
    s1 = dot_t(q, own_ref[0, :, :HD])
    s2 = dot_t(q, other_ref[0, :, :HD])
    s3 = dot_t(q, fresh)
    step = lax.broadcasted_iota(jnp.int32, s3.shape, 0) // 4
    pos = lax.broadcasted_iota(jnp.int32, s3.shape, 1)
    s3 = jnp.where(pos <= step, s3, NEG_FILL)
    scores = (s0, s1, s2, s3)
    values = (prefix_ref[0, :, HD:], own_ref[0, :, HD:], other_ref[0, :, HD:], fresh_v)
    peak = functools.reduce(jnp.maximum, [jnp.max(s, axis=-1, keepdims=True) for s in scores])
    mix = jnp.zeros((16, HD), f32)
    totals = jnp.zeros((16, 1), f32)
    for s, v in zip(scores, values):
        w = jnp.exp2((s - peak) * (FACTOR * LOG2E))
        totals += jnp.sum(w, axis=-1, keepdims=True)
        mix += dot(w.astype(bf16), v)
    out_ref[...] = jnp.zeros(out_ref.shape, bf16)
    out_ref[target] = (mix / totals).astype(bf16)


def first_row(matching, starts, moved, prefix, own, other):
    return pl.pallas_call(
        first_row_kernel,
        out_shape=jax.ShapeDtypeStruct((GROUPS, 16, HD), bf16),
        grid_spec=pltpu.PrefetchScalarGridSpec(
            num_scalar_prefetch=2,
            grid=(1,),
            in_specs=[whole(moved.shape), whole(prefix.shape), whole(own.shape), whole(other.shape)],
            out_specs=whole((GROUPS, 16, HD)),
        ),
        compiler_params=params(8),
        cost_estimate=pl.CostEstimate(
            flops=20000000, bytes_accessed=1300000, transcendentals=33000
        ),
        name="first_row",
    )(in_hbm(matching), in_hbm(starts), moved, prefix, own, other)


def merge_kernel(match_ref, parts_ref, first_ref, q_hbm, kv_hbm, out_ref, q_ref, kv_ref, sems):
    group = lax.axis_index("pair")
    block = lax.axis_index("side") * 8 + lax.axis_index("tp")
    q_col = pl.multiple_of(block * 512, 512)
    kv_col = pl.multiple_of((block // 2) * 256, 256)
    copies = [
        pltpu.make_async_copy(q_hbm.at[0, :, :, pl.ds(q_col, 512)], q_ref, sems.at[0]),
        pltpu.make_async_copy(kv_hbm.at[0, :, :, pl.ds(kv_col, 256)], kv_ref, sems.at[1]),
    ]
    for copy in copies:
        copy.start()
    for copy in copies:
        copy.wait()
    source = jnp.int32(0)
    for p in range(GROUPS):
        source = jnp.where(match_ref[p] == group, p, source)
    q = q_ref[...].astype(f32)
    kv = kv_ref[...].astype(f32)
    sub = lax.broadcasted_iota(jnp.int32, (ROWS, HD), 0)
    lane = lax.broadcasted_iota(jnp.int32, (ROWS, HD), 1)

    peaks, totals = [], []
    for b in range(BLOCKS):
        x = parts_ref[b, 128:144].astype(f32)[:ROWS]
        x = x + pltpu.roll(x, HD - 32, 1) + pltpu.roll(x, HD - 64, 1)
        peaks.append(x)
        totals.append(pltpu.roll(x, HD - 16, 1))
    top = functools.reduce(jnp.maximum, peaks)
    fresh = {}
    fresh_top = jnp.full((ROWS, HD), NEG_FILL, f32)
    for t in range(STEPS):
        for h in range(4):
            j = t * 4 + h
            qt = q[t, :, h * HD : (h + 1) * HD]
            for u in range(t + 1):
                s = jnp.sum(qt * kv[u, :, :HD], axis=-1, keepdims=True) * FACTOR
                fresh[j, u] = s
                fresh_top = jnp.where(lane == j, jnp.maximum(fresh_top, s), fresh_top)
    top = jnp.maximum(top, fresh_top)
    scales = [jnp.exp(p - top) for p in peaks]
    total = functools.reduce(jnp.add, [s * t for s, t in zip(scales, totals)])
    first = first_ref[source].astype(f32)
    for t in range(STEPS):
        for h in range(4):
            j = t * 4 + h
            acc = jnp.zeros((ROWS, HD), f32)
            for b in range(0, BLOCKS):
                tile = parts_ref[b, (j // 2) * 16 : (j // 2) * 16 + 16].astype(f32)
                acc += scales[b][:, j : j + 1] * tile[(j % 2) * 8 : (j % 2) * 8 + 8]
            denom = total[:, j : j + 1]
            for u in range(t + 1):
                w = jnp.exp(fresh[j, u] - top[:, j : j + 1])
                acc += w * kv[u, :, HD:]
                denom = denom + w
            out = acc / denom
            out = jnp.where(sub == 0, first[j : j + 1], out)
            out_ref[0, t, :, h * HD : (h + 1) * HD] = out.astype(bf16)


def merge(matching, parts, first, decode_queries, decode_kv):
    shape = (1, STEPS, ROWS, 512)
    return pl.pallas_call(
        merge_kernel,
        out_shape=jax.ShapeDtypeStruct(shape, bf16),
        grid_spec=pltpu.PrefetchScalarGridSpec(
            num_scalar_prefetch=1,
            grid=(1,),
            in_specs=[
                whole(parts.shape),
                whole(first.shape),
                pl.BlockSpec(memory_space=pltpu.HBM),
                pl.BlockSpec(memory_space=pltpu.HBM),
            ],
            out_specs=whole(shape),
            scratch_shapes=[
                pltpu.VMEM((STEPS, ROWS, 512), bf16),
                pltpu.VMEM((STEPS, ROWS, 256), bf16),
                pltpu.SemaphoreType.DMA((2,)),
            ],
        ),
        compiler_params=params(8),
        cost_estimate=pl.CostEstimate(flops=3000000, bytes_accessed=1300000, transcendentals=60000),
        name="merge",
    )(in_hbm(matching), parts, first, in_hbm(decode_queries), in_hbm(decode_kv))


def local(
    segment_queries,
    segment_kv,
    prefix_kv,
    kv_cache,
    decode_queries,
    decode_kv,
    matching,
    segment_starts,
    cache_lengths,
):
    other_kv = lax.ppermute(segment_kv, "side", [(0, 1), (1, 0)])
    moved = prep(decode_queries, decode_kv)
    parts = decode_parts(cache_lengths, decode_queries, kv_cache, moved)
    moved = lax.all_to_all(moved, "pair", split_axis=0, concat_axis=0, tiled=True)
    keys = (prefix_kv, segment_kv, other_kv)
    first = first_row(matching, segment_starts, moved, *keys)
    first = lax.all_to_all(first, "pair", split_axis=0, concat_axis=0, tiled=True)
    first, parts = lax.optimization_barrier((first, parts))
    first = lax.ppermute(
        first, ("side", "tp"), [(s * 8 + c, 2 * c + s) for s in range(2) for c in range(8)]
    )
    out = prompt(segment_starts, segment_queries, *keys, parts)
    parts = lax.all_to_all(parts, ("side", "tp"), split_axis=0, concat_axis=0, tiled=True)
    decode_out = merge(matching, parts, first, decode_queries, decode_kv)
    return (out, decode_out)


def solution(mesh):
    in_specs = (
        P("pair", "side", "tp"),
        P("pair", "side", "tp"),
        P("pair", None, "tp"),
        P("pair", None, ("side", "tp"), None),
        P("pair", None, None, None),
        P("pair", None, None, None),
        P(),
        P(),
        P("pair", None),
    )
    out_specs = (P("pair", "side", "tp"), P("pair", None, None, ("side", "tp")))
    return jax.shard_map(local, mesh=mesh, in_specs=in_specs, out_specs=out_specs, check_vma=False)
```

```python
import functools
import math

import jax
import jax.numpy as jnp
from jax import lax
from jax.experimental import pallas as pl
from jax.experimental.pallas import tpu as pltpu
from jax.sharding import PartitionSpec as P

H = 64
KVH = 8
HD = 128
STEPS = 4
ROWS = 8
GROUPS = 16
BLOCKS = 16
SEG_HALF = 512
PREFIX = 1024
CACHE_BLOCK = 128

FACTOR = 1.0 / math.sqrt(HD)
LOG2E = 1.4426950408889634
NEG_FILL = -1e30
PART_ROWS = 160

f32 = jnp.float32
bf16 = jnp.bfloat16


def params(mib):
    return pltpu.CompilerParams(vmem_limit_bytes=mib * 1024 * 1024)


def in_hbm(x):
    return pltpu.with_memory_space_constraint(x, pltpu.HBM)


def whole(shape):
    return pl.BlockSpec(shape, lambda *_: (0,) * len(shape))


def dot_t(a, b):
    return lax.dot_general(a, b, (((1,), (1,)), ((), ())), preferred_element_type=f32)


def dot(a, b):
    return jnp.dot(a, b, preferred_element_type=f32)


def prep_kernel(q_hbm, kv_hbm, out_ref, q_ref, kv_ref, sems):
    side = lax.axis_index("side")
    tp = lax.axis_index("tp")
    q_col = pl.multiple_of((2 * tp + side) * 512, 512)
    kv_col = pl.multiple_of(tp * 256, 256)
    copies = [
        pltpu.make_async_copy(q_hbm.at[0, :, :, pl.ds(q_col, 512)], q_ref, sems.at[0]),
        pltpu.make_async_copy(kv_hbm.at[0, :, :, pl.ds(kv_col, 256)], kv_ref, sems.at[1]),
    ]
    for copy in copies:
        copy.start()
    for copy in copies:
        copy.wait()
    q = q_ref[...].astype(f32)
    kv = kv_ref[...].astype(f32)
    rows = [q[t, 0:1, h * HD : (h + 1) * HD] for t in range(STEPS) for h in range(4)]
    pad = [jnp.zeros((4, HD), f32)]
    rows += [kv[u, 0:1, :HD] for u in range(STEPS)] + pad
    rows += [kv[u, 0:1, HD:] for u in range(STEPS)] + pad
    sent = jnp.concatenate(rows, axis=0).astype(bf16)
    for p in range(GROUPS):
        out_ref[p] = sent


def prep(decode_queries, decode_kv):
    shape = (GROUPS, 32, HD)
    return pl.pallas_call(
        prep_kernel,
        out_shape=jax.ShapeDtypeStruct(shape, bf16),
        grid=(1,),
        in_specs=[pl.BlockSpec(memory_space=pltpu.HBM)] * 2,
        out_specs=whole(shape),
        scratch_shapes=[
            pltpu.VMEM((STEPS, ROWS, 512), bf16),
            pltpu.VMEM((STEPS, ROWS, 256), bf16),
            pltpu.SemaphoreType.DMA((2,)),
        ],
        compiler_params=params(4),
        cost_estimate=pl.CostEstimate(flops=10000, bytes_accessed=200000, transcendentals=0),
        name="prep",
    )(in_hbm(decode_queries), in_hbm(decode_kv))


def decode_kernel(len_ref, q_ref, cache_ref, prior_ref, after_ref, out_ref):
    block = lax.axis_index("side") * 8 + lax.axis_index("tp")
    sub = lax.broadcasted_iota(jnp.int32, (ROWS, HD), 0)
    lane = lax.broadcasted_iota(jnp.int32, (ROWS, HD), 1)
    lens = jnp.zeros((ROWS, HD), jnp.int32)
    for k in range(ROWS - 1):
        lens = jnp.where(sub == k + 1, len_ref[0, k], lens)
    allowed = (block * CACHE_BLOCK + lane < lens)[None]
    tiles = STEPS * 8
    small = lane % 32
    row_of = lax.broadcasted_iota(jnp.int32, (tiles * ROWS, HD), 0) % ROWS
    keep = [jnp.where(row_of == k + 1, 1.0, 0.0).astype(bf16) for k in range(ROWS - 1)]

    def spread(x):
        return jnp.concatenate([x * k for k in keep], axis=1)

    scores = []
    for head in range(2):
        q = jnp.concatenate(
            [
                q_ref[0, t, :, (head * 8 + g) * HD : (head * 8 + g + 1) * HD].astype(f32)
                for t in range(STEPS)
                for g in range(8)
            ],
            axis=0,
        ).astype(bf16)
        keys = jnp.concatenate(
            [cache_ref[0, k, :, head * 256 : head * 256 + HD] for k in range(ROWS - 1)], axis=1
        )
        scores.append(dot_t(spread(q), keys).reshape(tiles, ROWS, HD))
    for head in range(2):
        s = jnp.where(allowed, scores[head] * FACTOR, NEG_FILL)
        peak = jnp.max(s, axis=-1, keepdims=True)
        weights = jnp.where(allowed, jnp.exp(s - peak), 0.0)
        values = cache_ref[0, :, :, head * 256 + HD : head * 256 + 256].reshape(-1, HD)
        values = jnp.concatenate([values, jnp.ones_like(values)], axis=1)
        both = dot(spread(weights.reshape(tiles * ROWS, HD).astype(bf16)), values)
        both = both.reshape(STEPS, 8, ROWS, 2 * HD)
        peak = peak.reshape(STEPS, 8, ROWS, 1)
        for half in range(2):
            stats = jnp.zeros((ROWS, HD), f32)
            for t in range(STEPS):
                for h in range(4):
                    j = t * 4 + h
                    stats = jnp.where(small == j, peak[t, half * 4 + h], stats)
                    stats = jnp.where(small == 16 + j, both[t, half * 4 + h, :, HD:], stats)
            high = stats.astype(bf16).astype(f32)
            rest = stats - high
            mid = rest.astype(bf16).astype(f32)
            low = rest - mid
            packed = jnp.where(lane < 32, high, jnp.where(lane < 64, mid, low))
            slot = head * 2 + half
            mix = both[:, half * 4 : half * 4 + 4, :, :HD].reshape(128, HD)
            out_ref[slot, 0:128] = mix.astype(bf16)
            out_ref[slot, 128:144] = jnp.concatenate(
                [packed, jnp.zeros((ROWS, HD), f32)], axis=0
            ).astype(bf16)


def decode_parts(share, cache_lengths, decode_queries, kv_cache, prior, after):
    return pl.pallas_call(
        decode_kernel,
        out_shape=jax.ShapeDtypeStruct((BLOCKS, PART_ROWS, HD), bf16),
        grid_spec=pltpu.PrefetchScalarGridSpec(
            num_scalar_prefetch=1,
            grid=(2,),
            in_specs=[
                pl.BlockSpec((1, STEPS, ROWS, 2048), lambda c, *_: (0, 0, 0, 2 * share + c)),
                pl.BlockSpec((1, ROWS - 1, CACHE_BLOCK, 512), lambda c, *_: (0, 0, 0, 2 * share + c)),
                pl.BlockSpec(memory_space=pl.ANY),
                pl.BlockSpec(memory_space=pl.ANY),
            ],
            out_specs=pl.BlockSpec((4, PART_ROWS, HD), lambda c, *_: (2 * share + c, 0, 0)),
        ),
        input_output_aliases={3: 0} if share else {},
        compiler_params=params(16),
        cost_estimate=pl.CostEstimate(
            flops=1000000000, bytes_accessed=2400000, transcendentals=150000
        ),
        name="decode_parts",
    )(in_hbm(cache_lengths), in_hbm(decode_queries), in_hbm(kv_cache), prior, after)


def hand_over_kernel(match_ref, parts_in, first_ref, parts_ref, sem):
    group = lax.axis_index("pair")
    slot = 2 * lax.axis_index("tp") + lax.axis_index("side")
    source = jnp.int32(0)
    for p in range(GROUPS):
        source = jnp.where(match_ref[p] == group, p, source)
    copy = pltpu.make_async_copy(first_ref.at[source], parts_ref.at[slot, 144:160], sem)
    copy.start()
    copy.wait()


def hand_over(matching, parts, first):
    return pl.pallas_call(
        hand_over_kernel,
        out_shape=jax.ShapeDtypeStruct(parts.shape, bf16),
        grid_spec=pltpu.PrefetchScalarGridSpec(
            num_scalar_prefetch=1,
            grid=(1,),
            in_specs=[pl.BlockSpec(memory_space=pl.ANY)] * 2,
            out_specs=pl.BlockSpec(memory_space=pl.ANY),
            scratch_shapes=[pltpu.SemaphoreType.DMA],
        ),
        input_output_aliases={1: 0},
        compiler_params=params(4),
        cost_estimate=pl.CostEstimate(flops=0, bytes_accessed=8192, transcendentals=0),
        name="hand_over",
    )(in_hbm(matching), parts, first)


def prompt_kernel(start_ref, q_ref, prefix_ref, own_ref, other_ref, after_ref, out_ref, mixed, turned, least, longest):
    side = lax.axis_index("side")
    start = start_ref[lax.axis_index("pair")]
    tokens = 256
    scale = FACTOR * LOG2E

    @pl.when(pl.program_id(0) == 0)
    def _():
        pos = lax.broadcasted_iota(jnp.int32, (PREFIX, 2 * HD), 0)
        wide = jnp.concatenate([prefix_ref[0, :, HD:], jnp.ones((PREFIX, HD), bf16)], axis=1)
        mixed[SEG_HALF : SEG_HALF + PREFIX] = jnp.where(pos < start, wide.astype(f32), 0.0).astype(
            bf16
        )
        ones = jnp.ones((SEG_HALF, HD), bf16)
        mixed[:SEG_HALF] = jnp.concatenate([other_ref[0, :, HD:], ones], axis=1)
        mixed[SEG_HALF + PREFIX :] = jnp.concatenate([own_ref[0, :, HD:], ones], axis=1)
        turned[:, :SEG_HALF] = other_ref[0, :, :HD].T
        turned[:, SEG_HALF : SEG_HALF + PREFIX] = prefix_ref[0, :, :HD].T
        turned[:, SEG_HALF + PREFIX :] = own_ref[0, :, :HD].T

        def norm(ref):
            k = ref[0, :, :HD].astype(f32)
            return jnp.max(jnp.sum(k * k, axis=-1, keepdims=True), axis=0, keepdims=True)

        most = jnp.maximum(norm(prefix_ref), jnp.maximum(norm(own_ref), norm(other_ref)))
        longest[...] = jnp.broadcast_to(most, longest.shape)

    causal = lax.broadcasted_iota(jnp.int32, (tokens, tokens), 1) <= lax.broadcasted_iota(
        jnp.int32, (tokens, tokens), 0
    )

    def key_parts(half, later):
        return range(0 if later else SEG_HALF, SEG_HALF + PREFIX + (half + 1) * tokens, 256)

    def mix(weights, half, later):
        first = 0 if later else SEG_HALF
        last = SEG_HALF + PREFIX + (half + 1) * tokens
        return dot(jnp.concatenate(weights, axis=1), mixed[first:last])

    def place(half, head):
        return slice(half * tokens, (half + 1) * tokens), slice(head * HD, (head + 1) * HD)

    def block(half, head, later):
        rows, cols = place(half, head)
        q = q_ref[0, rows, cols]
        wide_q = q.astype(f32)
        norms = jnp.sum(wide_q * wide_q, axis=-1, keepdims=True)
        bound = jnp.sqrt(norms * longest[0:1, 0:1]) * scale
        parts = key_parts(half, later)
        weights = []
        for number, n in enumerate(parts):
            w = jnp.exp2(dot(q, turned[:, n : n + 256]) * scale - bound)
            if number == len(parts) - 1:
                w = jnp.where(causal, w, 0.0)
            weights.append(w.astype(bf16))
        total = mix(weights, half, later)
        sums = total[:, HD:]
        out_ref[0, rows, cols] = (total[:, :HD] / sums).astype(bf16)
        least[...] = jnp.minimum(least[...], sums)

    def block_exact(half, head, later):
        rows, cols = place(half, head)
        q = q_ref[0, rows, cols]
        parts = key_parts(half, later)
        scores = []
        for number, n in enumerate(parts):
            s = dot(q, turned[:, n : n + 256])
            if SEG_HALF <= n < SEG_HALF + PREFIX:
                at = n - SEG_HALF + lax.broadcasted_iota(jnp.int32, s.shape, 1)
                s = jnp.where(at < start, s, NEG_FILL)
            if number == len(parts) - 1:
                s = jnp.where(causal, s, NEG_FILL)
            scores.append(s)
        peak = functools.reduce(
            jnp.maximum, [jnp.max(s, axis=-1, keepdims=True) for s in scores]
        )
        weights = [jnp.exp2((s - peak) * scale).astype(bf16) for s in scores]
        total = mix(weights, half, later)
        out_ref[0, rows, cols] = (total[:, :HD] / total[:, HD:]).astype(bf16)

    least[...] = jnp.ones(least.shape, f32)
    for later in (False, True):

        @pl.when(side == int(later))
        def _(later=later):
            for half in range(2):
                for head in range(2):
                    block(half, head, later)

            @pl.when(jnp.min(least[...]) < 1e-27)
            def _():
                for half in range(2):
                    for head in range(2):
                        block_exact(half, head, later)


def prompt(starts, queries, prefix, own, other, after):
    block = pl.BlockSpec((1, 2 * 256, 2 * HD), lambda g, *_: (0, 0, g))
    return pl.pallas_call(
        prompt_kernel,
        out_shape=jax.ShapeDtypeStruct(queries.shape, bf16),
        grid_spec=pltpu.PrefetchScalarGridSpec(
            num_scalar_prefetch=1,
            grid=(4,),
            in_specs=[
                block,
                whole(prefix.shape),
                whole(own.shape),
                whole(other.shape),
                pl.BlockSpec(memory_space=pl.ANY),
            ],
            out_specs=block,
            scratch_shapes=[
                pltpu.VMEM((2 * SEG_HALF + PREFIX, 2 * HD), bf16),
                pltpu.VMEM((HD, 2 * SEG_HALF + PREFIX), bf16),
                pltpu.VMEM((256, HD), f32),
                pltpu.VMEM((ROWS, HD), f32),
            ],
        ),
        compiler_params=params(32),
        cost_estimate=pl.CostEstimate(
            flops=4096 * 1920 * 128 * 8, bytes_accessed=3000000, transcendentals=4096 * 1920
        ),
        name="prompt",
    )(in_hbm(starts), queries, prefix, own, other, after)


def first_row_kernel(match_ref, start_ref, moved_ref, prefix_ref, own_ref, other_ref, after_ref, out_ref):
    group = lax.axis_index("pair")
    target = match_ref[group]
    start = start_ref[group]
    q = moved_ref[target, 0:16]
    fresh = moved_ref[target, 16:32]
    wide = fresh.astype(f32)
    fresh_v = jnp.concatenate([wide[8:], wide[:8]], axis=0).astype(bf16)
    s0 = dot_t(q, prefix_ref[0, :, :HD])
    pos = lax.broadcasted_iota(jnp.int32, s0.shape, 1)
    s0 = jnp.where(pos < start, s0, NEG_FILL)
    s1 = dot_t(q, own_ref[0, :, :HD])
    s2 = dot_t(q, other_ref[0, :, :HD])
    s3 = dot_t(q, fresh)
    step = lax.broadcasted_iota(jnp.int32, s3.shape, 0) // 4
    pos = lax.broadcasted_iota(jnp.int32, s3.shape, 1)
    s3 = jnp.where(pos <= step, s3, NEG_FILL)
    scores = (s0, s1, s2, s3)
    values = (prefix_ref[0, :, HD:], own_ref[0, :, HD:], other_ref[0, :, HD:], fresh_v)
    peak = functools.reduce(jnp.maximum, [jnp.max(s, axis=-1, keepdims=True) for s in scores])
    mix = jnp.zeros((16, HD), f32)
    totals = jnp.zeros((16, 1), f32)
    for s, v in zip(scores, values):
        w = jnp.exp2((s - peak) * (FACTOR * LOG2E))
        totals += jnp.sum(w, axis=-1, keepdims=True)
        mix += dot(w.astype(bf16), v)
    out_ref[...] = jnp.zeros(out_ref.shape, bf16)
    out_ref[target] = (mix / totals).astype(bf16)


def first_row(matching, starts, moved, prefix, own, other, after):
    return pl.pallas_call(
        first_row_kernel,
        out_shape=jax.ShapeDtypeStruct((GROUPS, 16, HD), bf16),
        grid_spec=pltpu.PrefetchScalarGridSpec(
            num_scalar_prefetch=2,
            grid=(1,),
            in_specs=[whole(moved.shape), whole(prefix.shape), whole(own.shape), whole(other.shape)]
            + [pl.BlockSpec(memory_space=pl.ANY)],
            out_specs=whole((GROUPS, 16, HD)),
        ),
        compiler_params=params(8),
        cost_estimate=pl.CostEstimate(
            flops=20000000, bytes_accessed=1300000, transcendentals=33000
        ),
        name="first_row",
    )(in_hbm(matching), in_hbm(starts), moved, prefix, own, other, after)


def merge_kernel(parts_ref, q_ref, kv_ref, out_ref):
    block = lax.axis_index("side") * 8 + lax.axis_index("tp")
    q = q_ref[0, :, :, pl.ds(pl.multiple_of(block * 512, 512), 512)].astype(f32)
    kv = kv_ref[0, :, :, pl.ds(pl.multiple_of((block // 2) * 256, 256), 256)].astype(f32)
    sub = lax.broadcasted_iota(jnp.int32, (ROWS, HD), 0)
    lane = lax.broadcasted_iota(jnp.int32, (ROWS, HD), 1)

    peaks, totals = [], []
    for b in range(BLOCKS):
        x = parts_ref[b, 128:144].astype(f32)[:ROWS]
        x = x + pltpu.roll(x, HD - 32, 1) + pltpu.roll(x, HD - 64, 1)
        peaks.append(x)
        totals.append(pltpu.roll(x, HD - 16, 1))
    top = functools.reduce(jnp.maximum, peaks)
    fresh = {}
    fresh_top = jnp.full((ROWS, HD), NEG_FILL, f32)
    for t in range(STEPS):
        for h in range(4):
            j = t * 4 + h
            qt = q[t, :, h * HD : (h + 1) * HD]
            for u in range(t + 1):
                s = jnp.sum(qt * kv[u, :, :HD], axis=-1, keepdims=True) * FACTOR
                fresh[j, u] = s
                fresh_top = jnp.where(lane == j, jnp.maximum(fresh_top, s), fresh_top)
    top = jnp.maximum(top, fresh_top)
    scales = [jnp.exp(p - top) for p in peaks]
    total = functools.reduce(jnp.add, [s * t for s, t in zip(scales, totals)])
    first = parts_ref[(block % 2) * 8 + block // 2, 144:160].astype(f32)
    for t in range(STEPS):
        for h in range(4):
            j = t * 4 + h
            acc = jnp.zeros((ROWS, HD), f32)
            for b in range(0, BLOCKS):
                tile = parts_ref[b, (j // 2) * 16 : (j // 2) * 16 + 16].astype(f32)
                acc += scales[b][:, j : j + 1] * tile[(j % 2) * 8 : (j % 2) * 8 + 8]
            denom = total[:, j : j + 1]
            for u in range(t + 1):
                w = jnp.exp(fresh[j, u] - top[:, j : j + 1])
                acc += w * kv[u, :, HD:]
                denom = denom + w
            out = acc / denom
            out = jnp.where(sub == 0, first[j : j + 1], out)
            out_ref[0, t, :, h * HD : (h + 1) * HD] = out.astype(bf16)


def merge(parts, decode_queries, decode_kv):
    shape = (1, STEPS, ROWS, 512)
    return pl.pallas_call(
        merge_kernel,
        out_shape=jax.ShapeDtypeStruct(shape, bf16),
        grid=(1,),
        in_specs=[whole(parts.shape), whole(decode_queries.shape), whole(decode_kv.shape)],
        out_specs=whole(shape),
        compiler_params=params(8),
        cost_estimate=pl.CostEstimate(flops=3000000, bytes_accessed=1300000, transcendentals=60000),
        name="merge",
    )(parts, decode_queries, decode_kv)


def local(
    segment_queries,
    segment_kv,
    prefix_kv,
    kv_cache,
    decode_queries,
    decode_kv,
    matching,
    segment_starts,
    cache_lengths,
):
    other_kv = lax.ppermute(segment_kv, "side", [(0, 1), (1, 0)])
    sent = prep(decode_queries, decode_kv)
    moved = lax.all_to_all(sent, "pair", split_axis=0, concat_axis=0, tiled=True)
    cache = (cache_lengths, decode_queries, kv_cache)
    parts = decode_parts(0, *cache, sent, sent)
    keys = (prefix_kv, segment_kv, other_kv)
    first = first_row(matching, segment_starts, moved, *keys, parts)
    parts = decode_parts(1, *cache, parts, first)
    first = lax.all_to_all(first, "pair", split_axis=0, concat_axis=0, tiled=True)
    parts = hand_over(matching, parts, first)
    out = prompt(segment_starts, segment_queries, *keys, parts)
    parts = lax.all_to_all(parts, ("side", "tp"), split_axis=0, concat_axis=0, tiled=True)
    decode_out = merge(parts, decode_queries, decode_kv)
    return (out, decode_out)


def solution(mesh):
    in_specs = (
        P("pair", "side", "tp"),
        P("pair", "side", "tp"),
        P("pair", None, "tp"),
        P("pair", None, ("side", "tp"), None),
        P("pair", None, None, None),
        P("pair", None, None, None),
        P(),
        P(),
        P("pair", None),
    )
    out_specs = (P("pair", "side", "tp"), P("pair", None, None, ("side", "tp")))
    return jax.shard_map(local, mesh=mesh, in_specs=in_specs, out_specs=out_specs, check_vma=False)
```

```python
import functools
import math

import jax
import jax.numpy as jnp
from jax import lax
from jax.experimental import pallas as pl
from jax.experimental.pallas import tpu as pltpu
from jax.sharding import PartitionSpec as P

H = 64
KVH = 8
HD = 128
STEPS = 4
ROWS = 8
GROUPS = 16
BLOCKS = 16
SEG_HALF = 512
PREFIX = 1024
CACHE_BLOCK = 128

FACTOR = 1.0 / math.sqrt(HD)
LOG2E = 1.4426950408889634
NEG_FILL = -1e30
PART_ROWS = 160

f32 = jnp.float32
bf16 = jnp.bfloat16


def params(mib):
    return pltpu.CompilerParams(vmem_limit_bytes=mib * 1024 * 1024)


def in_hbm(x):
    return pltpu.with_memory_space_constraint(x, pltpu.HBM)


def whole(shape):
    return pl.BlockSpec(shape, lambda *_: (0,) * len(shape))


def dot_t(a, b):
    return lax.dot_general(a, b, (((1,), (1,)), ((), ())), preferred_element_type=f32)


def dot(a, b):
    return jnp.dot(a, b, preferred_element_type=f32)


ASKED = 0
HOLDER = 1
START = 2


def prep_kernel(match_hbm, start_hbm, q_hbm, kv_hbm, out_ref, ctrl_ref, match, starts, q_ref, kv_ref, sems):
    side = lax.axis_index("side")
    tp = lax.axis_index("tp")
    group = lax.axis_index("pair")
    q_col = pl.multiple_of((2 * tp + side) * 512, 512)
    kv_col = pl.multiple_of(tp * 256, 256)
    copies = [
        pltpu.make_async_copy(match_hbm, match, sems.at[0]),
        pltpu.make_async_copy(start_hbm, starts, sems.at[1]),
        pltpu.make_async_copy(q_hbm.at[0, :, :, pl.ds(q_col, 512)], q_ref, sems.at[2]),
        pltpu.make_async_copy(kv_hbm.at[0, :, :, pl.ds(kv_col, 256)], kv_ref, sems.at[3]),
    ]
    for copy in copies:
        copy.start()
    for copy in copies:
        copy.wait()
    q = q_ref[...].astype(f32)
    kv = kv_ref[...].astype(f32)
    rows = [q[t, 0:1, h * HD : (h + 1) * HD] for t in range(STEPS) for h in range(4)]
    rows += [kv[u, 0:1, :HD] for u in range(STEPS)]
    rows += [kv[u, 0:1, HD:] for u in range(STEPS)]
    sent = jnp.concatenate(rows, axis=0).astype(bf16)
    for p in range(GROUPS):
        out_ref[p] = sent

    holder = jnp.int32(0)
    for p in range(GROUPS):
        holder = jnp.where(match[p] == group, p, holder)
    numbers = [match[group], holder, starts[group]]
    sub = lax.broadcasted_iota(jnp.int32, ctrl_ref.shape, 0)
    ctrl = jnp.zeros(ctrl_ref.shape, jnp.int32)
    for k, number in enumerate(numbers):
        ctrl = jnp.where(sub == k, number, ctrl)
    ctrl_ref[...] = ctrl


def prep(matching, starts, decode_queries, decode_kv):
    shape = (GROUPS, 24, HD)
    hbm = pl.BlockSpec(memory_space=pltpu.HBM)
    return pl.pallas_call(
        prep_kernel,
        out_shape=(
            jax.ShapeDtypeStruct(shape, bf16),
            jax.ShapeDtypeStruct((ROWS, HD), jnp.int32),
        ),
        grid=(1,),
        in_specs=[hbm] * 4,
        out_specs=(whole(shape), whole((ROWS, HD))),
        scratch_shapes=[
            pltpu.SMEM((GROUPS,), jnp.int32),
            pltpu.SMEM((GROUPS,), jnp.int32),
            pltpu.VMEM((STEPS, ROWS, 512), bf16),
            pltpu.VMEM((STEPS, ROWS, 256), bf16),
            pltpu.SemaphoreType.DMA((4,)),
        ],
        compiler_params=params(4),
        cost_estimate=pl.CostEstimate(flops=10000, bytes_accessed=200000, transcendentals=0),
        name="prep",
    )(in_hbm(matching), in_hbm(starts), in_hbm(decode_queries), in_hbm(decode_kv))


def pick(ctrl_ref, row, candidates_ref):
    wanted = ctrl_ref[row : row + 1, :]
    chosen = candidates_ref[0].astype(f32)
    for p in range(1, GROUPS):
        chosen = jnp.where(wanted == p, candidates_ref[p].astype(f32), chosen)
    return chosen


def decode_kernel(len_ref, q_ref, cache_ref, prior_ref, after_ref, out_ref):
    block = lax.axis_index("side") * 8 + lax.axis_index("tp")
    sub = lax.broadcasted_iota(jnp.int32, (ROWS, HD), 0)
    lane = lax.broadcasted_iota(jnp.int32, (ROWS, HD), 1)
    lens = jnp.zeros((ROWS, HD), jnp.int32)
    for k in range(ROWS - 1):
        lens = jnp.where(sub == k + 1, len_ref[0:1, k : k + 1], lens)
    allowed = (block * CACHE_BLOCK + lane < lens)[None]
    tiles = STEPS * 8
    small = lane % 32
    row_of = lax.broadcasted_iota(jnp.int32, (tiles * ROWS, HD), 0) % ROWS
    keep = [jnp.where(row_of == k + 1, 1.0, 0.0).astype(bf16) for k in range(ROWS - 1)]

    def spread(x):
        return jnp.concatenate([x * k for k in keep], axis=1)

    scores = []
    for head in range(2):
        q = jnp.concatenate(
            [
                q_ref[0, t, :, (head * 8 + g) * HD : (head * 8 + g + 1) * HD].astype(f32)
                for t in range(STEPS)
                for g in range(8)
            ],
            axis=0,
        ).astype(bf16)
        keys = jnp.concatenate(
            [cache_ref[0, k, :, head * 256 : head * 256 + HD] for k in range(ROWS - 1)], axis=1
        )
        scores.append(dot_t(spread(q), keys).reshape(tiles, ROWS, HD))
    for head in range(2):
        s = jnp.where(allowed, scores[head] * FACTOR, NEG_FILL)
        peak = jnp.max(s, axis=-1, keepdims=True)
        weights = jnp.where(allowed, jnp.exp(s - peak), 0.0)
        values = cache_ref[0, :, :, head * 256 + HD : head * 256 + 256].reshape(-1, HD)
        values = jnp.concatenate([values, jnp.ones_like(values)], axis=1)
        both = dot(spread(weights.reshape(tiles * ROWS, HD).astype(bf16)), values)
        both = both.reshape(STEPS, 8, ROWS, 2 * HD)
        peak = peak.reshape(STEPS, 8, ROWS, 1)
        for half in range(2):
            stats = jnp.zeros((ROWS, HD), f32)
            for t in range(STEPS):
                for h in range(4):
                    j = t * 4 + h
                    stats = jnp.where(small == j, peak[t, half * 4 + h], stats)
                    stats = jnp.where(small == 16 + j, both[t, half * 4 + h, :, HD:], stats)
            high = stats.astype(bf16).astype(f32)
            rest = stats - high
            mid = rest.astype(bf16).astype(f32)
            low = rest - mid
            packed = jnp.where(lane < 32, high, jnp.where(lane < 64, mid, low))
            slot = head * 2 + half
            mix = both[:, half * 4 : half * 4 + 4, :, :HD].reshape(128, HD)
            out_ref[slot, 0:128] = mix.astype(bf16)
            out_ref[slot, 128:144] = jnp.concatenate(
                [packed, jnp.zeros((ROWS, HD), f32)], axis=0
            ).astype(bf16)


def decode_parts(share, cache_lengths, decode_queries, kv_cache, prior, after):
    return pl.pallas_call(
        decode_kernel,
        out_shape=jax.ShapeDtypeStruct((BLOCKS, PART_ROWS, HD), bf16),
        grid=(2,),
        in_specs=[
            whole(cache_lengths.shape),
            pl.BlockSpec((1, STEPS, ROWS, 2048), lambda c: (0, 0, 0, 2 * share + c)),
            pl.BlockSpec((1, ROWS - 1, CACHE_BLOCK, 512), lambda c: (0, 0, 0, 2 * share + c)),
            pl.BlockSpec(memory_space=pl.ANY),
            pl.BlockSpec(memory_space=pl.ANY),
        ],
        out_specs=pl.BlockSpec((4, PART_ROWS, HD), lambda c: (2 * share + c, 0, 0)),
        input_output_aliases={3: 0} if share else {},
        compiler_params=params(16),
        cost_estimate=pl.CostEstimate(
            flops=1000000000, bytes_accessed=2400000, transcendentals=150000
        ),
        name="decode_parts",
    )(in_hbm(cache_lengths), in_hbm(decode_queries), in_hbm(kv_cache), prior, after)


def hand_over_kernel(ctrl_ref, got_ref, parts_in, parts_ref, chosen, sem):
    slot = 2 * lax.axis_index("tp") + lax.axis_index("side")
    chosen[...] = pick(ctrl_ref, HOLDER, got_ref).astype(bf16)
    copy = pltpu.make_async_copy(chosen, parts_ref.at[slot, 144:160], sem)
    copy.start()
    copy.wait()


def hand_over(ctrl, got, parts):
    return pl.pallas_call(
        hand_over_kernel,
        out_shape=jax.ShapeDtypeStruct(parts.shape, bf16),
        grid=(1,),
        in_specs=[whole(ctrl.shape), whole(got.shape), pl.BlockSpec(memory_space=pl.ANY)],
        out_specs=pl.BlockSpec(memory_space=pl.ANY),
        scratch_shapes=[pltpu.VMEM((16, HD), bf16), pltpu.SemaphoreType.DMA],
        input_output_aliases={2: 0},
        compiler_params=params(4),
        cost_estimate=pl.CostEstimate(flops=0, bytes_accessed=8192, transcendentals=0),
        name="hand_over",
    )(ctrl, got, parts)


def prompt_kernel(
    ctrl_ref, q_ref, prefix_ref, own_ref, other_ref, after_ref, out_hbm, mixed, least, done, sems
):
    side = lax.axis_index("side")
    tokens = 256
    scale = FACTOR * LOG2E

    pos = lax.broadcasted_iota(jnp.int32, (PREFIX, HD), 0)
    kept = jnp.where(pos < ctrl_ref[START : START + 1, :], 1.0, 0.0)
    mixed[SEG_HALF : SEG_HALF + PREFIX, :HD] = (prefix_ref[0, :, HD:].astype(f32) * kept).astype(bf16)
    mixed[SEG_HALF : SEG_HALF + PREFIX, HD:] = kept.astype(bf16)
    ones = jnp.ones((SEG_HALF, HD), bf16)
    mixed[:SEG_HALF] = jnp.concatenate([other_ref[0, :, HD:], ones], axis=1)
    mixed[SEG_HALF + PREFIX :] = jnp.concatenate([own_ref[0, :, HD:], ones], axis=1)

    def norm(ref):
        k = ref[0, :, :HD].astype(f32)
        return jnp.max(jnp.sum(k * k, axis=-1, keepdims=True), axis=0, keepdims=True)

    longest = jnp.maximum(norm(prefix_ref), jnp.maximum(norm(own_ref), norm(other_ref)))
    causal = lax.broadcasted_iota(jnp.int32, (tokens, tokens), 1) <= lax.broadcasted_iota(
        jnp.int32, (tokens, tokens), 0
    )

    def key_parts(half, later):
        parts = []
        if later:
            parts += [(other_ref, n) for n in range(0, SEG_HALF, 256)]
        parts += [(prefix_ref, n) for n in range(0, PREFIX, 256)]
        parts += [(own_ref, n) for n in range(0, (half + 1) * tokens, 256)]
        return parts

    def mix(weights, half, later):
        first = 0 if later else SEG_HALF
        last = SEG_HALF + PREFIX + (half + 1) * tokens
        return dot(jnp.concatenate(weights, axis=1), mixed[first:last])

    def queries(half, head):
        cols = pl.ds(pl.multiple_of(head * HD, HD), HD)
        return q_ref[0, half * tokens : (half + 1) * tokens, cols]

    def block(half, head, later):
        q = queries(half, head)
        wide_q = q.astype(f32)
        norms = jnp.sum(wide_q * wide_q, axis=-1, keepdims=True)
        bound = jnp.sqrt(norms * longest) * scale
        parts = key_parts(half, later)
        weights = []
        for number, (ref, n) in enumerate(parts):
            w = jnp.exp2(dot_t(q, ref[0, n : n + 256, :HD]) * scale - bound)
            if number == len(parts) - 1:
                w = jnp.where(causal, w, 0.0)
            weights.append(w.astype(bf16))
        total = mix(weights, half, later)
        sums = total[:, HD:]
        least[...] = jnp.minimum(least[...], sums)
        return (total[:, :HD] / sums).astype(bf16)

    def block_exact(half, head, later):
        q = queries(half, head)
        parts = key_parts(half, later)
        scores = []
        for number, (ref, n) in enumerate(parts):
            s = dot_t(q, ref[0, n : n + 256, :HD])
            if ref is prefix_ref:
                at = n + lax.broadcasted_iota(jnp.int32, s.shape, 1)
                s = jnp.where(at < ctrl_ref[START : START + 1, 0:1], s, NEG_FILL)
            if number == len(parts) - 1:
                s = jnp.where(causal, s, NEG_FILL)
            scores.append(s)
        peak = functools.reduce(
            jnp.maximum, [jnp.max(s, axis=-1, keepdims=True) for s in scores]
        )
        weights = [jnp.exp2((s - peak) * scale).astype(bf16) for s in scores]
        total = mix(weights, half, later)
        return (total[:, :HD] / total[:, HD:]).astype(bf16)

    def result_copy(pair, slot):
        cols = pl.ds(pl.multiple_of(pair * 2 * HD, 2 * HD), 2 * HD)
        return pltpu.make_async_copy(done.at[slot], out_hbm.at[0, :, cols], sems.at[slot])

    def two_heads(one, pair, slot, later):
        for half in range(2):
            for head in range(2):
                done[slot, half * tokens : (half + 1) * tokens, head * HD : (head + 1) * HD] = one(
                    half, pair * 2 + head, later
                )
        result_copy(pair, slot).start()

    least[...] = jnp.ones(least.shape, f32)
    for later in (False, True):

        @pl.when(side == int(later))
        def _(later=later):
            @pl.loop(0, 2)
            def _(step):
                for slot in range(2):

                    @pl.when(step > 0)
                    def _():
                        result_copy(slot, slot).wait()

                for slot in range(2):
                    two_heads(block, step * 2 + slot, slot, later)

            for slot in range(2):
                result_copy(2 + slot, slot).wait()

            @pl.when(jnp.min(least[...]) < 1e-27)
            def _():
                @pl.loop(0, 4)
                def _(pair):
                    two_heads(block_exact, pair, 0, later)
                    result_copy(pair, 0).wait()


def prompt(ctrl, queries, prefix, own, other, after):
    return pl.pallas_call(
        prompt_kernel,
        out_shape=jax.ShapeDtypeStruct(queries.shape, bf16),
        grid=(1,),
        in_specs=[
            whole(ctrl.shape),
            whole(queries.shape),
            whole(prefix.shape),
            whole(own.shape),
            whole(other.shape),
            pl.BlockSpec(memory_space=pl.ANY),
        ],
        out_specs=pl.BlockSpec(memory_space=pltpu.HBM),
        scratch_shapes=[
            pltpu.VMEM((2 * SEG_HALF + PREFIX, 2 * HD), bf16),
            pltpu.VMEM((256, HD), f32),
            pltpu.VMEM((2, 512, 2 * HD), bf16),
            pltpu.SemaphoreType.DMA((2,)),
        ],
        compiler_params=params(32),
        cost_estimate=pl.CostEstimate(
            flops=4096 * 1920 * 128 * 8, bytes_accessed=3000000, transcendentals=4096 * 1920
        ),
        name="prompt",
    )(ctrl, queries, prefix, own, other, after)


def first_row_kernel(ctrl_ref, got_ref, prefix_ref, own_ref, other_ref, after_ref, out_ref):
    asked = pick(ctrl_ref, ASKED, got_ref)
    q = asked[0:16].astype(bf16)
    fresh = asked[16:24]
    pad = jnp.zeros((12, HD), f32)
    fresh_k = jnp.concatenate([fresh[:4], pad], axis=0).astype(bf16)
    fresh_v = jnp.concatenate([fresh[4:], pad], axis=0).astype(bf16)
    s0 = dot_t(q, prefix_ref[0, :, :HD])
    pos = lax.broadcasted_iota(jnp.int32, s0.shape, 1)
    s0 = jnp.where(pos < ctrl_ref[START : START + 1, 0:1], s0, NEG_FILL)
    s1 = dot_t(q, own_ref[0, :, :HD])
    s2 = dot_t(q, other_ref[0, :, :HD])
    s3 = dot_t(q, fresh_k)
    step = lax.broadcasted_iota(jnp.int32, s3.shape, 0) // 4
    pos = lax.broadcasted_iota(jnp.int32, s3.shape, 1)
    s3 = jnp.where(pos <= step, s3, NEG_FILL)
    scores = (s0, s1, s2, s3)
    values = (prefix_ref[0, :, HD:], own_ref[0, :, HD:], other_ref[0, :, HD:], fresh_v)
    peak = functools.reduce(jnp.maximum, [jnp.max(s, axis=-1, keepdims=True) for s in scores])
    mix = jnp.zeros((16, HD), f32)
    totals = jnp.zeros((16, 1), f32)
    for s, v in zip(scores, values):
        w = jnp.exp2((s - peak) * (FACTOR * LOG2E))
        totals += jnp.sum(w, axis=-1, keepdims=True)
        mix += dot(w.astype(bf16), v)
    out = (mix / totals).astype(bf16)
    for p in range(GROUPS):
        out_ref[p] = out


def first_row(ctrl, got, prefix, own, other, after):
    shape = (GROUPS, 16, HD)
    return pl.pallas_call(
        first_row_kernel,
        out_shape=jax.ShapeDtypeStruct(shape, bf16),
        grid=(1,),
        in_specs=[
            whole(ctrl.shape),
            whole(got.shape),
            whole(prefix.shape),
            whole(own.shape),
            whole(other.shape),
            pl.BlockSpec(memory_space=pl.ANY),
        ],
        out_specs=whole(shape),
        compiler_params=params(8),
        cost_estimate=pl.CostEstimate(
            flops=20000000, bytes_accessed=1300000, transcendentals=33000
        ),
        name="first_row",
    )(ctrl, got, prefix, own, other, after)


def merge_kernel(parts_ref, q_ref, kv_ref, out_ref):
    block = lax.axis_index("side") * 8 + lax.axis_index("tp")
    q = q_ref[0, :, :, pl.ds(pl.multiple_of(block * 512, 512), 512)].astype(f32)
    kv = kv_ref[0, :, :, pl.ds(pl.multiple_of((block // 2) * 256, 256), 256)].astype(f32)
    sub = lax.broadcasted_iota(jnp.int32, (ROWS, HD), 0)
    lane = lax.broadcasted_iota(jnp.int32, (ROWS, HD), 1)

    peaks, totals = [], []
    for b in range(BLOCKS):
        x = parts_ref[b, 128:144].astype(f32)[:ROWS]
        x = x + pltpu.roll(x, HD - 32, 1) + pltpu.roll(x, HD - 64, 1)
        peaks.append(x)
        totals.append(pltpu.roll(x, HD - 16, 1))
    top = functools.reduce(jnp.maximum, peaks)
    fresh = {}
    fresh_top = jnp.full((ROWS, HD), NEG_FILL, f32)
    for t in range(STEPS):
        for h in range(4):
            j = t * 4 + h
            qt = q[t, :, h * HD : (h + 1) * HD]
            for u in range(t + 1):
                s = jnp.sum(qt * kv[u, :, :HD], axis=-1, keepdims=True) * FACTOR
                fresh[j, u] = s
                fresh_top = jnp.where(lane == j, jnp.maximum(fresh_top, s), fresh_top)
    top = jnp.maximum(top, fresh_top)
    scales = [jnp.exp(p - top) for p in peaks]
    total = functools.reduce(jnp.add, [s * t for s, t in zip(scales, totals)])
    first = parts_ref[(block % 2) * 8 + block // 2, 144:160].astype(f32)
    for t in range(STEPS):
        for h in range(4):
            j = t * 4 + h
            acc = jnp.zeros((ROWS, HD), f32)
            for b in range(0, BLOCKS):
                tile = parts_ref[b, (j // 2) * 16 : (j // 2) * 16 + 16].astype(f32)
                acc += scales[b][:, j : j + 1] * tile[(j % 2) * 8 : (j % 2) * 8 + 8]
            denom = total[:, j : j + 1]
            for u in range(t + 1):
                w = jnp.exp(fresh[j, u] - top[:, j : j + 1])
                acc += w * kv[u, :, HD:]
                denom = denom + w
            out = acc / denom
            out = jnp.where(sub == 0, first[j : j + 1], out)
            out_ref[0, t, :, h * HD : (h + 1) * HD] = out.astype(bf16)


def merge(parts, decode_queries, decode_kv):
    shape = (1, STEPS, ROWS, 512)
    return pl.pallas_call(
        merge_kernel,
        out_shape=jax.ShapeDtypeStruct(shape, bf16),
        grid=(1,),
        in_specs=[whole(parts.shape), whole(decode_queries.shape), whole(decode_kv.shape)],
        out_specs=whole(shape),
        compiler_params=params(8),
        cost_estimate=pl.CostEstimate(flops=3000000, bytes_accessed=1300000, transcendentals=60000),
        name="merge",
    )(parts, decode_queries, decode_kv)


def exchange(x, axis):
    return lax.all_to_all(x, axis, split_axis=0, concat_axis=0, tiled=True)


def local(
    segment_queries,
    segment_kv,
    prefix_kv,
    kv_cache,
    decode_queries,
    decode_kv,
    matching,
    segment_starts,
    cache_lengths,
):
    other_kv = lax.ppermute(segment_kv, "side", [(0, 1), (1, 0)])
    keys = (prefix_kv, segment_kv, other_kv)
    sent, ctrl = prep(matching, segment_starts, decode_queries, decode_kv)
    cache = (cache_lengths, decode_queries, kv_cache)
    parts = decode_parts(0, *cache, sent, sent)
    first = first_row(ctrl, exchange(sent, "pair"), *keys, parts)
    parts = decode_parts(1, *cache, parts, first)
    parts = hand_over(ctrl, exchange(first, "pair"), parts)
    out = prompt(ctrl, segment_queries, *keys, parts)
    parts = exchange(parts, ("side", "tp"))
    decode_out = merge(parts, decode_queries, decode_kv)
    return (out, decode_out)


def solution(mesh):
    in_specs = (
        P("pair", "side", "tp"),
        P("pair", "side", "tp"),
        P("pair", None, "tp"),
        P("pair", None, ("side", "tp"), None),
        P("pair", None, None, None),
        P("pair", None, None, None),
        P(),
        P(),
        P("pair", None),
    )
    out_specs = (P("pair", "side", "tp"), P("pair", None, None, ("side", "tp")))
    return jax.shard_map(local, mesh=mesh, in_specs=in_specs, out_specs=out_specs, check_vma=False)
```

```python
import functools
import math

import jax
import jax.numpy as jnp
from jax import lax
from jax.experimental import pallas as pl
from jax.experimental.pallas import tpu as pltpu
from jax.sharding import PartitionSpec as P

H = 64
KVH = 8
HD = 128
STEPS = 4
ROWS = 8
GROUPS = 16
BLOCKS = 16
SEG_HALF = 512
PREFIX = 1024
CACHE_BLOCK = 128

FACTOR = 1.0 / math.sqrt(HD)
LOG2E = 1.4426950408889634
NEG_FILL = -1e30
PART_ROWS = 160

f32 = jnp.float32
bf16 = jnp.bfloat16


def params(mib):
    return pltpu.CompilerParams(vmem_limit_bytes=mib * 1024 * 1024)


def in_hbm(x):
    return pltpu.with_memory_space_constraint(x, pltpu.HBM)


def whole(shape):
    return pl.BlockSpec(shape, lambda *_: (0,) * len(shape))


def dot_t(a, b):
    return lax.dot_general(a, b, (((1,), (1,)), ((), ())), preferred_element_type=f32)


def dot(a, b):
    return jnp.dot(a, b, preferred_element_type=f32)


ASKED = 0
HOLDER = 1
START = 2


def prep_kernel(match_hbm, start_hbm, q_hbm, kv_hbm, out_ref, ctrl_ref, match, starts, q_ref, kv_ref, sems):
    side = lax.axis_index("side")
    tp = lax.axis_index("tp")
    group = lax.axis_index("pair")
    q_col = pl.multiple_of((2 * tp + side) * 512, 512)
    kv_col = pl.multiple_of(tp * 256, 256)
    copies = [
        pltpu.make_async_copy(match_hbm, match, sems.at[0]),
        pltpu.make_async_copy(start_hbm, starts, sems.at[1]),
        pltpu.make_async_copy(q_hbm.at[0, :, :, pl.ds(q_col, 512)], q_ref, sems.at[2]),
        pltpu.make_async_copy(kv_hbm.at[0, :, :, pl.ds(kv_col, 256)], kv_ref, sems.at[3]),
    ]
    for copy in copies:
        copy.start()
    for copy in copies:
        copy.wait()
    q = q_ref[...].astype(f32)
    kv = kv_ref[...].astype(f32)
    rows = [q[t, 0:1, h * HD : (h + 1) * HD] for t in range(STEPS) for h in range(4)]
    rows += [kv[u, 0:1, :HD] for u in range(STEPS)]
    rows += [kv[u, 0:1, HD:] for u in range(STEPS)]
    sent = jnp.concatenate(rows, axis=0).astype(bf16)
    for p in range(GROUPS):
        out_ref[p] = sent

    holder = jnp.int32(0)
    for p in range(GROUPS):
        holder = jnp.where(match[p] == group, p, holder)
    numbers = [match[group], holder, starts[group]]
    sub = lax.broadcasted_iota(jnp.int32, ctrl_ref.shape, 0)
    ctrl = jnp.zeros(ctrl_ref.shape, f32)
    for k, number in enumerate(numbers):
        ctrl = jnp.where(sub == k, number.astype(f32), ctrl)
    ctrl_ref[...] = ctrl


def prep(matching, starts, decode_queries, decode_kv):
    shape = (GROUPS, 24, HD)
    hbm = pl.BlockSpec(memory_space=pltpu.HBM)
    return pl.pallas_call(
        prep_kernel,
        out_shape=(
            jax.ShapeDtypeStruct(shape, bf16),
            jax.ShapeDtypeStruct((ROWS, HD), f32),
        ),
        grid=(1,),
        in_specs=[hbm] * 4,
        out_specs=(whole(shape), whole((ROWS, HD))),
        scratch_shapes=[
            pltpu.SMEM((GROUPS,), jnp.int32),
            pltpu.SMEM((GROUPS,), jnp.int32),
            pltpu.VMEM((STEPS, ROWS, 512), bf16),
            pltpu.VMEM((STEPS, ROWS, 256), bf16),
            pltpu.SemaphoreType.DMA((4,)),
        ],
        compiler_params=params(4),
        cost_estimate=pl.CostEstimate(flops=10000, bytes_accessed=200000, transcendentals=0),
        name="prep",
    )(in_hbm(matching), in_hbm(starts), in_hbm(decode_queries), in_hbm(decode_kv))


def number_of(ctrl_ref, row):
    return jnp.max(ctrl_ref[row : row + 1, :]).astype(jnp.int32)


def decode_kernel(len_ref, q_ref, cache_ref, prior_ref, after_ref, out_ref):
    block = lax.axis_index("side") * 8 + lax.axis_index("tp")
    sub = lax.broadcasted_iota(jnp.int32, (ROWS, HD), 0)
    lane = lax.broadcasted_iota(jnp.int32, (ROWS, HD), 1)
    lens = jnp.zeros((ROWS, HD), jnp.int32)
    for k in range(ROWS - 1):
        lens = jnp.where(sub == k + 1, len_ref[0:1, k : k + 1], lens)
    allowed = (block * CACHE_BLOCK + lane < lens)[None]
    tiles = STEPS * 8
    small = lane % 32
    row_of = lax.broadcasted_iota(jnp.int32, (tiles * ROWS, HD), 0) % ROWS
    keep = [jnp.where(row_of == k + 1, 1.0, 0.0).astype(bf16) for k in range(ROWS - 1)]

    def spread(x):
        return jnp.concatenate([x * k for k in keep], axis=1)

    scores = []
    for head in range(2):
        q = jnp.concatenate(
            [
                q_ref[0, t, :, (head * 8 + g) * HD : (head * 8 + g + 1) * HD].astype(f32)
                for t in range(STEPS)
                for g in range(8)
            ],
            axis=0,
        ).astype(bf16)
        keys = jnp.concatenate(
            [cache_ref[0, k, :, head * 256 : head * 256 + HD] for k in range(ROWS - 1)], axis=1
        )
        scores.append(dot_t(spread(q), keys).reshape(tiles, ROWS, HD))
    for head in range(2):
        s = jnp.where(allowed, scores[head] * FACTOR, NEG_FILL)
        peak = jnp.max(s, axis=-1, keepdims=True)
        weights = jnp.where(allowed, jnp.exp(s - peak), 0.0)
        values = cache_ref[0, :, :, head * 256 + HD : head * 256 + 256].reshape(-1, HD)
        values = jnp.concatenate([values, jnp.ones_like(values)], axis=1)
        both = dot(spread(weights.reshape(tiles * ROWS, HD).astype(bf16)), values)
        both = both.reshape(STEPS, 8, ROWS, 2 * HD)
        peak = peak.reshape(STEPS, 8, ROWS, 1)
        for half in range(2):
            stats = jnp.zeros((ROWS, HD), f32)
            for t in range(STEPS):
                for h in range(4):
                    j = t * 4 + h
                    stats = jnp.where(small == j, peak[t, half * 4 + h], stats)
                    stats = jnp.where(small == 16 + j, both[t, half * 4 + h, :, HD:], stats)
            high = stats.astype(bf16).astype(f32)
            rest = stats - high
            mid = rest.astype(bf16).astype(f32)
            low = rest - mid
            packed = jnp.where(lane < 32, high, jnp.where(lane < 64, mid, low))
            slot = head * 2 + half
            mix = both[:, half * 4 : half * 4 + 4, :, :HD].reshape(128, HD)
            out_ref[slot, 0:128] = mix.astype(bf16)
            out_ref[slot, 128:144] = jnp.concatenate(
                [packed, jnp.zeros((ROWS, HD), f32)], axis=0
            ).astype(bf16)


def decode_parts(share, cache_lengths, decode_queries, kv_cache, prior, after):
    return pl.pallas_call(
        decode_kernel,
        out_shape=jax.ShapeDtypeStruct((BLOCKS, PART_ROWS, HD), bf16),
        grid=(2,),
        in_specs=[
            whole(cache_lengths.shape),
            pl.BlockSpec((1, STEPS, ROWS, 2048), lambda c: (0, 0, 0, 2 * share + c)),
            pl.BlockSpec((1, ROWS - 1, CACHE_BLOCK, 512), lambda c: (0, 0, 0, 2 * share + c)),
            pl.BlockSpec(memory_space=pl.ANY),
            pl.BlockSpec(memory_space=pl.ANY),
        ],
        out_specs=pl.BlockSpec((4, PART_ROWS, HD), lambda c: (2 * share + c, 0, 0)),
        input_output_aliases={3: 0} if share else {},
        compiler_params=params(16),
        cost_estimate=pl.CostEstimate(
            flops=1000000000, bytes_accessed=2400000, transcendentals=150000
        ),
        name="decode_parts",
    )(in_hbm(cache_lengths), in_hbm(decode_queries), in_hbm(kv_cache), prior, after)


def hand_over_kernel(ctrl_ref, got_ref, parts_in, parts_ref, sem):
    slot = 2 * lax.axis_index("tp") + lax.axis_index("side")
    holder = number_of(ctrl_ref, HOLDER)
    copy = pltpu.make_async_copy(got_ref.at[holder], parts_ref.at[slot, 144:160], sem)
    copy.start()
    copy.wait()


def hand_over(ctrl, got, parts):
    return pl.pallas_call(
        hand_over_kernel,
        out_shape=jax.ShapeDtypeStruct(parts.shape, bf16),
        grid=(1,),
        in_specs=[whole(ctrl.shape), whole(got.shape), pl.BlockSpec(memory_space=pl.ANY)],
        out_specs=pl.BlockSpec(memory_space=pl.ANY),
        scratch_shapes=[pltpu.SemaphoreType.DMA],
        input_output_aliases={2: 0},
        compiler_params=params(4),
        cost_estimate=pl.CostEstimate(flops=0, bytes_accessed=8192, transcendentals=0),
        name="hand_over",
    )(ctrl, got, parts)


def setup_kernel(ctrl_ref, prefix_ref, own_ref, other_ref, after_ref, mixed, longest_ref):
    pos = lax.broadcasted_iota(jnp.int32, (PREFIX, HD), 0).astype(f32)
    kept = jnp.where(pos < ctrl_ref[START : START + 1, :], 1.0, 0.0)
    mixed[SEG_HALF : SEG_HALF + PREFIX, :HD] = (prefix_ref[0, :, HD:].astype(f32) * kept).astype(bf16)
    mixed[SEG_HALF : SEG_HALF + PREFIX, HD:] = kept.astype(bf16)
    ones = jnp.ones((SEG_HALF, HD), bf16)
    mixed[:SEG_HALF] = jnp.concatenate([other_ref[0, :, HD:], ones], axis=1)
    mixed[SEG_HALF + PREFIX :] = jnp.concatenate([own_ref[0, :, HD:], ones], axis=1)

    def norm(ref):
        k = ref[0, :, :HD].astype(f32)
        return jnp.max(jnp.sum(k * k, axis=-1, keepdims=True), axis=0, keepdims=True)

    longest = jnp.maximum(norm(prefix_ref), jnp.maximum(norm(own_ref), norm(other_ref)))
    longest_ref[...] = jnp.broadcast_to(longest, longest_ref.shape)


def setup(ctrl, prefix, own, other, after):
    shapes = ((2 * SEG_HALF + PREFIX, 2 * HD), (ROWS, HD))
    return pl.pallas_call(
        setup_kernel,
        out_shape=(
            jax.ShapeDtypeStruct(shapes[0], bf16),
            jax.ShapeDtypeStruct(shapes[1], f32),
        ),
        grid=(1,),
        in_specs=[
            whole(ctrl.shape),
            whole(prefix.shape),
            whole(own.shape),
            whole(other.shape),
            pl.BlockSpec(memory_space=pl.ANY),
        ],
        out_specs=(whole(shapes[0]), whole(shapes[1])),
        compiler_params=params(12),
        cost_estimate=pl.CostEstimate(flops=2000000, bytes_accessed=2000000, transcendentals=0),
        name="setup",
    )(ctrl, prefix, own, other, after)


def prompt_kernel(
    ctrl_ref,
    q_ref,
    prefix_ref,
    own_ref,
    other_ref,
    mixed,
    longest_ref,
    after_ref,
    out_hbm,
    least,
    done,
    sems,
):
    side = lax.axis_index("side")
    tokens = 256
    scale = FACTOR * LOG2E
    longest = longest_ref[0:1, 0:1]
    causal = lax.broadcasted_iota(jnp.int32, (tokens, tokens), 1) <= lax.broadcasted_iota(
        jnp.int32, (tokens, tokens), 0
    )

    def key_parts(half, later):
        parts = []
        if later:
            parts += [(other_ref, n) for n in range(0, SEG_HALF, 256)]
        parts += [(prefix_ref, n) for n in range(0, PREFIX, 256)]
        parts += [(own_ref, n) for n in range(0, (half + 1) * tokens, 256)]
        return parts

    def mix(weights, half, later):
        first = 0 if later else SEG_HALF
        last = SEG_HALF + PREFIX + (half + 1) * tokens
        return dot(jnp.concatenate(weights, axis=1), mixed[first:last])

    def lanes(start, size):
        return pl.ds(start if isinstance(start, int) else pl.multiple_of(start, size), size)

    def queries(half, head):
        cols = lanes(head * HD, HD)
        return q_ref[0, half * tokens : (half + 1) * tokens, cols]

    def block(half, head, later):
        q = queries(half, head)
        wide_q = q.astype(f32)
        norms = jnp.sum(wide_q * wide_q, axis=-1, keepdims=True)
        bound = jnp.sqrt(norms * longest) * scale
        parts = key_parts(half, later)
        weights = []
        for number, (ref, n) in enumerate(parts):
            w = jnp.exp2(dot_t(q, ref[0, n : n + 256, :HD]) * scale - bound)
            if number == len(parts) - 1:
                w = jnp.where(causal, w, 0.0)
            weights.append(w.astype(bf16))
        total = mix(weights, half, later)
        sums = total[:, HD:]
        least[...] = jnp.minimum(least[...], sums)
        return (total[:, :HD] / sums).astype(bf16)

    def block_exact(half, head, later):
        q = queries(half, head)
        parts = key_parts(half, later)
        scores = []
        for number, (ref, n) in enumerate(parts):
            s = dot_t(q, ref[0, n : n + 256, :HD])
            if ref is prefix_ref:
                at = n + lax.broadcasted_iota(jnp.int32, s.shape, 1)
                s = jnp.where(at.astype(f32) < ctrl_ref[START : START + 1, 0:1], s, NEG_FILL)
            if number == len(parts) - 1:
                s = jnp.where(causal, s, NEG_FILL)
            scores.append(s)
        peak = functools.reduce(
            jnp.maximum, [jnp.max(s, axis=-1, keepdims=True) for s in scores]
        )
        weights = [jnp.exp2((s - peak) * scale).astype(bf16) for s in scores]
        total = mix(weights, half, later)
        return (total[:, :HD] / total[:, HD:]).astype(bf16)

    def result_copy(pair, slot):
        cols = lanes(pair * 2 * HD, 2 * HD)
        return pltpu.make_async_copy(done.at[slot], out_hbm.at[0, :, cols], sems.at[slot])

    def two_heads(one, pair, slot, later):
        for half in range(2):
            for head in range(2):
                done[slot, half * tokens : (half + 1) * tokens, head * HD : (head + 1) * HD] = one(
                    half, pair * 2 + head, later
                )
        result_copy(pair, slot).start()

    least[...] = jnp.ones(least.shape, f32)
    for later in (False, True):

        @pl.when(side == int(later))
        def _(later=later):
            for pair in range(4):
                two_heads(block, pair, pair, later)
            loose = jnp.min(least[...]) < 1e-27
            for pair in range(4):
                result_copy(pair, pair).wait()

            @pl.when(loose)
            def _():
                @pl.loop(0, 4)
                def _(pair):
                    two_heads(block_exact, pair, 0, later)
                    result_copy(pair, 0).wait()


def prompt(ctrl, queries, prefix, own, other, mixed, longest, after):
    return pl.pallas_call(
        prompt_kernel,
        out_shape=jax.ShapeDtypeStruct(queries.shape, bf16),
        grid=(1,),
        in_specs=[
            whole(ctrl.shape),
            whole(queries.shape),
            whole(prefix.shape),
            whole(own.shape),
            whole(other.shape),
            whole(mixed.shape),
            whole(longest.shape),
            pl.BlockSpec(memory_space=pl.ANY),
        ],
        out_specs=pl.BlockSpec(memory_space=pltpu.HBM),
        scratch_shapes=[
            pltpu.VMEM((256, HD), f32),
            pltpu.VMEM((4, 512, 2 * HD), bf16),
            pltpu.SemaphoreType.DMA((4,)),
        ],
        compiler_params=params(32),
        cost_estimate=pl.CostEstimate(
            flops=4096 * 1920 * 128 * 8, bytes_accessed=3000000, transcendentals=4096 * 1920
        ),
        name="prompt",
    )(ctrl, queries, prefix, own, other, mixed, longest, after)


def first_row_kernel(ctrl_ref, got_ref, prefix_ref, own_ref, other_ref, after_ref, out_ref):
    asked = got_ref[number_of(ctrl_ref, ASKED)].astype(f32)
    q = asked[0:16].astype(bf16)
    fresh = asked[16:24]
    pad = jnp.zeros((12, HD), f32)
    fresh_k = jnp.concatenate([fresh[:4], pad], axis=0).astype(bf16)
    fresh_v = jnp.concatenate([fresh[4:], pad], axis=0).astype(bf16)
    s0 = dot_t(q, prefix_ref[0, :, :HD])
    pos = lax.broadcasted_iota(jnp.int32, s0.shape, 1)
    s0 = jnp.where(pos.astype(f32) < ctrl_ref[START : START + 1, 0:1], s0, NEG_FILL)
    s1 = dot_t(q, own_ref[0, :, :HD])
    s2 = dot_t(q, other_ref[0, :, :HD])
    s3 = dot_t(q, fresh_k)
    step = lax.broadcasted_iota(jnp.int32, s3.shape, 0) // 4
    pos = lax.broadcasted_iota(jnp.int32, s3.shape, 1)
    s3 = jnp.where(pos <= step, s3, NEG_FILL)
    scores = (s0, s1, s2, s3)
    values = (prefix_ref[0, :, HD:], own_ref[0, :, HD:], other_ref[0, :, HD:], fresh_v)
    peak = functools.reduce(jnp.maximum, [jnp.max(s, axis=-1, keepdims=True) for s in scores])
    mix = jnp.zeros((16, HD), f32)
    totals = jnp.zeros((16, 1), f32)
    for s, v in zip(scores, values):
        w = jnp.exp2((s - peak) * (FACTOR * LOG2E))
        totals += jnp.sum(w, axis=-1, keepdims=True)
        mix += dot(w.astype(bf16), v)
    out = (mix / totals).astype(bf16)
    for p in range(GROUPS):
        out_ref[p] = out


def first_row(ctrl, got, prefix, own, other, after):
    shape = (GROUPS, 16, HD)
    return pl.pallas_call(
        first_row_kernel,
        out_shape=jax.ShapeDtypeStruct(shape, bf16),
        grid=(1,),
        in_specs=[
            whole(ctrl.shape),
            whole(got.shape),
            whole(prefix.shape),
            whole(own.shape),
            whole(other.shape),
            pl.BlockSpec(memory_space=pl.ANY),
        ],
        out_specs=whole(shape),
        compiler_params=params(8),
        cost_estimate=pl.CostEstimate(
            flops=20000000, bytes_accessed=1300000, transcendentals=33000
        ),
        name="first_row",
    )(ctrl, got, prefix, own, other, after)


def merge_kernel(parts_ref, q_ref, kv_ref, out_ref):
    block = lax.axis_index("side") * 8 + lax.axis_index("tp")
    q = q_ref[0, :, :, pl.ds(pl.multiple_of(block * 512, 512), 512)].astype(f32)
    kv = kv_ref[0, :, :, pl.ds(pl.multiple_of((block // 2) * 256, 256), 256)].astype(f32)
    sub = lax.broadcasted_iota(jnp.int32, (ROWS, HD), 0)
    lane = lax.broadcasted_iota(jnp.int32, (ROWS, HD), 1)

    peaks, totals = [], []
    for b in range(BLOCKS):
        x = parts_ref[b, 128:144].astype(f32)[:ROWS]
        x = x + pltpu.roll(x, HD - 32, 1) + pltpu.roll(x, HD - 64, 1)
        peaks.append(x)
        totals.append(pltpu.roll(x, HD - 16, 1))
    top = functools.reduce(jnp.maximum, peaks)
    fresh = {}
    fresh_top = jnp.full((ROWS, HD), NEG_FILL, f32)
    for t in range(STEPS):
        for h in range(4):
            j = t * 4 + h
            qt = q[t, :, h * HD : (h + 1) * HD]
            for u in range(t + 1):
                s = jnp.sum(qt * kv[u, :, :HD], axis=-1, keepdims=True) * FACTOR
                fresh[j, u] = s
                fresh_top = jnp.where(lane == j, jnp.maximum(fresh_top, s), fresh_top)
    top = jnp.maximum(top, fresh_top)
    scales = [jnp.exp(p - top) for p in peaks]
    total = functools.reduce(jnp.add, [s * t for s, t in zip(scales, totals)])
    first = parts_ref[(block % 2) * 8 + block // 2, 144:160].astype(f32)
    for t in range(STEPS):
        for h in range(4):
            j = t * 4 + h
            acc = jnp.zeros((ROWS, HD), f32)
            for b in range(0, BLOCKS):
                tile = parts_ref[b, (j // 2) * 16 : (j // 2) * 16 + 16].astype(f32)
                acc += scales[b][:, j : j + 1] * tile[(j % 2) * 8 : (j % 2) * 8 + 8]
            denom = total[:, j : j + 1]
            for u in range(t + 1):
                w = jnp.exp(fresh[j, u] - top[:, j : j + 1])
                acc += w * kv[u, :, HD:]
                denom = denom + w
            out = acc / denom
            out = jnp.where(sub == 0, first[j : j + 1], out)
            out_ref[0, t, :, h * HD : (h + 1) * HD] = out.astype(bf16)


def merge(parts, decode_queries, decode_kv):
    shape = (1, STEPS, ROWS, 512)
    return pl.pallas_call(
        merge_kernel,
        out_shape=jax.ShapeDtypeStruct(shape, bf16),
        grid=(1,),
        in_specs=[whole(parts.shape), whole(decode_queries.shape), whole(decode_kv.shape)],
        out_specs=whole(shape),
        compiler_params=params(8),
        cost_estimate=pl.CostEstimate(flops=3000000, bytes_accessed=1300000, transcendentals=60000),
        name="merge",
    )(parts, decode_queries, decode_kv)


def exchange(x, axis):
    return lax.all_to_all(x, axis, split_axis=0, concat_axis=0, tiled=True)


def local(
    segment_queries,
    segment_kv,
    prefix_kv,
    kv_cache,
    decode_queries,
    decode_kv,
    matching,
    segment_starts,
    cache_lengths,
):
    other_kv = lax.ppermute(segment_kv, "side", [(0, 1), (1, 0)])
    sent, ctrl = prep(matching, segment_starts, decode_queries, decode_kv)
    sent, prefix, own, queries = lax.optimization_barrier(
        (sent, prefix_kv, segment_kv, segment_queries)
    )
    keys = (prefix, own, other_kv)
    cache = (cache_lengths, decode_queries, kv_cache)
    parts = decode_parts(0, *cache, sent, sent)
    mixed, longest = setup(ctrl, *keys, parts)
    first = first_row(ctrl, exchange(sent, "pair"), *keys, longest)
    parts = decode_parts(1, *cache, parts, first)
    parts = hand_over(ctrl, exchange(first, "pair"), parts)
    out = prompt(ctrl, queries, *keys, mixed, longest, parts)
    parts = exchange(parts, ("side", "tp"))
    decode_out = merge(parts, decode_queries, decode_kv)
    return (out, decode_out)


def solution(mesh):
    in_specs = (
        P("pair", "side", "tp"),
        P("pair", "side", "tp"),
        P("pair", None, "tp"),
        P("pair", None, ("side", "tp"), None),
        P("pair", None, None, None),
        P("pair", None, None, None),
        P(),
        P(),
        P("pair", None),
    )
    out_specs = (P("pair", "side", "tp"), P("pair", None, None, ("side", "tp")))
    return jax.shard_map(local, mesh=mesh, in_specs=in_specs, out_specs=out_specs, check_vma=False)
```

```python
import functools
import math

import jax
import jax.numpy as jnp
from jax import lax
from jax.experimental import pallas as pl
from jax.experimental.pallas import tpu as pltpu
from jax.sharding import PartitionSpec as P

H = 64
KVH = 8
HD = 128
STEPS = 4
ROWS = 8
GROUPS = 16
BLOCKS = 16
SEG_HALF = 512
PREFIX = 1024
CACHE_BLOCK = 128

FACTOR = 1.0 / math.sqrt(HD)
LOG2E = 1.4426950408889634
NEG_FILL = -1e30
PART_ROWS = 160

f32 = jnp.float32
bf16 = jnp.bfloat16


def params(mib):
    return pltpu.CompilerParams(vmem_limit_bytes=mib * 1024 * 1024)


def in_vmem(shape, dtype):
    return pltpu.VMEM(shape, dtype)


def in_hbm(x):
    return pltpu.with_memory_space_constraint(x, pltpu.HBM)


def whole(shape):
    return pl.BlockSpec(shape, lambda *_: (0,) * len(shape))


def dot_t(a, b):
    return lax.dot_general(a, b, (((1,), (1,)), ((), ())), preferred_element_type=f32)


def dot(a, b):
    return jnp.dot(a, b, preferred_element_type=f32)


ASKED = 0
HOLDER = 1
START = 2


def prep_kernel(match_hbm, start_hbm, q_hbm, kv_hbm, out_ref, ctrl_ref, match, starts, q_ref, kv_ref, sems):
    side = lax.axis_index("side")
    tp = lax.axis_index("tp")
    group = lax.axis_index("pair")
    q_col = pl.multiple_of((2 * tp + side) * 512, 512)
    kv_col = pl.multiple_of(tp * 256, 256)
    copies = [
        pltpu.make_async_copy(match_hbm, match, sems.at[0]),
        pltpu.make_async_copy(start_hbm, starts, sems.at[1]),
        pltpu.make_async_copy(q_hbm.at[0, :, :, pl.ds(q_col, 512)], q_ref, sems.at[2]),
        pltpu.make_async_copy(kv_hbm.at[0, :, :, pl.ds(kv_col, 256)], kv_ref, sems.at[3]),
    ]
    for copy in copies:
        copy.start()
    for copy in copies:
        copy.wait()
    q = q_ref[...].astype(f32)
    kv = kv_ref[...].astype(f32)
    rows = [q[t, 0:1, h * HD : (h + 1) * HD] for t in range(STEPS) for h in range(4)]
    rows += [kv[u, 0:1, :HD] for u in range(STEPS)]
    rows += [kv[u, 0:1, HD:] for u in range(STEPS)]
    sent = jnp.concatenate(rows, axis=0).astype(bf16)
    for p in range(GROUPS):
        out_ref[p] = sent

    holder = jnp.int32(0)
    for p in range(GROUPS):
        holder = jnp.where(match[p] == group, p, holder)
    numbers = [match[group], holder, starts[group]]
    sub = lax.broadcasted_iota(jnp.int32, ctrl_ref.shape, 0)
    ctrl = jnp.zeros(ctrl_ref.shape, f32)
    for k, number in enumerate(numbers):
        ctrl = jnp.where(sub == k, number.astype(f32), ctrl)
    ctrl_ref[...] = ctrl


def prep(matching, starts, decode_queries, decode_kv):
    shape = (GROUPS, 24, HD)
    hbm = pl.BlockSpec(memory_space=pltpu.HBM)
    return pl.pallas_call(
        prep_kernel,
        out_shape=(
            in_vmem(shape, bf16),
            in_vmem((ROWS, HD), f32),
        ),
        grid=(1,),
        in_specs=[hbm] * 4,
        out_specs=(whole(shape), whole((ROWS, HD))),
        scratch_shapes=[
            pltpu.SMEM((GROUPS,), jnp.int32),
            pltpu.SMEM((GROUPS,), jnp.int32),
            pltpu.VMEM((STEPS, ROWS, 512), bf16),
            pltpu.VMEM((STEPS, ROWS, 256), bf16),
            pltpu.SemaphoreType.DMA((4,)),
        ],
        compiler_params=params(4),
        cost_estimate=pl.CostEstimate(flops=10000, bytes_accessed=200000, transcendentals=0),
        name="prep",
    )(in_hbm(matching), in_hbm(starts), in_hbm(decode_queries), in_hbm(decode_kv))


def number_of(ctrl_ref, row):
    return jnp.max(ctrl_ref[row : row + 1, :]).astype(jnp.int32)


def decode_kernel(len_ref, q_ref, cache_ref, prior_ref, after_ref, out_ref):
    block = lax.axis_index("side") * 8 + lax.axis_index("tp")
    sub = lax.broadcasted_iota(jnp.int32, (ROWS, HD), 0)
    lane = lax.broadcasted_iota(jnp.int32, (ROWS, HD), 1)
    lens = jnp.zeros((ROWS, HD), jnp.int32)
    for k in range(ROWS - 1):
        lens = jnp.where(sub == k + 1, len_ref[0:1, k : k + 1], lens)
    allowed = (block * CACHE_BLOCK + lane < lens)[None]
    tiles = STEPS * 8
    small = lane % 32
    row_of = lax.broadcasted_iota(jnp.int32, (tiles * ROWS, HD), 0) % ROWS
    keep = [jnp.where(row_of == k + 1, 1.0, 0.0).astype(bf16) for k in range(ROWS - 1)]

    def spread(x):
        return jnp.concatenate([x * k for k in keep], axis=1)

    scores = []
    for head in range(2):
        q = jnp.concatenate(
            [
                q_ref[0, t, :, (head * 8 + g) * HD : (head * 8 + g + 1) * HD].astype(f32)
                for t in range(STEPS)
                for g in range(8)
            ],
            axis=0,
        ).astype(bf16)
        keys = jnp.concatenate(
            [cache_ref[0, k, :, head * 256 : head * 256 + HD] for k in range(ROWS - 1)], axis=1
        )
        scores.append(dot_t(spread(q), keys).reshape(tiles, ROWS, HD))
    for head in range(2):
        s = jnp.where(allowed, scores[head] * FACTOR, NEG_FILL)
        peak = jnp.max(s, axis=-1, keepdims=True)
        weights = jnp.where(allowed, jnp.exp(s - peak), 0.0)
        values = cache_ref[0, :, :, head * 256 + HD : head * 256 + 256].reshape(-1, HD)
        values = jnp.concatenate([values, jnp.ones_like(values)], axis=1)
        both = dot(spread(weights.reshape(tiles * ROWS, HD).astype(bf16)), values)
        both = both.reshape(STEPS, 8, ROWS, 2 * HD)
        peak = peak.reshape(STEPS, 8, ROWS, 1)
        for half in range(2):
            stats = jnp.zeros((ROWS, HD), f32)
            for t in range(STEPS):
                for h in range(4):
                    j = t * 4 + h
                    stats = jnp.where(small == j, peak[t, half * 4 + h], stats)
                    stats = jnp.where(small == 16 + j, both[t, half * 4 + h, :, HD:], stats)
            high = stats.astype(bf16).astype(f32)
            rest = stats - high
            mid = rest.astype(bf16).astype(f32)
            low = rest - mid
            packed = jnp.where(lane < 32, high, jnp.where(lane < 64, mid, low))
            slot = head * 2 + half
            mix = both[:, half * 4 : half * 4 + 4, :, :HD].reshape(128, HD)
            out_ref[slot, 0:128] = mix.astype(bf16)
            out_ref[slot, 128:144] = jnp.concatenate(
                [packed, jnp.zeros((ROWS, HD), f32)], axis=0
            ).astype(bf16)


def decode_parts(share, cache_lengths, decode_queries, kv_cache, prior, after):
    return pl.pallas_call(
        decode_kernel,
        out_shape=in_vmem((BLOCKS, PART_ROWS, HD), bf16),
        grid=(2,),
        in_specs=[
            whole(cache_lengths.shape),
            pl.BlockSpec((1, STEPS, ROWS, 2048), lambda c: (0, 0, 0, 2 * share + c)),
            pl.BlockSpec((1, ROWS - 1, CACHE_BLOCK, 512), lambda c: (0, 0, 0, 2 * share + c)),
            pl.BlockSpec(memory_space=pl.ANY),
            pl.BlockSpec(memory_space=pl.ANY),
        ],
        out_specs=pl.BlockSpec((4, PART_ROWS, HD), lambda c: (2 * share + c, 0, 0)),
        input_output_aliases={3: 0} if share else {},
        compiler_params=params(16),
        cost_estimate=pl.CostEstimate(
            flops=1000000000, bytes_accessed=2400000, transcendentals=150000
        ),
        name="decode_parts",
    )(in_hbm(cache_lengths), in_hbm(decode_queries), in_hbm(kv_cache), prior, after)


def hand_over_kernel(ctrl_ref, got_ref, parts_in, parts_ref, sem):
    slot = 2 * lax.axis_index("tp") + lax.axis_index("side")
    holder = number_of(ctrl_ref, HOLDER)
    copy = pltpu.make_async_copy(got_ref.at[holder], parts_ref.at[slot, 144:160], sem)
    copy.start()
    copy.wait()


def hand_over(ctrl, got, parts):
    return pl.pallas_call(
        hand_over_kernel,
        out_shape=in_vmem(parts.shape, bf16),
        grid=(1,),
        in_specs=[whole(ctrl.shape), whole(got.shape), pl.BlockSpec(memory_space=pl.ANY)],
        out_specs=pl.BlockSpec(memory_space=pl.ANY),
        scratch_shapes=[pltpu.SemaphoreType.DMA],
        input_output_aliases={2: 0},
        compiler_params=params(4),
        cost_estimate=pl.CostEstimate(flops=0, bytes_accessed=8192, transcendentals=0),
        name="hand_over",
    )(ctrl, got, parts)


def setup_kernel(ctrl_ref, prefix_ref, own_ref, other_ref, after_ref, mixed, longest_ref):
    pos = lax.broadcasted_iota(jnp.int32, (PREFIX, HD), 0).astype(f32)
    kept = jnp.where(pos < ctrl_ref[START : START + 1, :], 1.0, 0.0)
    mixed[SEG_HALF : SEG_HALF + PREFIX, :HD] = (prefix_ref[0, :, HD:].astype(f32) * kept).astype(bf16)
    mixed[SEG_HALF : SEG_HALF + PREFIX, HD:] = kept.astype(bf16)
    ones = jnp.ones((SEG_HALF, HD), bf16)
    mixed[:SEG_HALF] = jnp.concatenate([other_ref[0, :, HD:], ones], axis=1)
    mixed[SEG_HALF + PREFIX :] = jnp.concatenate([own_ref[0, :, HD:], ones], axis=1)

    def norm(ref):
        k = ref[0, :, :HD].astype(f32)
        return jnp.max(jnp.sum(k * k, axis=-1, keepdims=True), axis=0, keepdims=True)

    longest = jnp.maximum(norm(prefix_ref), jnp.maximum(norm(own_ref), norm(other_ref)))
    longest_ref[...] = jnp.broadcast_to(longest, longest_ref.shape)


def setup(ctrl, prefix, own, other, after):
    shapes = ((2 * SEG_HALF + PREFIX, 2 * HD), (ROWS, HD))
    return pl.pallas_call(
        setup_kernel,
        out_shape=(
            in_vmem(shapes[0], bf16),
            in_vmem(shapes[1], f32),
        ),
        grid=(1,),
        in_specs=[
            whole(ctrl.shape),
            whole(prefix.shape),
            whole(own.shape),
            whole(other.shape),
            pl.BlockSpec(memory_space=pl.ANY),
        ],
        out_specs=(whole(shapes[0]), whole(shapes[1])),
        compiler_params=params(12),
        cost_estimate=pl.CostEstimate(flops=2000000, bytes_accessed=2000000, transcendentals=0),
        name="setup",
    )(ctrl, prefix, own, other, after)


def prompt_kernel(
    ctrl_ref,
    q_ref,
    prefix_ref,
    own_ref,
    other_ref,
    mixed,
    longest_ref,
    after_ref,
    out_hbm,
    least,
    done,
    sems,
):
    side = lax.axis_index("side")
    tokens = 256
    scale = FACTOR * LOG2E
    longest = longest_ref[0:1, 0:1]
    causal = lax.broadcasted_iota(jnp.int32, (tokens, tokens), 1) <= lax.broadcasted_iota(
        jnp.int32, (tokens, tokens), 0
    )

    def key_parts(half, later):
        parts = []
        if later:
            parts += [(other_ref, n) for n in range(0, SEG_HALF, 256)]
        parts += [(prefix_ref, n) for n in range(0, PREFIX, 256)]
        parts += [(own_ref, n) for n in range(0, (half + 1) * tokens, 256)]
        return parts

    def mix(weights, half, later):
        first = 0 if later else SEG_HALF
        last = SEG_HALF + PREFIX + (half + 1) * tokens
        return dot(jnp.concatenate(weights, axis=1), mixed[first:last])

    def lanes(start, size):
        return pl.ds(start if isinstance(start, int) else pl.multiple_of(start, size), size)

    def queries(half, head):
        cols = lanes(head * HD, HD)
        return q_ref[0, half * tokens : (half + 1) * tokens, cols]

    def block(half, head, later):
        q = queries(half, head)
        wide_q = q.astype(f32)
        norms = jnp.sum(wide_q * wide_q, axis=-1, keepdims=True)
        bound = jnp.sqrt(norms * longest) * scale
        parts = key_parts(half, later)
        weights = []
        for number, (ref, n) in enumerate(parts):
            w = jnp.exp2(dot_t(q, ref[0, n : n + 256, :HD]) * scale - bound)
            if number == len(parts) - 1:
                w = jnp.where(causal, w, 0.0)
            weights.append(w.astype(bf16))
        total = mix(weights, half, later)
        sums = total[:, HD:]
        least[...] = jnp.minimum(least[...], sums)
        return (total[:, :HD] / sums).astype(bf16)

    def block_exact(half, head, later):
        q = queries(half, head)
        parts = key_parts(half, later)
        scores = []
        for number, (ref, n) in enumerate(parts):
            s = dot_t(q, ref[0, n : n + 256, :HD])
            if ref is prefix_ref:
                at = n + lax.broadcasted_iota(jnp.int32, s.shape, 1)
                s = jnp.where(at.astype(f32) < ctrl_ref[START : START + 1, 0:1], s, NEG_FILL)
            if number == len(parts) - 1:
                s = jnp.where(causal, s, NEG_FILL)
            scores.append(s)
        peak = functools.reduce(
            jnp.maximum, [jnp.max(s, axis=-1, keepdims=True) for s in scores]
        )
        weights = [jnp.exp2((s - peak) * scale).astype(bf16) for s in scores]
        total = mix(weights, half, later)
        return (total[:, :HD] / total[:, HD:]).astype(bf16)

    def result_copy(pair, slot):
        cols = lanes(pair * 2 * HD, 2 * HD)
        return pltpu.make_async_copy(done.at[slot], out_hbm.at[0, :, cols], sems.at[slot])

    def two_heads(one, pair, slot, later):
        for half in range(2):
            for head in range(2):
                done[slot, half * tokens : (half + 1) * tokens, head * HD : (head + 1) * HD] = one(
                    half, pair * 2 + head, later
                )
        result_copy(pair, slot).start()

    least[...] = jnp.ones(least.shape, f32)
    for later in (False, True):

        @pl.when(side == int(later))
        def _(later=later):
            for pair in range(4):
                two_heads(block, pair, pair, later)
            loose = jnp.min(least[...]) < 1e-27
            for pair in range(4):
                result_copy(pair, pair).wait()

            @pl.when(loose)
            def _():
                @pl.loop(0, 4)
                def _(pair):
                    two_heads(block_exact, pair, 0, later)
                    result_copy(pair, 0).wait()


def prompt(ctrl, queries, prefix, own, other, mixed, longest, after):
    return pl.pallas_call(
        prompt_kernel,
        out_shape=jax.ShapeDtypeStruct(queries.shape, bf16),
        grid=(1,),
        in_specs=[
            whole(ctrl.shape),
            whole(queries.shape),
            whole(prefix.shape),
            whole(own.shape),
            whole(other.shape),
            whole(mixed.shape),
            whole(longest.shape),
            pl.BlockSpec(memory_space=pl.ANY),
        ],
        out_specs=pl.BlockSpec(memory_space=pltpu.HBM),
        scratch_shapes=[
            pltpu.VMEM((256, HD), f32),
            pltpu.VMEM((4, 512, 2 * HD), bf16),
            pltpu.SemaphoreType.DMA((4,)),
        ],
        compiler_params=params(32),
        cost_estimate=pl.CostEstimate(
            flops=4096 * 1920 * 128 * 8, bytes_accessed=3000000, transcendentals=4096 * 1920
        ),
        name="prompt",
    )(ctrl, queries, prefix, own, other, mixed, longest, after)


def first_row_kernel(ctrl_ref, got_ref, prefix_ref, own_ref, other_ref, after_ref, out_ref):
    asked = got_ref[number_of(ctrl_ref, ASKED)].astype(f32)
    q = asked[0:16].astype(bf16)
    fresh = asked[16:24]
    pad = jnp.zeros((12, HD), f32)
    fresh_k = jnp.concatenate([fresh[:4], pad], axis=0).astype(bf16)
    fresh_v = jnp.concatenate([fresh[4:], pad], axis=0).astype(bf16)
    s0 = dot_t(q, prefix_ref[0, :, :HD])
    pos = lax.broadcasted_iota(jnp.int32, s0.shape, 1)
    s0 = jnp.where(pos.astype(f32) < ctrl_ref[START : START + 1, 0:1], s0, NEG_FILL)
    s1 = dot_t(q, own_ref[0, :, :HD])
    s2 = dot_t(q, other_ref[0, :, :HD])
    s3 = dot_t(q, fresh_k)
    step = lax.broadcasted_iota(jnp.int32, s3.shape, 0) // 4
    pos = lax.broadcasted_iota(jnp.int32, s3.shape, 1)
    s3 = jnp.where(pos <= step, s3, NEG_FILL)
    scores = (s0, s1, s2, s3)
    values = (prefix_ref[0, :, HD:], own_ref[0, :, HD:], other_ref[0, :, HD:], fresh_v)
    peak = functools.reduce(jnp.maximum, [jnp.max(s, axis=-1, keepdims=True) for s in scores])
    mix = jnp.zeros((16, HD), f32)
    totals = jnp.zeros((16, 1), f32)
    for s, v in zip(scores, values):
        w = jnp.exp2((s - peak) * (FACTOR * LOG2E))
        totals += jnp.sum(w, axis=-1, keepdims=True)
        mix += dot(w.astype(bf16), v)
    out = (mix / totals).astype(bf16)
    for p in range(GROUPS):
        out_ref[p] = out


def first_row(ctrl, got, prefix, own, other, after):
    shape = (GROUPS, 16, HD)
    return pl.pallas_call(
        first_row_kernel,
        out_shape=in_vmem(shape, bf16),
        grid=(1,),
        in_specs=[
            whole(ctrl.shape),
            whole(got.shape),
            whole(prefix.shape),
            whole(own.shape),
            whole(other.shape),
            pl.BlockSpec(memory_space=pl.ANY),
        ],
        out_specs=whole(shape),
        compiler_params=params(8),
        cost_estimate=pl.CostEstimate(
            flops=20000000, bytes_accessed=1300000, transcendentals=33000
        ),
        name="first_row",
    )(ctrl, got, prefix, own, other, after)


def merge_kernel(parts_ref, q_ref, kv_ref, out_ref):
    block = lax.axis_index("side") * 8 + lax.axis_index("tp")
    q = q_ref[0, :, :, pl.ds(pl.multiple_of(block * 512, 512), 512)].astype(f32)
    kv = kv_ref[0, :, :, pl.ds(pl.multiple_of((block // 2) * 256, 256), 256)].astype(f32)
    sub = lax.broadcasted_iota(jnp.int32, (ROWS, HD), 0)
    lane = lax.broadcasted_iota(jnp.int32, (ROWS, HD), 1)

    peaks, totals = [], []
    for b in range(BLOCKS):
        x = parts_ref[b, 128:144].astype(f32)[:ROWS]
        x = x + pltpu.roll(x, HD - 32, 1) + pltpu.roll(x, HD - 64, 1)
        peaks.append(x)
        totals.append(pltpu.roll(x, HD - 16, 1))
    top = functools.reduce(jnp.maximum, peaks)
    fresh = {}
    fresh_top = jnp.full((ROWS, HD), NEG_FILL, f32)
    for t in range(STEPS):
        for h in range(4):
            j = t * 4 + h
            qt = q[t, :, h * HD : (h + 1) * HD]
            for u in range(t + 1):
                s = jnp.sum(qt * kv[u, :, :HD], axis=-1, keepdims=True) * FACTOR
                fresh[j, u] = s
                fresh_top = jnp.where(lane == j, jnp.maximum(fresh_top, s), fresh_top)
    top = jnp.maximum(top, fresh_top)
    scales = [jnp.exp(p - top) for p in peaks]
    total = functools.reduce(jnp.add, [s * t for s, t in zip(scales, totals)])
    first = parts_ref[(block % 2) * 8 + block // 2, 144:160].astype(f32)
    for t in range(STEPS):
        for h in range(4):
            j = t * 4 + h
            acc = jnp.zeros((ROWS, HD), f32)
            for b in range(0, BLOCKS):
                tile = parts_ref[b, (j // 2) * 16 : (j // 2) * 16 + 16].astype(f32)
                acc += scales[b][:, j : j + 1] * tile[(j % 2) * 8 : (j % 2) * 8 + 8]
            denom = total[:, j : j + 1]
            for u in range(t + 1):
                w = jnp.exp(fresh[j, u] - top[:, j : j + 1])
                acc += w * kv[u, :, HD:]
                denom = denom + w
            out = acc / denom
            out = jnp.where(sub == 0, first[j : j + 1], out)
            out_ref[0, t, :, h * HD : (h + 1) * HD] = out.astype(bf16)


def merge(parts, decode_queries, decode_kv):
    shape = (1, STEPS, ROWS, 512)
    return pl.pallas_call(
        merge_kernel,
        out_shape=jax.ShapeDtypeStruct(shape, bf16),
        grid=(1,),
        in_specs=[whole(parts.shape), whole(decode_queries.shape), whole(decode_kv.shape)],
        out_specs=whole(shape),
        compiler_params=params(8),
        cost_estimate=pl.CostEstimate(flops=3000000, bytes_accessed=1300000, transcendentals=60000),
        name="merge",
    )(parts, decode_queries, decode_kv)


def exchange(x, axis):
    return lax.all_to_all(x, axis, split_axis=0, concat_axis=0, tiled=True)


def local(
    segment_queries,
    segment_kv,
    prefix_kv,
    kv_cache,
    decode_queries,
    decode_kv,
    matching,
    segment_starts,
    cache_lengths,
):
    other_kv = lax.ppermute(segment_kv, "side", [(0, 1), (1, 0)])
    sent, ctrl = prep(matching, segment_starts, decode_queries, decode_kv)
    sent, prefix, own, queries = lax.optimization_barrier(
        (sent, prefix_kv, segment_kv, segment_queries)
    )
    keys = (prefix, own, other_kv)
    cache = (cache_lengths, decode_queries, kv_cache)
    parts = decode_parts(0, *cache, sent, sent)
    mixed, longest = setup(ctrl, *keys, parts)
    first = first_row(ctrl, exchange(sent, "pair"), *keys, longest)
    parts = decode_parts(1, *cache, parts, first)
    parts = hand_over(ctrl, exchange(first, "pair"), parts)
    out = prompt(ctrl, queries, *keys, mixed, longest, parts)
    parts = exchange(parts, ("side", "tp"))
    decode_out = merge(parts, decode_queries, decode_kv)
    return (out, decode_out)


def solution(mesh):
    in_specs = (
        P("pair", "side", "tp"),
        P("pair", "side", "tp"),
        P("pair", None, "tp"),
        P("pair", None, ("side", "tp"), None),
        P("pair", None, None, None),
        P("pair", None, None, None),
        P(),
        P(),
        P("pair", None),
    )
    out_specs = (P("pair", "side", "tp"), P("pair", None, None, ("side", "tp")))
    return jax.shard_map(local, mesh=mesh, in_specs=in_specs, out_specs=out_specs, check_vma=False)
```

```python
import functools
import math

import jax
import jax.numpy as jnp
from jax import lax
from jax.experimental import pallas as pl
from jax.experimental.pallas import tpu as pltpu
from jax.sharding import PartitionSpec as P

H = 64
KVH = 8
HD = 128
STEPS = 4
ROWS = 8
GROUPS = 16
BLOCKS = 16
PIECES = [(pair, half) for pair in range(4) for half in range(2)]
EARLY = 3
SEG_HALF = 512
PREFIX = 1024
CACHE_BLOCK = 128

FACTOR = 1.0 / math.sqrt(HD)
LOG2E = 1.4426950408889634
NEG_FILL = -1e30
PART_ROWS = 160

f32 = jnp.float32
bf16 = jnp.bfloat16


def params(mib):
    return pltpu.CompilerParams(vmem_limit_bytes=mib * 1024 * 1024)


def in_hbm(x):
    return pltpu.with_memory_space_constraint(x, pltpu.HBM)


def whole(shape):
    return pl.BlockSpec(shape, lambda *_: (0,) * len(shape))


def dot_t(a, b):
    return lax.dot_general(a, b, (((1,), (1,)), ((), ())), preferred_element_type=f32)


def dot(a, b):
    return jnp.dot(a, b, preferred_element_type=f32)


ASKED = 0
HOLDER = 1
START = 2


def prep_kernel(match_hbm, start_hbm, q_hbm, kv_hbm, out_ref, ctrl_ref, match, starts, q_ref, kv_ref, sems):
    side = lax.axis_index("side")
    tp = lax.axis_index("tp")
    group = lax.axis_index("pair")
    q_col = pl.multiple_of((2 * tp + side) * 512, 512)
    kv_col = pl.multiple_of(tp * 256, 256)
    copies = [
        pltpu.make_async_copy(match_hbm, match, sems.at[0]),
        pltpu.make_async_copy(start_hbm, starts, sems.at[1]),
        pltpu.make_async_copy(q_hbm.at[0, :, :, pl.ds(q_col, 512)], q_ref, sems.at[2]),
        pltpu.make_async_copy(kv_hbm.at[0, :, :, pl.ds(kv_col, 256)], kv_ref, sems.at[3]),
    ]
    for copy in copies:
        copy.start()
    for copy in copies:
        copy.wait()
    q = q_ref[...].astype(f32)
    kv = kv_ref[...].astype(f32)
    rows = [q[t, 0:1, h * HD : (h + 1) * HD] for t in range(STEPS) for h in range(4)]
    rows += [kv[u, 0:1, :HD] for u in range(STEPS)]
    rows += [kv[u, 0:1, HD:] for u in range(STEPS)]
    sent = jnp.concatenate(rows, axis=0).astype(bf16)
    for p in range(GROUPS):
        out_ref[p] = sent

    holder = jnp.int32(0)
    for p in range(GROUPS):
        holder = jnp.where(match[p] == group, p, holder)
    numbers = [match[group], holder, starts[group]]
    sub = lax.broadcasted_iota(jnp.int32, ctrl_ref.shape, 0)
    ctrl = jnp.zeros(ctrl_ref.shape, f32)
    for k, number in enumerate(numbers):
        ctrl = jnp.where(sub == k, number.astype(f32), ctrl)
    ctrl_ref[...] = ctrl


def prep(matching, starts, decode_queries, decode_kv):
    shape = (GROUPS, 24, HD)
    hbm = pl.BlockSpec(memory_space=pltpu.HBM)
    return pl.pallas_call(
        prep_kernel,
        out_shape=(
            jax.ShapeDtypeStruct(shape, bf16),
            jax.ShapeDtypeStruct((ROWS, HD), f32),
        ),
        grid=(1,),
        in_specs=[hbm] * 4,
        out_specs=(whole(shape), whole((ROWS, HD))),
        scratch_shapes=[
            pltpu.SMEM((GROUPS,), jnp.int32),
            pltpu.SMEM((GROUPS,), jnp.int32),
            pltpu.VMEM((STEPS, ROWS, 512), bf16),
            pltpu.VMEM((STEPS, ROWS, 256), bf16),
            pltpu.SemaphoreType.DMA((4,)),
        ],
        compiler_params=params(4),
        cost_estimate=pl.CostEstimate(flops=10000, bytes_accessed=200000, transcendentals=0),
        name="prep",
    )(in_hbm(matching), in_hbm(starts), in_hbm(decode_queries), in_hbm(decode_kv))


def number_of(ctrl_ref, row):
    return jnp.max(ctrl_ref[row : row + 1, :]).astype(jnp.int32)


def decode_kernel(len_ref, q_ref, cache_ref, prior_ref, after_ref, out_ref):
    block = lax.axis_index("side") * 8 + lax.axis_index("tp")
    sub = lax.broadcasted_iota(jnp.int32, (ROWS, HD), 0)
    lane = lax.broadcasted_iota(jnp.int32, (ROWS, HD), 1)
    lens = jnp.zeros((ROWS, HD), jnp.int32)
    for k in range(ROWS - 1):
        lens = jnp.where(sub == k + 1, len_ref[0:1, k : k + 1], lens)
    allowed = (block * CACHE_BLOCK + lane < lens)[None]
    tiles = STEPS * 8
    small = lane % 32
    row_of = lax.broadcasted_iota(jnp.int32, (tiles * ROWS, HD), 0) % ROWS
    keep = [jnp.where(row_of == k + 1, 1.0, 0.0).astype(bf16) for k in range(ROWS - 1)]

    def spread(x):
        return jnp.concatenate([x * k for k in keep], axis=1)

    scores = []
    for head in range(2):
        q = jnp.concatenate(
            [
                q_ref[0, t, :, (head * 8 + g) * HD : (head * 8 + g + 1) * HD].astype(f32)
                for t in range(STEPS)
                for g in range(8)
            ],
            axis=0,
        ).astype(bf16)
        keys = jnp.concatenate(
            [cache_ref[0, k, :, head * 256 : head * 256 + HD] for k in range(ROWS - 1)], axis=1
        )
        scores.append(dot_t(spread(q), keys).reshape(tiles, ROWS, HD))
    for head in range(2):
        s = jnp.where(allowed, scores[head] * FACTOR, NEG_FILL)
        peak = jnp.max(s, axis=-1, keepdims=True)
        weights = jnp.where(allowed, jnp.exp(s - peak), 0.0)
        values = cache_ref[0, :, :, head * 256 + HD : head * 256 + 256].reshape(-1, HD)
        values = jnp.concatenate([values, jnp.ones_like(values)], axis=1)
        both = dot(spread(weights.reshape(tiles * ROWS, HD).astype(bf16)), values)
        both = both.reshape(STEPS, 8, ROWS, 2 * HD)
        peak = peak.reshape(STEPS, 8, ROWS, 1)
        for half in range(2):
            stats = jnp.zeros((ROWS, HD), f32)
            for t in range(STEPS):
                for h in range(4):
                    j = t * 4 + h
                    stats = jnp.where(small == j, peak[t, half * 4 + h], stats)
                    stats = jnp.where(small == 16 + j, both[t, half * 4 + h, :, HD:], stats)
            high = stats.astype(bf16).astype(f32)
            rest = stats - high
            mid = rest.astype(bf16).astype(f32)
            low = rest - mid
            packed = jnp.where(lane < 32, high, jnp.where(lane < 64, mid, low))
            slot = head * 2 + half
            mix = both[:, half * 4 : half * 4 + 4, :, :HD].reshape(128, HD)
            out_ref[slot, 0, 0:128] = mix.astype(bf16)
            out_ref[slot, 0, 128:144] = jnp.concatenate(
                [packed, jnp.zeros((ROWS, HD), f32)], axis=0
            ).astype(bf16)


def decode_parts(share, cache_lengths, decode_queries, kv_cache, prior, after):
    return pl.pallas_call(
        decode_kernel,
        out_shape=jax.ShapeDtypeStruct((8, 2, PART_ROWS, HD), bf16),
        grid=(2,),
        in_specs=[
            whole(cache_lengths.shape),
            pl.BlockSpec((1, STEPS, ROWS, 2048), lambda c: (0, 0, 0, 2 * share + c)),
            pl.BlockSpec((1, ROWS - 1, CACHE_BLOCK, 512), lambda c: (0, 0, 0, 2 * share + c)),
            pl.BlockSpec(memory_space=pl.ANY),
            pl.BlockSpec(memory_space=pl.ANY),
        ],
        out_specs=pl.BlockSpec((4, 1, PART_ROWS, HD), lambda c: (c, share, 0, 0)),
        input_output_aliases={3: 0} if share else {},
        compiler_params=params(16),
        cost_estimate=pl.CostEstimate(
            flops=1000000000, bytes_accessed=2400000, transcendentals=150000
        ),
        name="decode_parts",
    )(in_hbm(cache_lengths), in_hbm(decode_queries), in_hbm(kv_cache), prior, after)


def hand_over_kernel(ctrl_ref, got_ref, parts_in, after_ref, parts_ref, sem):
    owner = 2 * lax.axis_index("tp") + lax.axis_index("side")
    slot = (owner % 8) * 2 + owner // 8
    holder = number_of(ctrl_ref, HOLDER)
    copy = pltpu.make_async_copy(got_ref.at[holder], parts_ref.at[slot, 144:160], sem)
    copy.start()
    copy.wait()


def hand_over(ctrl, got, parts, after):
    return pl.pallas_call(
        hand_over_kernel,
        out_shape=jax.ShapeDtypeStruct(parts.shape, bf16),
        grid=(1,),
        in_specs=[whole(ctrl.shape), whole(got.shape)] + [pl.BlockSpec(memory_space=pl.ANY)] * 2,
        out_specs=pl.BlockSpec(memory_space=pl.ANY),
        scratch_shapes=[pltpu.SemaphoreType.DMA],
        input_output_aliases={2: 0},
        compiler_params=params(4),
        cost_estimate=pl.CostEstimate(flops=0, bytes_accessed=8192, transcendentals=0),
        name="hand_over",
    )(ctrl, got, parts, in_hbm(after))


def norms_kernel(prefix_ref, own_ref, other_ref, after_ref, longest_ref):
    def norm(ref):
        k = ref[0, :, :HD].astype(f32)
        return jnp.max(jnp.sum(k * k, axis=-1, keepdims=True), axis=0, keepdims=True)

    longest = jnp.maximum(norm(prefix_ref), jnp.maximum(norm(own_ref), norm(other_ref)))
    longest_ref[...] = jnp.broadcast_to(longest, longest_ref.shape)


def norms(prefix, own, other, after):
    return pl.pallas_call(
        norms_kernel,
        out_shape=jax.ShapeDtypeStruct((ROWS, HD), f32),
        grid=(1,),
        in_specs=[
            whole(prefix.shape),
            whole(own.shape),
            whole(other.shape),
            pl.BlockSpec(memory_space=pl.ANY),
        ],
        out_specs=whole((ROWS, HD)),
        compiler_params=params(8),
        cost_estimate=pl.CostEstimate(flops=2000000, bytes_accessed=1000000, transcendentals=0),
        name="norms",
    )(prefix, own, other, after)


def prompt_kernel(
    pieces, ctrl_ref, q_ref, prefix_ref, own_ref, other_ref, longest_ref, after_ref, prior, out_hbm, mixed, least, done, sems
):
    side = lax.axis_index("side")
    tokens = 256
    scale = FACTOR * LOG2E
    longest = longest_ref[0:1, 0:1]
    pos = lax.broadcasted_iota(jnp.int32, (PREFIX, HD), 0).astype(f32)
    kept = jnp.where(pos < ctrl_ref[START : START + 1, :], 1.0, 0.0)
    mixed[SEG_HALF : SEG_HALF + PREFIX, :HD] = (prefix_ref[0, :, HD:].astype(f32) * kept).astype(bf16)
    mixed[SEG_HALF : SEG_HALF + PREFIX, HD:] = kept.astype(bf16)
    ones = jnp.ones((SEG_HALF, HD), bf16)
    mixed[:SEG_HALF] = jnp.concatenate([other_ref[0, :, HD:], ones], axis=1)
    mixed[SEG_HALF + PREFIX :] = jnp.concatenate([own_ref[0, :, HD:], ones], axis=1)
    causal = lax.broadcasted_iota(jnp.int32, (tokens, tokens), 1) <= lax.broadcasted_iota(
        jnp.int32, (tokens, tokens), 0
    )

    def key_parts(half, later):
        parts = []
        if later:
            parts += [(other_ref, n) for n in range(0, SEG_HALF, 256)]
        parts += [(prefix_ref, n) for n in range(0, PREFIX, 256)]
        parts += [(own_ref, n) for n in range(0, (half + 1) * tokens, 256)]
        return parts

    def mix(weights, half, later):
        first = 0 if later else SEG_HALF
        last = SEG_HALF + PREFIX + (half + 1) * tokens
        return dot(jnp.concatenate(weights, axis=1), mixed[first:last])

    def lanes(start, size):
        return pl.ds(start if isinstance(start, int) else pl.multiple_of(start, size), size)

    def queries(half, head):
        cols = lanes(head * HD, HD)
        return q_ref[0, half * tokens : (half + 1) * tokens, cols]

    def block(half, head, later):
        q = queries(half, head)
        wide_q = q.astype(f32)
        norms = jnp.sum(wide_q * wide_q, axis=-1, keepdims=True)
        bound = jnp.sqrt(norms * longest) * scale
        parts = key_parts(half, later)
        weights = []
        for number, (ref, n) in enumerate(parts):
            w = jnp.exp2(dot_t(q, ref[0, n : n + 256, :HD]) * scale - bound)
            if number == len(parts) - 1:
                w = jnp.where(causal, w, 0.0)
            weights.append(w.astype(bf16))
        total = mix(weights, half, later)
        sums = total[:, HD:]
        least[...] = jnp.minimum(least[...], sums)
        return (total[:, :HD] / sums).astype(bf16)

    def block_exact(half, head, later):
        q = queries(half, head)
        parts = key_parts(half, later)
        scores = []
        for number, (ref, n) in enumerate(parts):
            s = dot_t(q, ref[0, n : n + 256, :HD])
            if ref is prefix_ref:
                at = n + lax.broadcasted_iota(jnp.int32, s.shape, 1)
                s = jnp.where(at.astype(f32) < ctrl_ref[START : START + 1, 0:1], s, NEG_FILL)
            if number == len(parts) - 1:
                s = jnp.where(causal, s, NEG_FILL)
            scores.append(s)
        peak = functools.reduce(
            jnp.maximum, [jnp.max(s, axis=-1, keepdims=True) for s in scores]
        )
        weights = [jnp.exp2((s - peak) * scale).astype(bf16) for s in scores]
        total = mix(weights, half, later)
        return (total[:, :HD] / total[:, HD:]).astype(bf16)

    def result_copy(pair, half, slot):
        rows = pl.ds(half * tokens, tokens)
        cols = lanes(pair * 2 * HD, 2 * HD)
        return pltpu.make_async_copy(done.at[slot], out_hbm.at[0, rows, cols], sems.at[slot])

    def piece(one, pair, half, slot, later):
        for head in range(2):
            done[slot, :, head * HD : (head + 1) * HD] = one(half, pair * 2 + head, later)
        result_copy(pair, half, slot).start()

    least[...] = jnp.ones(least.shape, f32)
    for later in (False, True):

        @pl.when(side == int(later))
        def _(later=later):
            for slot, (pair, half) in enumerate(pieces):
                piece(block, pair, half, slot, later)
            loose = jnp.min(least[...]) < 1e-27
            for slot, (pair, half) in enumerate(pieces):
                result_copy(pair, half, slot).wait()

            @pl.when(loose)
            def _():
                for half in range(2):
                    pairs = [pair for pair, h in pieces if h == half]

                    @pl.loop(pairs[0], pairs[-1] + 1)
                    def _(pair):
                        piece(block_exact, pair, half, 0, later)
                        result_copy(pair, half, 0).wait()


def prompt(pieces, ctrl, queries, prefix, own, other, longest, after, prior):
    operands = [ctrl, queries, prefix, own, other, longest, after]
    units = sum(6 + half for _, half in pieces) * 2
    anywhere = pl.BlockSpec(memory_space=pl.ANY)
    return pl.pallas_call(
        functools.partial(prompt_kernel, pieces),
        out_shape=jax.ShapeDtypeStruct(queries.shape, bf16),
        grid=(1,),
        in_specs=[whole(x.shape) for x in operands[:-1]]
        + [anywhere, pl.BlockSpec(memory_space=pltpu.HBM) if prior is not None else anywhere],
        out_specs=pl.BlockSpec(memory_space=pltpu.HBM),
        scratch_shapes=[
            pltpu.VMEM((2 * SEG_HALF + PREFIX, 2 * HD), bf16),
            pltpu.VMEM((256, HD), f32),
            pltpu.VMEM((len(pieces), 256, 2 * HD), bf16),
            pltpu.SemaphoreType.DMA((len(pieces),)),
        ],
        input_output_aliases={7: 0} if prior is not None else {},
        compiler_params=params(24),
        cost_estimate=pl.CostEstimate(
            flops=units * 256 * 256 * 128 * 6, bytes_accessed=2000000, transcendentals=units * 65536
        ),
        name="prompt",
    )(*operands, after if prior is None else in_hbm(prior))


def first_row_kernel(ctrl_ref, got_ref, prefix_ref, own_ref, other_ref, after_ref, out_ref):
    asked = got_ref[number_of(ctrl_ref, ASKED)].astype(f32)
    q = asked[0:16].astype(bf16)
    fresh = asked[16:24]
    pad = jnp.zeros((12, HD), f32)
    fresh_k = jnp.concatenate([fresh[:4], pad], axis=0).astype(bf16)
    fresh_v = jnp.concatenate([fresh[4:], pad], axis=0).astype(bf16)
    s0 = dot_t(q, prefix_ref[0, :, :HD])
    pos = lax.broadcasted_iota(jnp.int32, s0.shape, 1)
    s0 = jnp.where(pos.astype(f32) < ctrl_ref[START : START + 1, 0:1], s0, NEG_FILL)
    s1 = dot_t(q, own_ref[0, :, :HD])
    s2 = dot_t(q, other_ref[0, :, :HD])
    s3 = dot_t(q, fresh_k)
    step = lax.broadcasted_iota(jnp.int32, s3.shape, 0) // 4
    pos = lax.broadcasted_iota(jnp.int32, s3.shape, 1)
    s3 = jnp.where(pos <= step, s3, NEG_FILL)
    scores = (s0, s1, s2, s3)
    values = (prefix_ref[0, :, HD:], own_ref[0, :, HD:], other_ref[0, :, HD:], fresh_v)
    peak = functools.reduce(jnp.maximum, [jnp.max(s, axis=-1, keepdims=True) for s in scores])
    mix = jnp.zeros((16, HD), f32)
    totals = jnp.zeros((16, 1), f32)
    for s, v in zip(scores, values):
        w = jnp.exp2((s - peak) * (FACTOR * LOG2E))
        totals += jnp.sum(w, axis=-1, keepdims=True)
        mix += dot(w.astype(bf16), v)
    out = (mix / totals).astype(bf16)
    for p in range(GROUPS):
        out_ref[p] = out


def first_row(ctrl, got, prefix, own, other, after):
    shape = (GROUPS, 16, HD)
    return pl.pallas_call(
        first_row_kernel,
        out_shape=jax.ShapeDtypeStruct(shape, bf16),
        grid=(1,),
        in_specs=[
            whole(ctrl.shape),
            whole(got.shape),
            whole(prefix.shape),
            whole(own.shape),
            whole(other.shape),
            pl.BlockSpec(memory_space=pl.ANY),
        ],
        out_specs=whole(shape),
        compiler_params=params(8),
        cost_estimate=pl.CostEstimate(
            flops=20000000, bytes_accessed=1300000, transcendentals=33000
        ),
        name="first_row",
    )(ctrl, got, prefix, own, other, after)


def merge_kernel(parts_ref, q_ref, kv_ref, out_ref):
    block = lax.axis_index("side") * 8 + lax.axis_index("tp")
    q = q_ref[0, :, :, pl.ds(pl.multiple_of(block * 512, 512), 512)].astype(f32)
    kv = kv_ref[0, :, :, pl.ds(pl.multiple_of((block // 2) * 256, 256), 256)].astype(f32)
    sub = lax.broadcasted_iota(jnp.int32, (ROWS, HD), 0)
    lane = lax.broadcasted_iota(jnp.int32, (ROWS, HD), 1)

    peaks, totals = [], []
    for b in range(BLOCKS):
        x = parts_ref[b, 128:144].astype(f32)[:ROWS]
        x = x + pltpu.roll(x, HD - 32, 1) + pltpu.roll(x, HD - 64, 1)
        peaks.append(x)
        totals.append(pltpu.roll(x, HD - 16, 1))
    top = functools.reduce(jnp.maximum, peaks)
    fresh = {}
    fresh_top = jnp.full((ROWS, HD), NEG_FILL, f32)
    for t in range(STEPS):
        for h in range(4):
            j = t * 4 + h
            qt = q[t, :, h * HD : (h + 1) * HD]
            for u in range(t + 1):
                s = jnp.sum(qt * kv[u, :, :HD], axis=-1, keepdims=True) * FACTOR
                fresh[j, u] = s
                fresh_top = jnp.where(lane == j, jnp.maximum(fresh_top, s), fresh_top)
    top = jnp.maximum(top, fresh_top)
    scales = [jnp.exp(p - top) for p in peaks]
    total = functools.reduce(jnp.add, [s * t for s, t in zip(scales, totals)])
    first = parts_ref[block, 144:160].astype(f32)
    for t in range(STEPS):
        for h in range(4):
            j = t * 4 + h
            acc = jnp.zeros((ROWS, HD), f32)
            for b in range(0, BLOCKS):
                tile = parts_ref[b, (j // 2) * 16 : (j // 2) * 16 + 16].astype(f32)
                acc += scales[b][:, j : j + 1] * tile[(j % 2) * 8 : (j % 2) * 8 + 8]
            denom = total[:, j : j + 1]
            for u in range(t + 1):
                w = jnp.exp(fresh[j, u] - top[:, j : j + 1])
                acc += w * kv[u, :, HD:]
                denom = denom + w
            out = acc / denom
            out = jnp.where(sub == 0, first[j : j + 1], out)
            out_ref[0, t, :, h * HD : (h + 1) * HD] = out.astype(bf16)


def merge(parts, decode_queries, decode_kv):
    shape = (1, STEPS, ROWS, 512)
    return pl.pallas_call(
        merge_kernel,
        out_shape=jax.ShapeDtypeStruct(shape, bf16),
        grid=(1,),
        in_specs=[whole(parts.shape), whole(decode_queries.shape), whole(decode_kv.shape)],
        out_specs=whole(shape),
        compiler_params=params(8),
        cost_estimate=pl.CostEstimate(flops=3000000, bytes_accessed=1300000, transcendentals=60000),
        name="merge",
    )(parts, decode_queries, decode_kv)


def exchange(x, axis):
    return lax.all_to_all(x, axis, split_axis=0, concat_axis=0, tiled=True)


def local(
    segment_queries,
    segment_kv,
    prefix_kv,
    kv_cache,
    decode_queries,
    decode_kv,
    matching,
    segment_starts,
    cache_lengths,
):
    other_kv = lax.ppermute(segment_kv, "side", [(0, 1), (1, 0)])
    sent, ctrl = prep(matching, segment_starts, decode_queries, decode_kv)
    sent, prefix, own, queries = lax.optimization_barrier(
        (sent, prefix_kv, segment_kv, segment_queries)
    )
    keys = (prefix, own, other_kv)
    cache = (cache_lengths, decode_queries, kv_cache)
    parts = decode_parts(0, *cache, sent, sent)
    longest = norms(*keys, parts)
    first = first_row(ctrl, exchange(sent, "pair"), *keys, longest)
    parts = decode_parts(1, *cache, parts, first).reshape(BLOCKS, PART_ROWS, HD)
    tokens = (ctrl, queries, *keys, longest)
    out = prompt(PIECES[:EARLY], *tokens, parts, None)
    parts = hand_over(ctrl, exchange(first, "pair"), parts, out)
    out = prompt(PIECES[EARLY:], *tokens, parts, out)
    parts = exchange(parts, ("tp", "side"))
    decode_out = merge(parts, decode_queries, decode_kv)
    return (out, decode_out)


def solution(mesh):
    in_specs = (
        P("pair", "side", "tp"),
        P("pair", "side", "tp"),
        P("pair", None, "tp"),
        P("pair", None, ("side", "tp"), None),
        P("pair", None, None, None),
        P("pair", None, None, None),
        P(),
        P(),
        P("pair", None),
    )
    out_specs = (P("pair", "side", "tp"), P("pair", None, None, ("side", "tp")))
    return jax.shard_map(local, mesh=mesh, in_specs=in_specs, out_specs=out_specs, check_vma=False)
```

```python
import functools
import math

import jax
import jax.numpy as jnp
from jax import lax
from jax.experimental import pallas as pl
from jax.experimental.pallas import tpu as pltpu
from jax.sharding import PartitionSpec as P

H = 64
KVH = 8
HD = 128
STEPS = 4
ROWS = 8
GROUPS = 16
PIECES = [(pair, half) for pair in range(4) for half in range(2)]
SEG_HALF = 512
PREFIX = 1024
CACHE_BLOCK = 128

FACTOR = 1.0 / math.sqrt(HD)
LOG2E = 1.4426950408889634
NEG_FILL = -1e30
STAT_ROWS = 144
PART_ROWS = 160

f32 = jnp.float32
bf16 = jnp.bfloat16


def params(mib):
    return pltpu.CompilerParams(vmem_limit_bytes=mib * 1024 * 1024)


def in_hbm(x):
    return pltpu.with_memory_space_constraint(x, pltpu.HBM)


def whole(shape):
    return pl.BlockSpec(shape, lambda *_: (0,) * len(shape))


def dot_t(a, b):
    return lax.dot_general(a, b, (((1,), (1,)), ((), ())), preferred_element_type=f32)


def dot(a, b):
    return jnp.dot(a, b, preferred_element_type=f32)


ASKED = 0
HOLDER = 1
START = 2


def prep_kernel(match_hbm, start_hbm, q_hbm, kv_hbm, out_ref, ctrl_ref, match, starts, q_ref, kv_ref, sems):
    side = lax.axis_index("side")
    tp = lax.axis_index("tp")
    group = lax.axis_index("pair")
    q_col = pl.multiple_of((2 * tp + side) * 512, 512)
    kv_col = pl.multiple_of(tp * 256, 256)
    copies = [
        pltpu.make_async_copy(match_hbm, match, sems.at[0]),
        pltpu.make_async_copy(start_hbm, starts, sems.at[1]),
        pltpu.make_async_copy(q_hbm.at[0, :, :, pl.ds(q_col, 512)], q_ref, sems.at[2]),
        pltpu.make_async_copy(kv_hbm.at[0, :, :, pl.ds(kv_col, 256)], kv_ref, sems.at[3]),
    ]
    for copy in copies:
        copy.start()
    for copy in copies:
        copy.wait()
    q = q_ref[...].astype(f32)
    kv = kv_ref[...].astype(f32)
    rows = [q[t, 0:1, h * HD : (h + 1) * HD] for t in range(STEPS) for h in range(4)]
    rows += [kv[u, 0:1, :HD] for u in range(STEPS)]
    rows += [kv[u, 0:1, HD:] for u in range(STEPS)]
    sent = jnp.concatenate(rows, axis=0).astype(bf16)
    for p in range(GROUPS):
        out_ref[p] = sent

    holder = jnp.int32(0)
    for p in range(GROUPS):
        holder = jnp.where(match[p] == group, p, holder)
    numbers = [match[group], holder, starts[group]]
    sub = lax.broadcasted_iota(jnp.int32, ctrl_ref.shape, 0)
    ctrl = jnp.zeros(ctrl_ref.shape, f32)
    for k, number in enumerate(numbers):
        ctrl = jnp.where(sub == k, number.astype(f32), ctrl)
    ctrl_ref[...] = ctrl


def prep(matching, starts, decode_queries, decode_kv):
    shape = (GROUPS, 24, HD)
    hbm = pl.BlockSpec(memory_space=pltpu.HBM)
    return pl.pallas_call(
        prep_kernel,
        out_shape=(
            jax.ShapeDtypeStruct(shape, bf16),
            jax.ShapeDtypeStruct((ROWS, HD), f32),
        ),
        grid=(1,),
        in_specs=[hbm] * 4,
        out_specs=(whole(shape), whole((ROWS, HD))),
        scratch_shapes=[
            pltpu.SMEM((GROUPS,), jnp.int32),
            pltpu.SMEM((GROUPS,), jnp.int32),
            pltpu.VMEM((STEPS, ROWS, 512), bf16),
            pltpu.VMEM((STEPS, ROWS, 256), bf16),
            pltpu.SemaphoreType.DMA((4,)),
        ],
        compiler_params=params(4),
        cost_estimate=pl.CostEstimate(flops=10000, bytes_accessed=200000, transcendentals=0),
        name="prep",
    )(in_hbm(matching), in_hbm(starts), in_hbm(decode_queries), in_hbm(decode_kv))


def number_of(ctrl_ref, row):
    return jnp.max(ctrl_ref[row : row + 1, :]).astype(jnp.int32)


def decode_kernel(len_ref, q_ref, cache_ref, after_ref, *rest):
    theirs_ref, out_ref = rest if len(rest) == 2 else (None, rest[0])
    block = lax.axis_index("side") * 8 + lax.axis_index("tp")
    sub = lax.broadcasted_iota(jnp.int32, (ROWS, HD), 0)
    lane = lax.broadcasted_iota(jnp.int32, (ROWS, HD), 1)
    lens = jnp.zeros((ROWS, HD), jnp.int32)
    for k in range(ROWS - 1):
        lens = jnp.where(sub == k + 1, len_ref[0:1, k : k + 1], lens)
    allowed = (block * CACHE_BLOCK + lane < lens)[None]
    tiles = STEPS * 8
    small = lane % 32
    row_of = lax.broadcasted_iota(jnp.int32, (tiles * ROWS, HD), 0) % ROWS
    keep = [jnp.where(row_of == k + 1, 1.0, 0.0).astype(bf16) for k in range(ROWS - 1)]

    def spread(x):
        return jnp.concatenate([x * k for k in keep], axis=1)

    scores = []
    for head in range(2):
        q = jnp.concatenate(
            [
                q_ref[0, t, :, (head * 8 + g) * HD : (head * 8 + g + 1) * HD].astype(f32)
                for t in range(STEPS)
                for g in range(8)
            ],
            axis=0,
        ).astype(bf16)
        keys = jnp.concatenate(
            [cache_ref[0, k, :, head * 256 : head * 256 + HD] for k in range(ROWS - 1)], axis=1
        )
        scores.append(dot_t(spread(q), keys).reshape(tiles, ROWS, HD))
    for head in range(2):
        s = jnp.where(allowed, scores[head] * FACTOR, NEG_FILL)
        peak = jnp.max(s, axis=-1, keepdims=True)
        weights = jnp.where(allowed, jnp.exp(s - peak), 0.0)
        values = cache_ref[0, :, :, head * 256 + HD : head * 256 + 256].reshape(-1, HD)
        values = jnp.concatenate([values, jnp.ones_like(values)], axis=1)
        both = dot(spread(weights.reshape(tiles * ROWS, HD).astype(bf16)), values)
        both = both.reshape(STEPS, 8, ROWS, 2 * HD)
        peak = peak.reshape(STEPS, 8, ROWS, 1)
        for half in range(2):
            stats = jnp.zeros((ROWS, HD), f32)
            for t in range(STEPS):
                for h in range(4):
                    j = t * 4 + h
                    stats = jnp.where(small == j, peak[t, half * 4 + h], stats)
                    stats = jnp.where(small == 16 + j, both[t, half * 4 + h, :, HD:], stats)
            slot = head * 2 + half
            mix = both[:, half * 4 : half * 4 + 4, :, :HD].reshape(16, ROWS, HD)
            if theirs_ref is not None:
                other = theirs_ref[slot, 128:144].astype(f32)[:ROWS]
                other = other + pltpu.roll(other, HD - 32, 1) + pltpu.roll(other, HD - 64, 1)
                top = jnp.maximum(stats, other)
                mine, its = jnp.exp(stats - top), jnp.exp(other - top)
                total = mine * pltpu.roll(stats, HD - 16, 1) + its * pltpu.roll(other, HD - 16, 1)
                joined = jnp.where(lane < 16, top, jnp.where(lane < 32, pltpu.roll(total, 16, 1), 0.0))
                stats = joined + pltpu.roll(joined, 32, 1) + pltpu.roll(joined, 64, 1)
                tiles_in = theirs_ref[slot, 0:128].astype(f32).reshape(16, ROWS, HD)
                mix = jnp.stack(
                    [mine[:, j : j + 1] * mix[j] + its[:, j : j + 1] * tiles_in[j] for j in range(16)]
                )
            high = stats.astype(bf16).astype(f32)
            rest_of = stats - high
            mid = rest_of.astype(bf16).astype(f32)
            low = rest_of - mid
            packed = jnp.where(lane < 32, high, jnp.where(lane < 64, mid, low))
            out_ref[slot, 0:128] = mix.reshape(128, HD).astype(bf16)
            out_ref[slot, 128:144] = jnp.concatenate(
                [packed, jnp.zeros((ROWS, HD), f32)], axis=0
            ).astype(bf16)


def decode_parts(cache_lengths, decode_queries, kv_cache, after, theirs):
    rows = STAT_ROWS if theirs is None else PART_ROWS

    def heads(c):
        side = lax.axis_index("side")
        return (0, 0, 0, 2 * (1 - side if theirs is None else side) + c)

    operands = [in_hbm(cache_lengths), in_hbm(decode_queries), in_hbm(kv_cache), after]
    in_specs = [
        whole(cache_lengths.shape),
        pl.BlockSpec((1, STEPS, ROWS, 2048), heads),
        pl.BlockSpec((1, ROWS - 1, CACHE_BLOCK, 512), heads),
        pl.BlockSpec(memory_space=pl.ANY),
    ]
    if theirs is not None:
        operands.append(theirs)
        in_specs.append(pl.BlockSpec((4, STAT_ROWS, HD), lambda c: (c, 0, 0)))
    return pl.pallas_call(
        decode_kernel,
        out_shape=jax.ShapeDtypeStruct((8, rows, HD), bf16),
        grid=(2,),
        in_specs=in_specs,
        out_specs=pl.BlockSpec((4, rows, HD), lambda c: (c, 0, 0)),
        compiler_params=params(16),
        cost_estimate=pl.CostEstimate(
            flops=1000000000, bytes_accessed=2400000, transcendentals=150000
        ),
        name="decode_parts",
    )(*operands)


def hand_over_kernel(ctrl_ref, own_ref, other_ref, parts_in, parts_ref, sems):
    side = lax.axis_index("side")
    tp = lax.axis_index("tp")
    holder = number_of(ctrl_ref, HOLDER)

    @pl.when(tp // 4 == side)
    def _():
        copies = []
        for k, (ref, core) in enumerate(((own_ref, side), (other_ref, 1 - side))):
            target = parts_ref.at[(2 * tp + core) % 8, 144:160]
            copies.append(pltpu.make_async_copy(ref.at[holder], target, sems.at[k]))
        for copy in copies:
            copy.start()
        for copy in copies:
            copy.wait()


def hand_over(ctrl, own, other, parts):
    anywhere = pl.BlockSpec(memory_space=pl.ANY)
    return pl.pallas_call(
        hand_over_kernel,
        out_shape=jax.ShapeDtypeStruct(parts.shape, bf16),
        grid=(1,),
        in_specs=[whole(ctrl.shape), anywhere, anywhere, anywhere],
        out_specs=anywhere,
        scratch_shapes=[pltpu.SemaphoreType.DMA((2,))],
        input_output_aliases={3: 0},
        compiler_params=params(4),
        cost_estimate=pl.CostEstimate(flops=0, bytes_accessed=16384, transcendentals=0),
        name="hand_over",
    )(ctrl, own, other, parts)


def norms_kernel(prefix_ref, own_ref, other_ref, after_ref, longest_ref):
    def norm(ref):
        k = ref[0, :, :HD].astype(f32)
        return jnp.max(jnp.sum(k * k, axis=-1, keepdims=True), axis=0, keepdims=True)

    longest = jnp.maximum(norm(prefix_ref), jnp.maximum(norm(own_ref), norm(other_ref)))
    longest_ref[...] = jnp.broadcast_to(longest, longest_ref.shape)


def norms(prefix, own, other, after):
    return pl.pallas_call(
        norms_kernel,
        out_shape=jax.ShapeDtypeStruct((ROWS, HD), f32),
        grid=(1,),
        in_specs=[
            whole(prefix.shape),
            whole(own.shape),
            whole(other.shape),
            pl.BlockSpec(memory_space=pl.ANY),
        ],
        out_specs=whole((ROWS, HD)),
        compiler_params=params(8),
        cost_estimate=pl.CostEstimate(flops=2000000, bytes_accessed=1000000, transcendentals=0),
        name="norms",
    )(prefix, own, other, after)


def prompt_kernel(
    pieces, ctrl_ref, q_ref, prefix_ref, own_ref, other_ref, longest_ref, after_ref, prior, out_hbm, mixed, least, done, sems
):
    side = lax.axis_index("side")
    tokens = 256
    scale = FACTOR * LOG2E
    longest = longest_ref[0:1, 0:1]
    pos = lax.broadcasted_iota(jnp.int32, (PREFIX, HD), 0).astype(f32)
    kept = jnp.where(pos < ctrl_ref[START : START + 1, :], 1.0, 0.0)
    mixed[SEG_HALF : SEG_HALF + PREFIX, :HD] = (prefix_ref[0, :, HD:].astype(f32) * kept).astype(bf16)
    mixed[SEG_HALF : SEG_HALF + PREFIX, HD:] = kept.astype(bf16)
    ones = jnp.ones((SEG_HALF, HD), bf16)
    mixed[:SEG_HALF] = jnp.concatenate([other_ref[0, :, HD:], ones], axis=1)
    mixed[SEG_HALF + PREFIX :] = jnp.concatenate([own_ref[0, :, HD:], ones], axis=1)
    causal = lax.broadcasted_iota(jnp.int32, (tokens, tokens), 1) <= lax.broadcasted_iota(
        jnp.int32, (tokens, tokens), 0
    )

    def key_parts(half, later):
        parts = []
        if later:
            parts += [(other_ref, n) for n in range(0, SEG_HALF, 256)]
        parts += [(prefix_ref, n) for n in range(0, PREFIX, 256)]
        parts += [(own_ref, n) for n in range(0, (half + 1) * tokens, 256)]
        return parts

    def mix(weights, half, later):
        first = 0 if later else SEG_HALF
        last = SEG_HALF + PREFIX + (half + 1) * tokens
        return dot(jnp.concatenate(weights, axis=1), mixed[first:last])

    def lanes(start, size):
        return pl.ds(start if isinstance(start, int) else pl.multiple_of(start, size), size)

    def queries(half, head):
        cols = lanes(head * HD, HD)
        return q_ref[0, half * tokens : (half + 1) * tokens, cols]

    def block(half, head, later):
        q = queries(half, head)
        wide_q = q.astype(f32)
        norms = jnp.sum(wide_q * wide_q, axis=-1, keepdims=True)
        bound = jnp.sqrt(norms * longest) * scale
        parts = key_parts(half, later)
        weights = []
        for number, (ref, n) in enumerate(parts):
            w = jnp.exp2(dot_t(q, ref[0, n : n + 256, :HD]) * scale - bound)
            if number == len(parts) - 1:
                w = jnp.where(causal, w, 0.0)
            weights.append(w.astype(bf16))
        total = mix(weights, half, later)
        sums = total[:, HD:]
        least[...] = jnp.minimum(least[...], sums)
        return (total[:, :HD] / sums).astype(bf16)

    def block_exact(half, head, later):
        q = queries(half, head)
        parts = key_parts(half, later)
        scores = []
        for number, (ref, n) in enumerate(parts):
            s = dot_t(q, ref[0, n : n + 256, :HD])
            if ref is prefix_ref:
                at = n + lax.broadcasted_iota(jnp.int32, s.shape, 1)
                s = jnp.where(at.astype(f32) < ctrl_ref[START : START + 1, 0:1], s, NEG_FILL)
            if number == len(parts) - 1:
                s = jnp.where(causal, s, NEG_FILL)
            scores.append(s)
        peak = functools.reduce(
            jnp.maximum, [jnp.max(s, axis=-1, keepdims=True) for s in scores]
        )
        weights = [jnp.exp2((s - peak) * scale).astype(bf16) for s in scores]
        total = mix(weights, half, later)
        return (total[:, :HD] / total[:, HD:]).astype(bf16)

    def result_copy(pair, half, slot):
        rows = pl.ds(half * tokens, tokens)
        cols = lanes(pair * 2 * HD, 2 * HD)
        return pltpu.make_async_copy(done.at[slot], out_hbm.at[0, rows, cols], sems.at[slot])

    def piece(one, pair, half, slot, later):
        for head in range(2):
            done[slot, :, head * HD : (head + 1) * HD] = one(half, pair * 2 + head, later)
        result_copy(pair, half, slot).start()

    least[...] = jnp.ones(least.shape, f32)
    for later in (False, True):

        @pl.when(side == int(later))
        def _(later=later):
            for slot, (pair, half) in enumerate(pieces):
                piece(block, pair, half, slot, later)
            loose = jnp.min(least[...]) < 1e-27
            for slot, (pair, half) in enumerate(pieces):
                result_copy(pair, half, slot).wait()

            @pl.when(loose)
            def _():
                for half in range(2):
                    pairs = [pair for pair, h in pieces if h == half]

                    @pl.loop(pairs[0], pairs[-1] + 1)
                    def _(pair):
                        piece(block_exact, pair, half, 0, later)
                        result_copy(pair, half, 0).wait()


def prompt(pieces, ctrl, queries, prefix, own, other, longest, after, prior):
    operands = [ctrl, queries, prefix, own, other, longest, after]
    units = sum(6 + half for _, half in pieces) * 2
    anywhere = pl.BlockSpec(memory_space=pl.ANY)
    return pl.pallas_call(
        functools.partial(prompt_kernel, pieces),
        out_shape=jax.ShapeDtypeStruct(queries.shape, bf16),
        grid=(1,),
        in_specs=[whole(x.shape) for x in operands[:-1]]
        + [anywhere, pl.BlockSpec(memory_space=pltpu.HBM) if prior is not None else anywhere],
        out_specs=pl.BlockSpec(memory_space=pltpu.HBM),
        scratch_shapes=[
            pltpu.VMEM((2 * SEG_HALF + PREFIX, 2 * HD), bf16),
            pltpu.VMEM((256, HD), f32),
            pltpu.VMEM((len(pieces), 256, 2 * HD), bf16),
            pltpu.SemaphoreType.DMA((len(pieces),)),
        ],
        input_output_aliases={7: 0} if prior is not None else {},
        compiler_params=params(24),
        cost_estimate=pl.CostEstimate(
            flops=units * 256 * 256 * 128 * 6, bytes_accessed=2000000, transcendentals=units * 65536
        ),
        name="prompt",
    )(*operands, after if prior is None else in_hbm(prior))


def first_row_kernel(ctrl_ref, got_ref, prefix_ref, own_ref, other_ref, after_ref, out_ref):
    asked = got_ref[number_of(ctrl_ref, ASKED)].astype(f32)
    q = asked[0:16].astype(bf16)
    fresh = asked[16:24]
    pad = jnp.zeros((12, HD), f32)
    fresh_k = jnp.concatenate([fresh[:4], pad], axis=0).astype(bf16)
    fresh_v = jnp.concatenate([fresh[4:], pad], axis=0).astype(bf16)
    s0 = dot_t(q, prefix_ref[0, :, :HD])
    pos = lax.broadcasted_iota(jnp.int32, s0.shape, 1)
    s0 = jnp.where(pos.astype(f32) < ctrl_ref[START : START + 1, 0:1], s0, NEG_FILL)
    s1 = dot_t(q, own_ref[0, :, :HD])
    s2 = dot_t(q, other_ref[0, :, :HD])
    s3 = dot_t(q, fresh_k)
    step = lax.broadcasted_iota(jnp.int32, s3.shape, 0) // 4
    pos = lax.broadcasted_iota(jnp.int32, s3.shape, 1)
    s3 = jnp.where(pos <= step, s3, NEG_FILL)
    scores = (s0, s1, s2, s3)
    values = (prefix_ref[0, :, HD:], own_ref[0, :, HD:], other_ref[0, :, HD:], fresh_v)
    peak = functools.reduce(jnp.maximum, [jnp.max(s, axis=-1, keepdims=True) for s in scores])
    mix = jnp.zeros((16, HD), f32)
    totals = jnp.zeros((16, 1), f32)
    for s, v in zip(scores, values):
        w = jnp.exp2((s - peak) * (FACTOR * LOG2E))
        totals += jnp.sum(w, axis=-1, keepdims=True)
        mix += dot(w.astype(bf16), v)
    out = (mix / totals).astype(bf16)
    for p in range(GROUPS):
        out_ref[p] = out


def first_row(ctrl, got, prefix, own, other, after):
    shape = (GROUPS, 16, HD)
    return pl.pallas_call(
        first_row_kernel,
        out_shape=jax.ShapeDtypeStruct(shape, bf16),
        grid=(1,),
        in_specs=[
            whole(ctrl.shape),
            whole(got.shape),
            whole(prefix.shape),
            whole(own.shape),
            whole(other.shape),
            pl.BlockSpec(memory_space=pl.ANY),
        ],
        out_specs=whole(shape),
        compiler_params=params(8),
        cost_estimate=pl.CostEstimate(
            flops=20000000, bytes_accessed=1300000, transcendentals=33000
        ),
        name="first_row",
    )(ctrl, got, prefix, own, other, after)


def merge_kernel(parts_ref, q_ref, kv_ref, out_ref):
    side = lax.axis_index("side")
    tp = lax.axis_index("tp")
    block = side * 8 + tp
    q = q_ref[0, :, :, pl.ds(pl.multiple_of(block * 512, 512), 512)].astype(f32)
    kv = kv_ref[0, :, :, pl.ds(pl.multiple_of((block // 2) * 256, 256), 256)].astype(f32)
    sub = lax.broadcasted_iota(jnp.int32, (ROWS, HD), 0)
    lane = lax.broadcasted_iota(jnp.int32, (ROWS, HD), 1)

    peaks, totals = [], []
    for b in range(8):
        x = parts_ref[b, 128:144].astype(f32)[:ROWS]
        x = x + pltpu.roll(x, HD - 32, 1) + pltpu.roll(x, HD - 64, 1)
        peaks.append(x)
        totals.append(pltpu.roll(x, HD - 16, 1))
    top = functools.reduce(jnp.maximum, peaks)
    fresh = {}
    fresh_top = jnp.full((ROWS, HD), NEG_FILL, f32)
    for t in range(STEPS):
        for h in range(4):
            j = t * 4 + h
            qt = q[t, :, h * HD : (h + 1) * HD]
            for u in range(t + 1):
                s = jnp.sum(qt * kv[u, :, :HD], axis=-1, keepdims=True) * FACTOR
                fresh[j, u] = s
                fresh_top = jnp.where(lane == j, jnp.maximum(fresh_top, s), fresh_top)
    top = jnp.maximum(top, fresh_top)
    scales = [jnp.exp(p - top) for p in peaks]
    total = functools.reduce(jnp.add, [s * t for s, t in zip(scales, totals)])
    first = parts_ref[side * 4 + tp // 2, 144:160].astype(f32)
    for t in range(STEPS):
        for h in range(4):
            j = t * 4 + h
            acc = jnp.zeros((ROWS, HD), f32)
            for b in range(8):
                tile = parts_ref[b, (j // 2) * 16 : (j // 2) * 16 + 16].astype(f32)
                acc += scales[b][:, j : j + 1] * tile[(j % 2) * 8 : (j % 2) * 8 + 8]
            denom = total[:, j : j + 1]
            for u in range(t + 1):
                w = jnp.exp(fresh[j, u] - top[:, j : j + 1])
                acc += w * kv[u, :, HD:]
                denom = denom + w
            out = acc / denom
            out = jnp.where(sub == 0, first[j : j + 1], out)
            out_ref[0, t, :, h * HD : (h + 1) * HD] = out.astype(bf16)


def merge(parts, decode_queries, decode_kv):
    shape = (1, STEPS, ROWS, 512)
    return pl.pallas_call(
        merge_kernel,
        out_shape=jax.ShapeDtypeStruct(shape, bf16),
        grid=(1,),
        in_specs=[whole(parts.shape), whole(decode_queries.shape), whole(decode_kv.shape)],
        out_specs=whole(shape),
        compiler_params=params(8),
        cost_estimate=pl.CostEstimate(flops=3000000, bytes_accessed=1300000, transcendentals=60000),
        name="merge",
    )(parts, decode_queries, decode_kv)


def exchange(x, axis):
    return lax.all_to_all(x, axis, split_axis=0, concat_axis=0, tiled=True)


def local(
    segment_queries,
    segment_kv,
    prefix_kv,
    kv_cache,
    decode_queries,
    decode_kv,
    matching,
    segment_starts,
    cache_lengths,
):
    other_kv = lax.ppermute(segment_kv, "side", [(0, 1), (1, 0)])
    sent, ctrl = prep(matching, segment_starts, decode_queries, decode_kv)
    sent, prefix, own, queries = lax.optimization_barrier(
        (sent, prefix_kv, segment_kv, segment_queries)
    )
    keys = (prefix, own, other_kv)
    cache = (cache_lengths, decode_queries, kv_cache)
    given = decode_parts(*cache, sent, None)
    theirs = lax.ppermute(given, "side", [(0, 1), (1, 0)])
    longest = norms(*keys, given)
    first = first_row(ctrl, exchange(sent, "pair"), *keys, longest)
    parts = decode_parts(*cache, first, theirs)
    answered, parts = lax.optimization_barrier((exchange(first, "pair"), parts))
    swapped = lax.ppermute(answered, "side", [(0, 1), (1, 0)])
    parts = hand_over(ctrl, answered, swapped, parts)
    out = prompt(PIECES, ctrl, queries, *keys, longest, parts, None)
    parts = exchange(parts, "tp")
    decode_out = merge(parts, decode_queries, decode_kv)
    return (out, decode_out)


def solution(mesh):
    in_specs = (
        P("pair", "side", "tp"),
        P("pair", "side", "tp"),
        P("pair", None, "tp"),
        P("pair", None, ("side", "tp"), None),
        P("pair", None, None, None),
        P("pair", None, None, None),
        P(),
        P(),
        P("pair", None),
    )
    out_specs = (P("pair", "side", "tp"), P("pair", None, None, ("side", "tp")))
    return jax.shard_map(local, mesh=mesh, in_specs=in_specs, out_specs=out_specs, check_vma=False)
```

```python
import functools
import math

import jax
import jax.numpy as jnp
from jax import lax
from jax.experimental import pallas as pl
from jax.experimental.pallas import tpu as pltpu
from jax.sharding import PartitionSpec as P

H = 64
KVH = 8
HD = 128
STEPS = 4
ROWS = 8
GROUPS = 16
PIECES = [(pair, half) for pair in range(4) for half in range(2)]
EARLY = 2
SEG_HALF = 512
PREFIX = 1024
CACHE_BLOCK = 128

FACTOR = 1.0 / math.sqrt(HD)
LOG2E = 1.4426950408889634
NEG_FILL = -1e30
STAT_ROWS = 144
PART_ROWS = 160

f32 = jnp.float32
bf16 = jnp.bfloat16


def params(mib):
    return pltpu.CompilerParams(vmem_limit_bytes=mib * 1024 * 1024)


def in_hbm(x):
    return pltpu.with_memory_space_constraint(x, pltpu.HBM)


def whole(shape):
    return pl.BlockSpec(shape, lambda *_: (0,) * len(shape))


def dot_t(a, b):
    return lax.dot_general(a, b, (((1,), (1,)), ((), ())), preferred_element_type=f32)


def dot(a, b):
    return jnp.dot(a, b, preferred_element_type=f32)


ASKED = 0
HOLDER = 1
START = 2


def prep_kernel(match_hbm, start_hbm, q_hbm, kv_hbm, out_ref, ctrl_ref, match, starts, q_ref, kv_ref, sems):
    side = lax.axis_index("side")
    tp = lax.axis_index("tp")
    group = lax.axis_index("pair")
    q_col = pl.multiple_of((2 * tp + side) * 512, 512)
    kv_col = pl.multiple_of(tp * 256, 256)
    copies = [
        pltpu.make_async_copy(match_hbm, match, sems.at[0]),
        pltpu.make_async_copy(start_hbm, starts, sems.at[1]),
        pltpu.make_async_copy(q_hbm.at[0, :, :, pl.ds(q_col, 512)], q_ref, sems.at[2]),
        pltpu.make_async_copy(kv_hbm.at[0, :, :, pl.ds(kv_col, 256)], kv_ref, sems.at[3]),
    ]
    for copy in copies:
        copy.start()
    for copy in copies:
        copy.wait()
    q = q_ref[...].astype(f32)
    kv = kv_ref[...].astype(f32)
    rows = [q[t, 0:1, h * HD : (h + 1) * HD] for t in range(STEPS) for h in range(4)]
    rows += [kv[u, 0:1, :HD] for u in range(STEPS)]
    rows += [kv[u, 0:1, HD:] for u in range(STEPS)]
    sent = jnp.concatenate(rows, axis=0).astype(bf16)
    for p in range(GROUPS):
        out_ref[p] = sent

    holder = jnp.int32(0)
    for p in range(GROUPS):
        holder = jnp.where(match[p] == group, p, holder)
    numbers = [match[group], holder, starts[group]]
    sub = lax.broadcasted_iota(jnp.int32, ctrl_ref.shape, 0)
    ctrl = jnp.zeros(ctrl_ref.shape, f32)
    for k, number in enumerate(numbers):
        ctrl = jnp.where(sub == k, number.astype(f32), ctrl)
    ctrl_ref[...] = ctrl


def prep(matching, starts, decode_queries, decode_kv):
    shape = (GROUPS, 24, HD)
    hbm = pl.BlockSpec(memory_space=pltpu.HBM)
    return pl.pallas_call(
        prep_kernel,
        out_shape=(
            jax.ShapeDtypeStruct(shape, bf16),
            jax.ShapeDtypeStruct((ROWS, HD), f32),
        ),
        grid=(1,),
        in_specs=[hbm] * 4,
        out_specs=(whole(shape), whole((ROWS, HD))),
        scratch_shapes=[
            pltpu.SMEM((GROUPS,), jnp.int32),
            pltpu.SMEM((GROUPS,), jnp.int32),
            pltpu.VMEM((STEPS, ROWS, 512), bf16),
            pltpu.VMEM((STEPS, ROWS, 256), bf16),
            pltpu.SemaphoreType.DMA((4,)),
        ],
        compiler_params=params(4),
        cost_estimate=pl.CostEstimate(flops=10000, bytes_accessed=200000, transcendentals=0),
        name="prep",
    )(in_hbm(matching), in_hbm(starts), in_hbm(decode_queries), in_hbm(decode_kv))


def number_of(ctrl_ref, row):
    return jnp.max(ctrl_ref[row : row + 1, :]).astype(jnp.int32)


def decode_kernel(len_ref, q_ref, cache_ref, after_ref, *rest):
    theirs_ref, out_ref = rest if len(rest) == 2 else (None, rest[0])
    block = lax.axis_index("side") * 8 + lax.axis_index("tp")
    sub = lax.broadcasted_iota(jnp.int32, (ROWS, HD), 0)
    lane = lax.broadcasted_iota(jnp.int32, (ROWS, HD), 1)
    lens = jnp.zeros((ROWS, HD), jnp.int32)
    for k in range(ROWS - 1):
        lens = jnp.where(sub == k + 1, len_ref[0:1, k : k + 1], lens)
    allowed = (block * CACHE_BLOCK + lane < lens)[None]
    tiles = STEPS * 8
    small = lane % 32
    row_of = lax.broadcasted_iota(jnp.int32, (tiles * ROWS, HD), 0) % ROWS
    keep = [jnp.where(row_of == k + 1, 1.0, 0.0).astype(bf16) for k in range(ROWS - 1)]

    def spread(x):
        return jnp.concatenate([x * k for k in keep], axis=1)

    scores = []
    for head in range(2):
        q = jnp.concatenate(
            [
                q_ref[0, t, :, (head * 8 + g) * HD : (head * 8 + g + 1) * HD].astype(f32)
                for t in range(STEPS)
                for g in range(8)
            ],
            axis=0,
        ).astype(bf16)
        keys = jnp.concatenate(
            [cache_ref[0, k, :, head * 256 : head * 256 + HD] for k in range(ROWS - 1)], axis=1
        )
        scores.append(dot_t(spread(q), keys).reshape(tiles, ROWS, HD))
    for head in range(2):
        s = jnp.where(allowed, scores[head] * FACTOR, NEG_FILL)
        peak = jnp.max(s, axis=-1, keepdims=True)
        weights = jnp.where(allowed, jnp.exp(s - peak), 0.0)
        values = cache_ref[0, :, :, head * 256 + HD : head * 256 + 256].reshape(-1, HD)
        values = jnp.concatenate([values, jnp.ones_like(values)], axis=1)
        both = dot(spread(weights.reshape(tiles * ROWS, HD).astype(bf16)), values)
        both = both.reshape(STEPS, 8, ROWS, 2 * HD)
        peak = peak.reshape(STEPS, 8, ROWS, 1)
        for half in range(2):
            stats = jnp.zeros((ROWS, HD), f32)
            for t in range(STEPS):
                for h in range(4):
                    j = t * 4 + h
                    stats = jnp.where(small == j, peak[t, half * 4 + h], stats)
                    stats = jnp.where(small == 16 + j, both[t, half * 4 + h, :, HD:], stats)
            slot = head * 2 + half
            mix = both[:, half * 4 : half * 4 + 4, :, :HD].reshape(16, ROWS, HD)
            if theirs_ref is not None:
                other = theirs_ref[slot, 128:144].astype(f32)[:ROWS]
                other = other + pltpu.roll(other, HD - 32, 1) + pltpu.roll(other, HD - 64, 1)
                top = jnp.maximum(stats, other)
                mine, its = jnp.exp(stats - top), jnp.exp(other - top)
                total = mine * pltpu.roll(stats, HD - 16, 1) + its * pltpu.roll(other, HD - 16, 1)
                joined = jnp.where(lane < 16, top, jnp.where(lane < 32, pltpu.roll(total, 16, 1), 0.0))
                stats = joined + pltpu.roll(joined, 32, 1) + pltpu.roll(joined, 64, 1)
                tiles_in = theirs_ref[slot, 0:128].astype(f32).reshape(16, ROWS, HD)
                mix = jnp.stack(
                    [mine[:, j : j + 1] * mix[j] + its[:, j : j + 1] * tiles_in[j] for j in range(16)]
                )
            high = stats.astype(bf16).astype(f32)
            rest_of = stats - high
            mid = rest_of.astype(bf16).astype(f32)
            low = rest_of - mid
            packed = jnp.where(lane < 32, high, jnp.where(lane < 64, mid, low))
            out_ref[slot, 0:128] = mix.reshape(128, HD).astype(bf16)
            out_ref[slot, 128:144] = jnp.concatenate(
                [packed, jnp.zeros((ROWS, HD), f32)], axis=0
            ).astype(bf16)


def decode_parts(cache_lengths, decode_queries, kv_cache, after, theirs):
    rows = STAT_ROWS if theirs is None else PART_ROWS

    def heads(c):
        side = lax.axis_index("side")
        return (0, 0, 0, 2 * (1 - side if theirs is None else side) + c)

    operands = [in_hbm(cache_lengths), in_hbm(decode_queries), in_hbm(kv_cache), after]
    in_specs = [
        whole(cache_lengths.shape),
        pl.BlockSpec((1, STEPS, ROWS, 2048), heads),
        pl.BlockSpec((1, ROWS - 1, CACHE_BLOCK, 512), heads),
        pl.BlockSpec(memory_space=pl.ANY),
    ]
    if theirs is not None:
        operands.append(theirs)
        in_specs.append(pl.BlockSpec((4, STAT_ROWS, HD), lambda c: (c, 0, 0)))
    return pl.pallas_call(
        decode_kernel,
        out_shape=jax.ShapeDtypeStruct((8, rows, HD), bf16),
        grid=(2,),
        in_specs=in_specs,
        out_specs=pl.BlockSpec((4, rows, HD), lambda c: (c, 0, 0)),
        compiler_params=params(16),
        cost_estimate=pl.CostEstimate(
            flops=1000000000, bytes_accessed=2400000, transcendentals=150000
        ),
        name="decode_parts",
    )(*operands)


def hand_over_kernel(ctrl_ref, own_ref, other_ref, parts_in, parts_ref, sems):
    side = lax.axis_index("side")
    tp = lax.axis_index("tp")
    holder = number_of(ctrl_ref, HOLDER)

    @pl.when(tp // 4 == side)
    def _():
        copies = []
        for k, (ref, core) in enumerate(((own_ref, side), (other_ref, 1 - side))):
            target = parts_ref.at[(2 * tp + core) % 8, 144:160]
            copies.append(pltpu.make_async_copy(ref.at[holder], target, sems.at[k]))
        for copy in copies:
            copy.start()
        for copy in copies:
            copy.wait()


def hand_over(ctrl, own, other, parts):
    anywhere = pl.BlockSpec(memory_space=pl.ANY)
    return pl.pallas_call(
        hand_over_kernel,
        out_shape=jax.ShapeDtypeStruct(parts.shape, bf16),
        grid=(1,),
        in_specs=[whole(ctrl.shape), anywhere, anywhere, anywhere],
        out_specs=anywhere,
        scratch_shapes=[pltpu.SemaphoreType.DMA((2,))],
        input_output_aliases={3: 0},
        compiler_params=params(4),
        cost_estimate=pl.CostEstimate(flops=0, bytes_accessed=16384, transcendentals=0),
        name="hand_over",
    )(ctrl, own, other, parts)


def norms_kernel(prefix_ref, own_ref, other_ref, after_ref, longest_ref):
    def norm(ref):
        k = ref[0, :, :HD].astype(f32)
        return jnp.max(jnp.sum(k * k, axis=-1, keepdims=True), axis=0, keepdims=True)

    longest = jnp.maximum(norm(prefix_ref), jnp.maximum(norm(own_ref), norm(other_ref)))
    longest_ref[...] = jnp.broadcast_to(longest, longest_ref.shape)


def norms(prefix, own, other, after):
    return pl.pallas_call(
        norms_kernel,
        out_shape=jax.ShapeDtypeStruct((ROWS, HD), f32),
        grid=(1,),
        in_specs=[
            whole(prefix.shape),
            whole(own.shape),
            whole(other.shape),
            pl.BlockSpec(memory_space=pl.ANY),
        ],
        out_specs=whole((ROWS, HD)),
        compiler_params=params(8),
        cost_estimate=pl.CostEstimate(flops=2000000, bytes_accessed=1000000, transcendentals=0),
        name="norms",
    )(prefix, own, other, after)


def prompt_kernel(
    pieces, ctrl_ref, q_ref, prefix_ref, own_ref, other_ref, longest_ref, after_ref, prior, out_hbm, mixed, least, done, sems
):
    side = lax.axis_index("side")
    tokens = 256
    scale = FACTOR * LOG2E
    longest = longest_ref[0:1, 0:1]
    pos = lax.broadcasted_iota(jnp.int32, (PREFIX, HD), 0).astype(f32)
    kept = jnp.where(pos < ctrl_ref[START : START + 1, :], 1.0, 0.0)
    mixed[SEG_HALF : SEG_HALF + PREFIX, :HD] = (prefix_ref[0, :, HD:].astype(f32) * kept).astype(bf16)
    mixed[SEG_HALF : SEG_HALF + PREFIX, HD:] = kept.astype(bf16)
    ones = jnp.ones((SEG_HALF, HD), bf16)
    mixed[:SEG_HALF] = jnp.concatenate([other_ref[0, :, HD:], ones], axis=1)
    mixed[SEG_HALF + PREFIX :] = jnp.concatenate([own_ref[0, :, HD:], ones], axis=1)
    causal = lax.broadcasted_iota(jnp.int32, (tokens, tokens), 1) <= lax.broadcasted_iota(
        jnp.int32, (tokens, tokens), 0
    )

    def key_parts(half, later):
        parts = []
        if later:
            parts += [(other_ref, n) for n in range(0, SEG_HALF, 256)]
        parts += [(prefix_ref, n) for n in range(0, PREFIX, 256)]
        parts += [(own_ref, n) for n in range(0, (half + 1) * tokens, 256)]
        return parts

    def mix(weights, half, later):
        first = 0 if later else SEG_HALF
        last = SEG_HALF + PREFIX + (half + 1) * tokens
        return dot(jnp.concatenate(weights, axis=1), mixed[first:last])

    def lanes(start, size):
        return pl.ds(start if isinstance(start, int) else pl.multiple_of(start, size), size)

    def queries(half, head):
        cols = lanes(head * HD, HD)
        return q_ref[0, half * tokens : (half + 1) * tokens, cols]

    def block(half, head, later):
        q = queries(half, head)
        wide_q = q.astype(f32)
        norms = jnp.sum(wide_q * wide_q, axis=-1, keepdims=True)
        bound = jnp.sqrt(norms * longest) * scale
        parts = key_parts(half, later)
        weights = []
        for number, (ref, n) in enumerate(parts):
            w = jnp.exp2(dot_t(q, ref[0, n : n + 256, :HD]) * scale - bound)
            if number == len(parts) - 1:
                w = jnp.where(causal, w, 0.0)
            weights.append(w.astype(bf16))
        total = mix(weights, half, later)
        sums = total[:, HD:]
        least[...] = jnp.minimum(least[...], sums)
        return (total[:, :HD] / sums).astype(bf16)

    def block_exact(half, head, later):
        q = queries(half, head)
        parts = key_parts(half, later)
        scores = []
        for number, (ref, n) in enumerate(parts):
            s = dot_t(q, ref[0, n : n + 256, :HD])
            if ref is prefix_ref:
                at = n + lax.broadcasted_iota(jnp.int32, s.shape, 1)
                s = jnp.where(at.astype(f32) < ctrl_ref[START : START + 1, 0:1], s, NEG_FILL)
            if number == len(parts) - 1:
                s = jnp.where(causal, s, NEG_FILL)
            scores.append(s)
        peak = functools.reduce(
            jnp.maximum, [jnp.max(s, axis=-1, keepdims=True) for s in scores]
        )
        weights = [jnp.exp2((s - peak) * scale).astype(bf16) for s in scores]
        total = mix(weights, half, later)
        return (total[:, :HD] / total[:, HD:]).astype(bf16)

    def result_copy(pair, half, slot):
        rows = pl.ds(half * tokens, tokens)
        cols = lanes(pair * 2 * HD, 2 * HD)
        return pltpu.make_async_copy(done.at[slot], out_hbm.at[0, rows, cols], sems.at[slot])

    def piece(one, pair, half, slot, later):
        for head in range(2):
            done[slot, :, head * HD : (head + 1) * HD] = one(half, pair * 2 + head, later)
        result_copy(pair, half, slot).start()

    least[...] = jnp.ones(least.shape, f32)
    for later in (False, True):

        @pl.when(side == int(later))
        def _(later=later):
            for slot, (pair, half) in enumerate(pieces):
                piece(block, pair, half, slot, later)
            loose = jnp.min(least[...]) < 1e-27
            for slot, (pair, half) in enumerate(pieces):
                result_copy(pair, half, slot).wait()

            @pl.when(loose)
            def _():
                for half in range(2):
                    pairs = [pair for pair, h in pieces if h == half]

                    @pl.loop(pairs[0], pairs[-1] + 1)
                    def _(pair):
                        piece(block_exact, pair, half, 0, later)
                        result_copy(pair, half, 0).wait()


def prompt(pieces, ctrl, queries, prefix, own, other, longest, after, prior):
    operands = [ctrl, queries, prefix, own, other, longest, after]
    units = sum(6 + half for _, half in pieces) * 2 if prior is not None else 0
    anywhere = pl.BlockSpec(memory_space=pl.ANY)
    return pl.pallas_call(
        functools.partial(prompt_kernel, pieces),
        out_shape=jax.ShapeDtypeStruct(queries.shape, bf16),
        grid=(1,),
        in_specs=[whole(x.shape) for x in operands[:-1]]
        + [anywhere, pl.BlockSpec(memory_space=pltpu.HBM) if prior is not None else anywhere],
        out_specs=pl.BlockSpec(memory_space=pltpu.HBM),
        scratch_shapes=[
            pltpu.VMEM((2 * SEG_HALF + PREFIX, 2 * HD), bf16),
            pltpu.VMEM((256, HD), f32),
            pltpu.VMEM((len(pieces), 256, 2 * HD), bf16),
            pltpu.SemaphoreType.DMA((len(pieces),)),
        ],
        input_output_aliases={7: 0} if prior is not None else {},
        compiler_params=params(24),
        cost_estimate=pl.CostEstimate(
            flops=units * 256 * 256 * 128 * 6 + 1000, bytes_accessed=1000, transcendentals=0
        ),
        name="prompt",
    )(*operands, after if prior is None else in_hbm(prior))


def first_row_kernel(ctrl_ref, got_ref, prefix_ref, own_ref, other_ref, after_ref, out_ref):
    asked = got_ref[number_of(ctrl_ref, ASKED)].astype(f32)
    q = asked[0:16].astype(bf16)
    fresh = asked[16:24]
    pad = jnp.zeros((12, HD), f32)
    fresh_k = jnp.concatenate([fresh[:4], pad], axis=0).astype(bf16)
    fresh_v = jnp.concatenate([fresh[4:], pad], axis=0).astype(bf16)
    s0 = dot_t(q, prefix_ref[0, :, :HD])
    pos = lax.broadcasted_iota(jnp.int32, s0.shape, 1)
    s0 = jnp.where(pos.astype(f32) < ctrl_ref[START : START + 1, 0:1], s0, NEG_FILL)
    s1 = dot_t(q, own_ref[0, :, :HD])
    s2 = dot_t(q, other_ref[0, :, :HD])
    s3 = dot_t(q, fresh_k)
    step = lax.broadcasted_iota(jnp.int32, s3.shape, 0) // 4
    pos = lax.broadcasted_iota(jnp.int32, s3.shape, 1)
    s3 = jnp.where(pos <= step, s3, NEG_FILL)
    scores = (s0, s1, s2, s3)
    values = (prefix_ref[0, :, HD:], own_ref[0, :, HD:], other_ref[0, :, HD:], fresh_v)
    peak = functools.reduce(jnp.maximum, [jnp.max(s, axis=-1, keepdims=True) for s in scores])
    mix = jnp.zeros((16, HD), f32)
    totals = jnp.zeros((16, 1), f32)
    for s, v in zip(scores, values):
        w = jnp.exp2((s - peak) * (FACTOR * LOG2E))
        totals += jnp.sum(w, axis=-1, keepdims=True)
        mix += dot(w.astype(bf16), v)
    out = (mix / totals).astype(bf16)
    for p in range(GROUPS):
        out_ref[p] = out


def first_row(ctrl, got, prefix, own, other, after):
    shape = (GROUPS, 16, HD)
    return pl.pallas_call(
        first_row_kernel,
        out_shape=jax.ShapeDtypeStruct(shape, bf16),
        grid=(1,),
        in_specs=[
            whole(ctrl.shape),
            whole(got.shape),
            whole(prefix.shape),
            whole(own.shape),
            whole(other.shape),
            pl.BlockSpec(memory_space=pl.ANY),
        ],
        out_specs=whole(shape),
        compiler_params=params(8),
        cost_estimate=pl.CostEstimate(
            flops=20000000, bytes_accessed=1300000, transcendentals=33000
        ),
        name="first_row",
    )(ctrl, got, prefix, own, other, after)


def merge_kernel(parts_ref, q_ref, kv_ref, out_ref):
    side = lax.axis_index("side")
    tp = lax.axis_index("tp")
    block = side * 8 + tp
    q = q_ref[0, :, :, pl.ds(pl.multiple_of(block * 512, 512), 512)].astype(f32)
    kv = kv_ref[0, :, :, pl.ds(pl.multiple_of((block // 2) * 256, 256), 256)].astype(f32)
    sub = lax.broadcasted_iota(jnp.int32, (ROWS, HD), 0)
    lane = lax.broadcasted_iota(jnp.int32, (ROWS, HD), 1)

    peaks, totals = [], []
    for b in range(8):
        x = parts_ref[b, 128:144].astype(f32)[:ROWS]
        x = x + pltpu.roll(x, HD - 32, 1) + pltpu.roll(x, HD - 64, 1)
        peaks.append(x)
        totals.append(pltpu.roll(x, HD - 16, 1))
    top = functools.reduce(jnp.maximum, peaks)
    fresh = {}
    fresh_top = jnp.full((ROWS, HD), NEG_FILL, f32)
    for t in range(STEPS):
        for h in range(4):
            j = t * 4 + h
            qt = q[t, :, h * HD : (h + 1) * HD]
            for u in range(t + 1):
                s = jnp.sum(qt * kv[u, :, :HD], axis=-1, keepdims=True) * FACTOR
                fresh[j, u] = s
                fresh_top = jnp.where(lane == j, jnp.maximum(fresh_top, s), fresh_top)
    top = jnp.maximum(top, fresh_top)
    scales = [jnp.exp(p - top) for p in peaks]
    total = functools.reduce(jnp.add, [s * t for s, t in zip(scales, totals)])
    first = parts_ref[side * 4 + tp // 2, 144:160].astype(f32)
    for t in range(STEPS):
        for h in range(4):
            j = t * 4 + h
            acc = jnp.zeros((ROWS, HD), f32)
            for b in range(8):
                tile = parts_ref[b, (j // 2) * 16 : (j // 2) * 16 + 16].astype(f32)
                acc += scales[b][:, j : j + 1] * tile[(j % 2) * 8 : (j % 2) * 8 + 8]
            denom = total[:, j : j + 1]
            for u in range(t + 1):
                w = jnp.exp(fresh[j, u] - top[:, j : j + 1])
                acc += w * kv[u, :, HD:]
                denom = denom + w
            out = acc / denom
            out = jnp.where(sub == 0, first[j : j + 1], out)
            out_ref[0, t, :, h * HD : (h + 1) * HD] = out.astype(bf16)


def merge(parts, decode_queries, decode_kv):
    shape = (1, STEPS, ROWS, 512)
    return pl.pallas_call(
        merge_kernel,
        out_shape=jax.ShapeDtypeStruct(shape, bf16),
        grid=(1,),
        in_specs=[whole(parts.shape), whole(decode_queries.shape), whole(decode_kv.shape)],
        out_specs=whole(shape),
        compiler_params=params(8),
        cost_estimate=pl.CostEstimate(flops=3000000, bytes_accessed=1300000, transcendentals=60000),
        name="merge",
    )(parts, decode_queries, decode_kv)


def exchange(x, axis):
    return lax.all_to_all(x, axis, split_axis=0, concat_axis=0, tiled=True)


def local(
    segment_queries,
    segment_kv,
    prefix_kv,
    kv_cache,
    decode_queries,
    decode_kv,
    matching,
    segment_starts,
    cache_lengths,
):
    other_kv = lax.ppermute(segment_kv, "side", [(0, 1), (1, 0)])
    sent, ctrl = prep(matching, segment_starts, decode_queries, decode_kv)
    sent, prefix, own, queries = lax.optimization_barrier(
        (sent, prefix_kv, segment_kv, segment_queries)
    )
    keys = (prefix, own, other_kv)
    cache = (cache_lengths, decode_queries, kv_cache)
    given = decode_parts(*cache, sent, None)
    longest = norms(*keys, given)
    moved, given = lax.optimization_barrier((exchange(sent, "pair"), given))
    theirs = lax.ppermute(given, "side", [(0, 1), (1, 0)])
    first = first_row(ctrl, moved, *keys, longest)
    parts = decode_parts(*cache, first, theirs)
    tokens = (ctrl, queries, *keys, longest)
    out = prompt(PIECES[:EARLY], *tokens, parts, None)
    answered, parts, out = lax.optimization_barrier((exchange(first, "pair"), parts, out))
    swapped = lax.ppermute(answered, "side", [(0, 1), (1, 0)])
    parts = hand_over(ctrl, answered, swapped, parts)
    out = prompt(PIECES[EARLY:], *tokens, parts, out)
    parts = exchange(parts, "tp")
    decode_out = merge(parts, decode_queries, decode_kv)
    return (out, decode_out)


def solution(mesh):
    in_specs = (
        P("pair", "side", "tp"),
        P("pair", "side", "tp"),
        P("pair", None, "tp"),
        P("pair", None, ("side", "tp"), None),
        P("pair", None, None, None),
        P("pair", None, None, None),
        P(),
        P(),
        P("pair", None),
    )
    out_specs = (P("pair", "side", "tp"), P("pair", None, None, ("side", "tp")))
    return jax.shard_map(local, mesh=mesh, in_specs=in_specs, out_specs=out_specs, check_vma=False)
```

```python
import functools
import math

import jax
import jax.numpy as jnp
from jax import lax
from jax.experimental import pallas as pl
from jax.experimental.pallas import tpu as pltpu
from jax.sharding import PartitionSpec as P

H = 64
KVH = 8
HD = 128
STEPS = 4
ROWS = 8
GROUPS = 16
PIECES = [(pair, half) for pair in range(4) for half in range(2)]
EARLY = 2
SEG_HALF = 512
PREFIX = 1024
CACHE_BLOCK = 128

FACTOR = 1.0 / math.sqrt(HD)
LOG2E = 1.4426950408889634
NEG_FILL = -1e30
STAT_ROWS = 144
PART_ROWS = 160

f32 = jnp.float32
bf16 = jnp.bfloat16


def params(mib):
    return pltpu.CompilerParams(vmem_limit_bytes=mib * 1024 * 1024)


def in_hbm(x):
    return pltpu.with_memory_space_constraint(x, pltpu.HBM)


def whole(shape):
    return pl.BlockSpec(shape, lambda *_: (0,) * len(shape))


def dot_t(a, b):
    return lax.dot_general(a, b, (((1,), (1,)), ((), ())), preferred_element_type=f32)


def dot(a, b):
    return jnp.dot(a, b, preferred_element_type=f32)


ASKED = 0
HOLDER = 1
START = 2


def prep_kernel(match_hbm, start_hbm, q_hbm, kv_hbm, out_ref, ctrl_ref, match, starts, q_ref, kv_ref, sems):
    side = lax.axis_index("side")
    tp = lax.axis_index("tp")
    group = lax.axis_index("pair")
    q_col = pl.multiple_of((2 * tp + side) * 512, 512)
    kv_col = pl.multiple_of(tp * 256, 256)
    copies = [
        pltpu.make_async_copy(match_hbm, match, sems.at[0]),
        pltpu.make_async_copy(start_hbm, starts, sems.at[1]),
        pltpu.make_async_copy(q_hbm.at[0, :, :, pl.ds(q_col, 512)], q_ref, sems.at[2]),
        pltpu.make_async_copy(kv_hbm.at[0, :, :, pl.ds(kv_col, 256)], kv_ref, sems.at[3]),
    ]
    for copy in copies:
        copy.start()
    for copy in copies:
        copy.wait()
    q = q_ref[...].astype(f32)
    kv = kv_ref[...].astype(f32)
    rows = [q[t, 0:1, h * HD : (h + 1) * HD] for t in range(STEPS) for h in range(4)]
    rows += [kv[u, 0:1, :HD] for u in range(STEPS)]
    rows += [kv[u, 0:1, HD:] for u in range(STEPS)]
    sent = jnp.concatenate(rows, axis=0).astype(bf16)
    for p in range(GROUPS):
        out_ref[p] = sent

    holder = jnp.int32(0)
    for p in range(GROUPS):
        holder = jnp.where(match[p] == group, p, holder)
    numbers = [match[group], holder, starts[group]]
    sub = lax.broadcasted_iota(jnp.int32, ctrl_ref.shape, 0)
    ctrl = jnp.zeros(ctrl_ref.shape, f32)
    for k, number in enumerate(numbers):
        ctrl = jnp.where(sub == k, number.astype(f32), ctrl)
    ctrl_ref[...] = ctrl


def prep(matching, starts, decode_queries, decode_kv):
    shape = (GROUPS, 24, HD)
    hbm = pl.BlockSpec(memory_space=pltpu.HBM)
    return pl.pallas_call(
        prep_kernel,
        out_shape=(
            jax.ShapeDtypeStruct(shape, bf16),
            jax.ShapeDtypeStruct((ROWS, HD), f32),
        ),
        grid=(1,),
        in_specs=[hbm] * 4,
        out_specs=(whole(shape), whole((ROWS, HD))),
        scratch_shapes=[
            pltpu.SMEM((GROUPS,), jnp.int32),
            pltpu.SMEM((GROUPS,), jnp.int32),
            pltpu.VMEM((STEPS, ROWS, 512), bf16),
            pltpu.VMEM((STEPS, ROWS, 256), bf16),
            pltpu.SemaphoreType.DMA((4,)),
        ],
        compiler_params=params(4),
        cost_estimate=pl.CostEstimate(flops=10000, bytes_accessed=200000, transcendentals=0),
        name="prep",
    )(in_hbm(matching), in_hbm(starts), in_hbm(decode_queries), in_hbm(decode_kv))


def number_of(ctrl_ref, row):
    return jnp.max(ctrl_ref[row : row + 1, :]).astype(jnp.int32)


def decode_kernel(len_ref, q_ref, cache_ref, after_ref, *rest):
    theirs_ref, out_ref = rest if len(rest) == 2 else (None, rest[0])
    block = lax.axis_index("side") * 8 + lax.axis_index("tp")
    sub = lax.broadcasted_iota(jnp.int32, (ROWS, HD), 0)
    lane = lax.broadcasted_iota(jnp.int32, (ROWS, HD), 1)
    lens = jnp.zeros((ROWS, HD), jnp.int32)
    for k in range(ROWS - 1):
        lens = jnp.where(sub == k + 1, len_ref[0:1, k : k + 1], lens)
    allowed = (block * CACHE_BLOCK + lane < lens)[None]
    tiles = STEPS * 8
    small = lane % 32
    row_of = lax.broadcasted_iota(jnp.int32, (tiles * ROWS, HD), 0) % ROWS
    keep = [jnp.where(row_of == k + 1, 1.0, 0.0).astype(bf16) for k in range(ROWS - 1)]

    def spread(x):
        return jnp.concatenate([x * k for k in keep], axis=1)

    scores = []
    for head in range(2):
        q = jnp.concatenate(
            [
                q_ref[0, t, :, (head * 8 + g) * HD : (head * 8 + g + 1) * HD].astype(f32)
                for t in range(STEPS)
                for g in range(8)
            ],
            axis=0,
        ).astype(bf16)
        keys = jnp.concatenate(
            [cache_ref[0, k, :, head * 256 : head * 256 + HD] for k in range(ROWS - 1)], axis=1
        )
        scores.append(dot_t(spread(q), keys).reshape(tiles, ROWS, HD))
    for head in range(2):
        s = jnp.where(allowed, scores[head] * FACTOR, NEG_FILL)
        peak = jnp.max(s, axis=-1, keepdims=True)
        weights = jnp.where(allowed, jnp.exp(s - peak), 0.0)
        values = cache_ref[0, :, :, head * 256 + HD : head * 256 + 256].reshape(-1, HD)
        values = jnp.concatenate([values, jnp.ones_like(values)], axis=1)
        both = dot(spread(weights.reshape(tiles * ROWS, HD).astype(bf16)), values)
        both = both.reshape(STEPS, 8, ROWS, 2 * HD)
        peak = peak.reshape(STEPS, 8, ROWS, 1)
        for half in range(2):
            stats = jnp.zeros((ROWS, HD), f32)
            for t in range(STEPS):
                for h in range(4):
                    j = t * 4 + h
                    stats = jnp.where(small == j, peak[t, half * 4 + h], stats)
                    stats = jnp.where(small == 16 + j, both[t, half * 4 + h, :, HD:], stats)
            slot = head * 2 + half
            mix = both[:, half * 4 : half * 4 + 4, :, :HD].reshape(16, ROWS, HD)
            if theirs_ref is not None:
                other = theirs_ref[slot, 128:144].astype(f32)[:ROWS]
                other = other + pltpu.roll(other, HD - 32, 1) + pltpu.roll(other, HD - 64, 1)
                top = jnp.maximum(stats, other)
                mine, its = jnp.exp(stats - top), jnp.exp(other - top)
                total = mine * pltpu.roll(stats, HD - 16, 1) + its * pltpu.roll(other, HD - 16, 1)
                joined = jnp.where(lane < 16, top, jnp.where(lane < 32, pltpu.roll(total, 16, 1), 0.0))
                stats = joined + pltpu.roll(joined, 32, 1) + pltpu.roll(joined, 64, 1)
                tiles_in = theirs_ref[slot, 0:128].astype(f32).reshape(16, ROWS, HD)
                mix = jnp.stack(
                    [mine[:, j : j + 1] * mix[j] + its[:, j : j + 1] * tiles_in[j] for j in range(16)]
                )
            high = stats.astype(bf16).astype(f32)
            rest_of = stats - high
            mid = rest_of.astype(bf16).astype(f32)
            low = rest_of - mid
            packed = jnp.where(lane < 32, high, jnp.where(lane < 64, mid, low))
            out_ref[slot, 0:128] = mix.reshape(128, HD).astype(bf16)
            out_ref[slot, 128:144] = jnp.concatenate(
                [packed, jnp.zeros((ROWS, HD), f32)], axis=0
            ).astype(bf16)


def decode_parts(cache_lengths, decode_queries, kv_cache, after, theirs):
    rows = STAT_ROWS if theirs is None else PART_ROWS

    def heads(c):
        side = lax.axis_index("side")
        return (0, 0, 0, 2 * (1 - side if theirs is None else side) + c)

    operands = [in_hbm(cache_lengths), in_hbm(decode_queries), in_hbm(kv_cache), after]
    in_specs = [
        whole(cache_lengths.shape),
        pl.BlockSpec((1, STEPS, ROWS, 2048), heads),
        pl.BlockSpec((1, ROWS - 1, CACHE_BLOCK, 512), heads),
        pl.BlockSpec(memory_space=pl.ANY),
    ]
    if theirs is not None:
        operands.append(theirs)
        in_specs.append(pl.BlockSpec((4, STAT_ROWS, HD), lambda c: (c, 0, 0)))
    return pl.pallas_call(
        decode_kernel,
        out_shape=jax.ShapeDtypeStruct((8, rows, HD), bf16),
        grid=(2,),
        in_specs=in_specs,
        out_specs=pl.BlockSpec((4, rows, HD), lambda c: (c, 0, 0)),
        compiler_params=params(16),
        cost_estimate=pl.CostEstimate(
            flops=1000000000, bytes_accessed=2400000, transcendentals=150000
        ),
        name="decode_parts",
    )(*operands)


def hand_over_kernel(ctrl_ref, own_ref, other_ref, parts_in, parts_ref, sems):
    side = lax.axis_index("side")
    tp = lax.axis_index("tp")
    holder = number_of(ctrl_ref, HOLDER)

    @pl.when(tp // 4 == side)
    def _():
        copies = []
        for k, (ref, core) in enumerate(((own_ref, side), (other_ref, 1 - side))):
            target = parts_ref.at[(2 * tp + core) % 8, 144:160]
            copies.append(pltpu.make_async_copy(ref.at[holder], target, sems.at[k]))
        for copy in copies:
            copy.start()
        for copy in copies:
            copy.wait()


def hand_over(ctrl, own, other, parts):
    anywhere = pl.BlockSpec(memory_space=pl.ANY)
    return pl.pallas_call(
        hand_over_kernel,
        out_shape=jax.ShapeDtypeStruct(parts.shape, bf16),
        grid=(1,),
        in_specs=[whole(ctrl.shape), anywhere, anywhere, anywhere],
        out_specs=anywhere,
        scratch_shapes=[pltpu.SemaphoreType.DMA((2,))],
        input_output_aliases={3: 0},
        compiler_params=params(4),
        cost_estimate=pl.CostEstimate(flops=0, bytes_accessed=16384, transcendentals=0),
        name="hand_over",
    )(ctrl, own, other, parts)


def norms_kernel(prefix_ref, own_ref, other_ref, after_ref, longest_ref):
    def norm(ref):
        k = ref[0, :, :HD].astype(f32)
        return jnp.max(jnp.sum(k * k, axis=-1, keepdims=True), axis=0, keepdims=True)

    longest = jnp.maximum(norm(prefix_ref), jnp.maximum(norm(own_ref), norm(other_ref)))
    longest_ref[...] = jnp.broadcast_to(longest, longest_ref.shape)


def norms(prefix, own, other, after):
    return pl.pallas_call(
        norms_kernel,
        out_shape=jax.ShapeDtypeStruct((ROWS, HD), f32),
        grid=(1,),
        in_specs=[
            whole(prefix.shape),
            whole(own.shape),
            whole(other.shape),
            pl.BlockSpec(memory_space=pl.ANY),
        ],
        out_specs=whole((ROWS, HD)),
        compiler_params=params(8),
        cost_estimate=pl.CostEstimate(flops=2000000, bytes_accessed=1000000, transcendentals=0),
        name="norms",
    )(prefix, own, other, after)


def prompt_kernel(
    pieces, ctrl_ref, q_ref, prefix_ref, own_ref, other_ref, longest_ref, after_ref, prior, out_hbm, mixed, least, done, sems
):
    side = lax.axis_index("side")
    tokens = 256
    scale = FACTOR * LOG2E
    longest = longest_ref[0:1, 0:1]
    pos = lax.broadcasted_iota(jnp.int32, (PREFIX, HD), 0).astype(f32)
    kept = jnp.where(pos < ctrl_ref[START : START + 1, :], 1.0, 0.0)
    mixed[SEG_HALF : SEG_HALF + PREFIX, :HD] = (prefix_ref[0, :, HD:].astype(f32) * kept).astype(bf16)
    mixed[SEG_HALF : SEG_HALF + PREFIX, HD:] = kept.astype(bf16)
    ones = jnp.ones((SEG_HALF, HD), bf16)
    mixed[:SEG_HALF] = jnp.concatenate([other_ref[0, :, HD:], ones], axis=1)
    mixed[SEG_HALF + PREFIX :] = jnp.concatenate([own_ref[0, :, HD:], ones], axis=1)
    causal = lax.broadcasted_iota(jnp.int32, (tokens, tokens), 1) <= lax.broadcasted_iota(
        jnp.int32, (tokens, tokens), 0
    )

    def key_parts(half, later):
        parts = []
        if later:
            parts += [(other_ref, n) for n in range(0, SEG_HALF, 256)]
        parts += [(prefix_ref, n) for n in range(0, PREFIX, 256)]
        parts += [(own_ref, n) for n in range(0, (half + 1) * tokens, 256)]
        return parts

    def mix(weights, half, later):
        first = 0 if later else SEG_HALF
        last = SEG_HALF + PREFIX + (half + 1) * tokens
        return dot(jnp.concatenate(weights, axis=1), mixed[first:last])

    def lanes(start, size):
        return pl.ds(start if isinstance(start, int) else pl.multiple_of(start, size), size)

    def queries(half, head):
        cols = lanes(head * HD, HD)
        return q_ref[0, half * tokens : (half + 1) * tokens, cols]

    def block(half, head, later):
        q = queries(half, head)
        wide_q = q.astype(f32)
        norms = jnp.sum(wide_q * wide_q, axis=-1, keepdims=True)
        bound = jnp.sqrt(norms * longest) * scale
        parts = key_parts(half, later)
        weights = []
        for number, (ref, n) in enumerate(parts):
            w = jnp.exp2(dot_t(q, ref[0, n : n + 256, :HD]) * scale - bound)
            if number == len(parts) - 1:
                w = jnp.where(causal, w, 0.0)
            weights.append(w.astype(bf16))
        total = mix(weights, half, later)
        sums = total[:, HD:]
        least[...] = jnp.minimum(least[...], sums)
        return (total[:, :HD] / sums).astype(bf16)

    def block_exact(half, head, later):
        q = queries(half, head)
        parts = key_parts(half, later)
        scores = []
        for number, (ref, n) in enumerate(parts):
            s = dot_t(q, ref[0, n : n + 256, :HD])
            if ref is prefix_ref:
                at = n + lax.broadcasted_iota(jnp.int32, s.shape, 1)
                s = jnp.where(at.astype(f32) < ctrl_ref[START : START + 1, 0:1], s, NEG_FILL)
            if number == len(parts) - 1:
                s = jnp.where(causal, s, NEG_FILL)
            scores.append(s)
        peak = functools.reduce(
            jnp.maximum, [jnp.max(s, axis=-1, keepdims=True) for s in scores]
        )
        weights = [jnp.exp2((s - peak) * scale).astype(bf16) for s in scores]
        total = mix(weights, half, later)
        return (total[:, :HD] / total[:, HD:]).astype(bf16)

    def result_copy(pair, half, slot):
        rows = pl.ds(half * tokens, tokens)
        cols = lanes(pair * 2 * HD, 2 * HD)
        return pltpu.make_async_copy(done.at[slot], out_hbm.at[0, rows, cols], sems.at[slot])

    def piece(one, pair, half, slot, later):
        for head in range(2):
            done[slot, :, head * HD : (head + 1) * HD] = one(half, pair * 2 + head, later)
        result_copy(pair, half, slot).start()

    least[...] = jnp.ones(least.shape, f32)
    for later in (False, True):

        @pl.when(side == int(later))
        def _(later=later):
            for slot, (pair, half) in enumerate(pieces):
                piece(block, pair, half, slot, later)
            loose = jnp.min(least[...]) < 1e-27
            for slot, (pair, half) in enumerate(pieces):
                result_copy(pair, half, slot).wait()

            @pl.when(loose)
            def _():
                for half in range(2):
                    pairs = [pair for pair, h in pieces if h == half]

                    @pl.loop(pairs[0], pairs[-1] + 1)
                    def _(pair):
                        piece(block_exact, pair, half, 0, later)
                        result_copy(pair, half, 0).wait()


def prompt(pieces, ctrl, queries, prefix, own, other, longest, after, prior):
    operands = [ctrl, queries, prefix, own, other, longest, after]
    units = sum(6 + half for _, half in pieces) * 2 if prior is not None else 0
    anywhere = pl.BlockSpec(memory_space=pl.ANY)
    return pl.pallas_call(
        functools.partial(prompt_kernel, pieces),
        out_shape=jax.ShapeDtypeStruct(queries.shape, bf16),
        grid=(1,),
        in_specs=[whole(x.shape) for x in operands[:-1]]
        + [anywhere, pl.BlockSpec(memory_space=pltpu.HBM) if prior is not None else anywhere],
        out_specs=pl.BlockSpec(memory_space=pltpu.HBM),
        scratch_shapes=[
            pltpu.VMEM((2 * SEG_HALF + PREFIX, 2 * HD), bf16),
            pltpu.VMEM((256, HD), f32),
            pltpu.VMEM((len(pieces), 256, 2 * HD), bf16),
            pltpu.SemaphoreType.DMA((len(pieces),)),
        ],
        input_output_aliases={7: 0} if prior is not None else {},
        compiler_params=params(24),
        cost_estimate=pl.CostEstimate(
            flops=units * 256 * 256 * 128 * 6 + 1000, bytes_accessed=1000, transcendentals=0
        ),
        name="prompt",
    )(*operands, after if prior is None else in_hbm(prior))


def first_row_kernel(ctrl_ref, got_ref, prefix_ref, own_ref, other_ref, after_ref, out_ref):
    asked = got_ref[number_of(ctrl_ref, ASKED)].astype(f32)
    q = asked[0:16].astype(bf16)
    fresh = asked[16:24]
    pad = jnp.zeros((12, HD), f32)
    fresh_k = jnp.concatenate([fresh[:4], pad], axis=0).astype(bf16)
    fresh_v = jnp.concatenate([fresh[4:], pad], axis=0).astype(bf16)
    s0 = dot_t(q, prefix_ref[0, :, :HD])
    pos = lax.broadcasted_iota(jnp.int32, s0.shape, 1)
    s0 = jnp.where(pos.astype(f32) < ctrl_ref[START : START + 1, 0:1], s0, NEG_FILL)
    s1 = dot_t(q, own_ref[0, :, :HD])
    s2 = dot_t(q, other_ref[0, :, :HD])
    s3 = dot_t(q, fresh_k)
    step = lax.broadcasted_iota(jnp.int32, s3.shape, 0) // 4
    pos = lax.broadcasted_iota(jnp.int32, s3.shape, 1)
    s3 = jnp.where(pos <= step, s3, NEG_FILL)
    scores = (s0, s1, s2, s3)
    values = (prefix_ref[0, :, HD:], own_ref[0, :, HD:], other_ref[0, :, HD:], fresh_v)
    peak = functools.reduce(jnp.maximum, [jnp.max(s, axis=-1, keepdims=True) for s in scores])
    mix = jnp.zeros((16, HD), f32)
    totals = jnp.zeros((16, 1), f32)
    for s, v in zip(scores, values):
        w = jnp.exp2((s - peak) * (FACTOR * LOG2E))
        totals += jnp.sum(w, axis=-1, keepdims=True)
        mix += dot(w.astype(bf16), v)
    out = (mix / totals).astype(bf16)
    for p in range(GROUPS):
        out_ref[p] = out


def first_row(ctrl, got, prefix, own, other, after):
    shape = (GROUPS, 16, HD)
    return pl.pallas_call(
        first_row_kernel,
        out_shape=jax.ShapeDtypeStruct(shape, bf16),
        grid=(1,),
        in_specs=[
            whole(ctrl.shape),
            whole(got.shape),
            whole(prefix.shape),
            whole(own.shape),
            whole(other.shape),
            pl.BlockSpec(memory_space=pl.ANY),
        ],
        out_specs=whole(shape),
        compiler_params=params(8),
        cost_estimate=pl.CostEstimate(
            flops=20000000, bytes_accessed=1300000, transcendentals=33000
        ),
        name="first_row",
    )(ctrl, got, prefix, own, other, after)


def merge_kernel(parts_ref, q_ref, kv_ref, out_ref):
    side = lax.axis_index("side")
    tp = lax.axis_index("tp")
    block = side * 8 + tp
    q = q_ref[0, :, :, pl.ds(pl.multiple_of(block * 512, 512), 512)].astype(f32)
    kv = kv_ref[0, :, :, pl.ds(pl.multiple_of((block // 2) * 256, 256), 256)].astype(f32)
    sub = lax.broadcasted_iota(jnp.int32, (ROWS, HD), 0)
    lane = lax.broadcasted_iota(jnp.int32, (ROWS, HD), 1)

    peaks, totals = [], []
    for b in range(8):
        x = parts_ref[b, 128:144].astype(f32)[:ROWS]
        x = x + pltpu.roll(x, HD - 32, 1) + pltpu.roll(x, HD - 64, 1)
        peaks.append(x)
        totals.append(pltpu.roll(x, HD - 16, 1))
    top = functools.reduce(jnp.maximum, peaks)
    fresh = {}
    fresh_top = jnp.full((ROWS, HD), NEG_FILL, f32)
    for t in range(STEPS):
        for h in range(4):
            j = t * 4 + h
            qt = q[t, :, h * HD : (h + 1) * HD]
            for u in range(t + 1):
                s = jnp.sum(qt * kv[u, :, :HD], axis=-1, keepdims=True) * FACTOR
                fresh[j, u] = s
                fresh_top = jnp.where(lane == j, jnp.maximum(fresh_top, s), fresh_top)
    top = jnp.maximum(top, fresh_top)
    scales = [jnp.exp(p - top) for p in peaks]
    total = functools.reduce(jnp.add, [s * t for s, t in zip(scales, totals)])
    first = parts_ref[side * 4 + tp // 2, 144:160].astype(f32)
    for t in range(STEPS):
        for h in range(4):
            j = t * 4 + h
            acc = jnp.zeros((ROWS, HD), f32)
            for b in range(8):
                tile = parts_ref[b, (j // 2) * 16 : (j // 2) * 16 + 16].astype(f32)
                acc += scales[b][:, j : j + 1] * tile[(j % 2) * 8 : (j % 2) * 8 + 8]
            denom = total[:, j : j + 1]
            for u in range(t + 1):
                w = jnp.exp(fresh[j, u] - top[:, j : j + 1])
                acc += w * kv[u, :, HD:]
                denom = denom + w
            out = acc / denom
            out = jnp.where(sub == 0, first[j : j + 1], out)
            out_ref[0, t, :, h * HD : (h + 1) * HD] = out.astype(bf16)


def merge(parts, decode_queries, decode_kv):
    shape = (1, STEPS, ROWS, 512)
    return pl.pallas_call(
        merge_kernel,
        out_shape=jax.ShapeDtypeStruct(shape, bf16),
        grid=(1,),
        in_specs=[whole(parts.shape), whole(decode_queries.shape), whole(decode_kv.shape)],
        out_specs=whole(shape),
        compiler_params=params(8),
        cost_estimate=pl.CostEstimate(flops=3000000, bytes_accessed=1300000, transcendentals=60000),
        name="merge",
    )(parts, decode_queries, decode_kv)


def exchange(x, axis):
    return lax.all_to_all(x, axis, split_axis=0, concat_axis=0, tiled=True)


def local(
    segment_queries,
    segment_kv,
    prefix_kv,
    kv_cache,
    decode_queries,
    decode_kv,
    matching,
    segment_starts,
    cache_lengths,
):
    other_kv = lax.ppermute(segment_kv, "side", [(0, 1), (1, 0)])
    sent, ctrl = prep(matching, segment_starts, decode_queries, decode_kv)
    sent, other_kv, prefix, own, queries = lax.optimization_barrier(
        (sent, other_kv, prefix_kv, segment_kv, segment_queries)
    )
    keys = (prefix, own, other_kv)
    cache = (cache_lengths, decode_queries, kv_cache)
    given = decode_parts(*cache, sent, None)
    longest = norms(*keys, given)
    moved, given = lax.optimization_barrier((exchange(sent, "pair"), given))
    first = first_row(ctrl, moved, *keys, longest)
    first, given = lax.optimization_barrier((first, given))
    theirs = lax.ppermute(given, "side", [(0, 1), (1, 0)])
    parts = decode_parts(*cache, first, theirs)
    tokens = (ctrl, queries, *keys, longest)
    out = prompt(PIECES[:EARLY], *tokens, parts, None)
    answered, parts, out = lax.optimization_barrier((exchange(first, "pair"), parts, out))
    swapped = lax.ppermute(answered, "side", [(0, 1), (1, 0)])
    parts = hand_over(ctrl, answered, swapped, parts)
    out = prompt(PIECES[EARLY:], *tokens, parts, out)
    parts = exchange(parts, "tp")
    decode_out = merge(parts, decode_queries, decode_kv)
    return (out, decode_out)


def solution(mesh):
    in_specs = (
        P("pair", "side", "tp"),
        P("pair", "side", "tp"),
        P("pair", None, "tp"),
        P("pair", None, ("side", "tp"), None),
        P("pair", None, None, None),
        P("pair", None, None, None),
        P(),
        P(),
        P("pair", None),
    )
    out_specs = (P("pair", "side", "tp"), P("pair", None, None, ("side", "tp")))
    return jax.shard_map(local, mesh=mesh, in_specs=in_specs, out_specs=out_specs, check_vma=False)
```

```python
import functools
import math

import jax
import jax.numpy as jnp
from jax import lax
from jax.experimental import pallas as pl
from jax.experimental.pallas import tpu as pltpu
from jax.sharding import PartitionSpec as P

H = 64
KVH = 8
HD = 128
STEPS = 4
ROWS = 8
GROUPS = 16
PIECES = [(pair, half) for pair in range(4) for half in range(2)]
EARLY = 2
SEG_HALF = 512
PREFIX = 1024
CACHE_BLOCK = 128

FACTOR = 1.0 / math.sqrt(HD)
LOG2E = 1.4426950408889634
NEG_FILL = -1e30
PART_ROWS = 144

f32 = jnp.float32
bf16 = jnp.bfloat16


def params(mib):
    return pltpu.CompilerParams(vmem_limit_bytes=mib * 1024 * 1024)


def in_hbm(x):
    return pltpu.with_memory_space_constraint(x, pltpu.HBM)


def whole(shape):
    return pl.BlockSpec(shape, lambda *_: (0,) * len(shape))


def dot_t(a, b):
    return lax.dot_general(a, b, (((1,), (1,)), ((), ())), preferred_element_type=f32)


def dot(a, b):
    return jnp.dot(a, b, preferred_element_type=f32)


ASKED = 0
HOLDER = 1
START = 2


def prep_kernel(match_hbm, start_hbm, q_hbm, kv_hbm, out_ref, ctrl_ref, match, starts, q_ref, kv_ref, sems):
    side = lax.axis_index("side")
    tp = lax.axis_index("tp")
    group = lax.axis_index("pair")
    q_col = pl.multiple_of((2 * tp + side) * 512, 512)
    kv_col = pl.multiple_of(tp * 256, 256)
    copies = [
        pltpu.make_async_copy(match_hbm, match, sems.at[0]),
        pltpu.make_async_copy(start_hbm, starts, sems.at[1]),
        pltpu.make_async_copy(q_hbm.at[0, :, :, pl.ds(q_col, 512)], q_ref, sems.at[2]),
        pltpu.make_async_copy(kv_hbm.at[0, :, :, pl.ds(kv_col, 256)], kv_ref, sems.at[3]),
    ]
    for copy in copies:
        copy.start()
    for copy in copies:
        copy.wait()
    q = q_ref[...].astype(f32)
    kv = kv_ref[...].astype(f32)
    rows = [q[t, 0:1, h * HD : (h + 1) * HD] for t in range(STEPS) for h in range(4)]
    rows += [kv[u, 0:1, :HD] for u in range(STEPS)]
    rows += [kv[u, 0:1, HD:] for u in range(STEPS)]
    sent = jnp.concatenate(rows, axis=0).astype(bf16)
    for p in range(GROUPS):
        out_ref[p] = sent

    holder = jnp.int32(0)
    for p in range(GROUPS):
        holder = jnp.where(match[p] == group, p, holder)
    numbers = [match[group], holder, starts[group]]
    sub = lax.broadcasted_iota(jnp.int32, ctrl_ref.shape, 0)
    ctrl = jnp.zeros(ctrl_ref.shape, f32)
    for k, number in enumerate(numbers):
        ctrl = jnp.where(sub == k, number.astype(f32), ctrl)
    ctrl_ref[...] = ctrl


def prep(matching, starts, decode_queries, decode_kv):
    shape = (GROUPS, 24, HD)
    hbm = pl.BlockSpec(memory_space=pltpu.HBM)
    return pl.pallas_call(
        prep_kernel,
        out_shape=(
            jax.ShapeDtypeStruct(shape, bf16),
            jax.ShapeDtypeStruct((ROWS, HD), f32),
        ),
        grid=(1,),
        in_specs=[hbm] * 4,
        out_specs=(whole(shape), whole((ROWS, HD))),
        scratch_shapes=[
            pltpu.SMEM((GROUPS,), jnp.int32),
            pltpu.SMEM((GROUPS,), jnp.int32),
            pltpu.VMEM((STEPS, ROWS, 512), bf16),
            pltpu.VMEM((STEPS, ROWS, 256), bf16),
            pltpu.SemaphoreType.DMA((4,)),
        ],
        compiler_params=params(4),
        cost_estimate=pl.CostEstimate(flops=10000, bytes_accessed=200000, transcendentals=0),
        name="prep",
    )(in_hbm(matching), in_hbm(starts), in_hbm(decode_queries), in_hbm(decode_kv))


def number_of(ctrl_ref, row):
    return jnp.max(ctrl_ref[row : row + 1, :]).astype(jnp.int32)


def decode_kernel(len_ref, q_ref, cache_ref, after_ref, *rest):
    theirs_ref, out_ref = rest if len(rest) == 2 else (None, rest[0])
    block = lax.axis_index("side") * 8 + lax.axis_index("tp")
    sub = lax.broadcasted_iota(jnp.int32, (ROWS, HD), 0)
    lane = lax.broadcasted_iota(jnp.int32, (ROWS, HD), 1)
    lens = jnp.zeros((ROWS, HD), jnp.int32)
    for k in range(ROWS - 1):
        lens = jnp.where(sub == k + 1, len_ref[0:1, k : k + 1], lens)
    allowed = (block * CACHE_BLOCK + lane < lens)[None]
    tiles = STEPS * 8
    small = lane % 32
    row_of = lax.broadcasted_iota(jnp.int32, (tiles * ROWS, HD), 0) % ROWS
    keep = [jnp.where(row_of == k + 1, 1.0, 0.0).astype(bf16) for k in range(ROWS - 1)]

    def spread(x):
        return jnp.concatenate([x * k for k in keep], axis=1)

    scores = []
    for head in range(2):
        q = jnp.concatenate(
            [
                q_ref[0, t, :, (head * 8 + g) * HD : (head * 8 + g + 1) * HD].astype(f32)
                for t in range(STEPS)
                for g in range(8)
            ],
            axis=0,
        ).astype(bf16)
        keys = jnp.concatenate(
            [cache_ref[0, k, :, head * 256 : head * 256 + HD] for k in range(ROWS - 1)], axis=1
        )
        scores.append(dot_t(spread(q), keys).reshape(tiles, ROWS, HD))
    for head in range(2):
        s = jnp.where(allowed, scores[head] * FACTOR, NEG_FILL)
        peak = jnp.max(s, axis=-1, keepdims=True)
        weights = jnp.where(allowed, jnp.exp(s - peak), 0.0)
        values = cache_ref[0, :, :, head * 256 + HD : head * 256 + 256].reshape(-1, HD)
        values = jnp.concatenate([values, jnp.ones_like(values)], axis=1)
        both = dot(spread(weights.reshape(tiles * ROWS, HD).astype(bf16)), values)
        both = both.reshape(STEPS, 8, ROWS, 2 * HD)
        peak = peak.reshape(STEPS, 8, ROWS, 1)
        for half in range(2):
            stats = jnp.zeros((ROWS, HD), f32)
            for t in range(STEPS):
                for h in range(4):
                    j = t * 4 + h
                    stats = jnp.where(small == j, peak[t, half * 4 + h], stats)
                    stats = jnp.where(small == 16 + j, both[t, half * 4 + h, :, HD:], stats)
            slot = head * 2 + half
            mix = both[:, half * 4 : half * 4 + 4, :, :HD].reshape(16, ROWS, HD)
            if theirs_ref is not None:
                other = theirs_ref[slot, 128:144].astype(f32)[:ROWS]
                other = other + pltpu.roll(other, HD - 32, 1) + pltpu.roll(other, HD - 64, 1)
                top = jnp.maximum(stats, other)
                mine, its = jnp.exp(stats - top), jnp.exp(other - top)
                total = mine * pltpu.roll(stats, HD - 16, 1) + its * pltpu.roll(other, HD - 16, 1)
                joined = jnp.where(lane < 16, top, jnp.where(lane < 32, pltpu.roll(total, 16, 1), 0.0))
                stats = joined + pltpu.roll(joined, 32, 1) + pltpu.roll(joined, 64, 1)
                tiles_in = theirs_ref[slot, 0:128].astype(f32).reshape(16, ROWS, HD)
                mix = jnp.stack(
                    [mine[:, j : j + 1] * mix[j] + its[:, j : j + 1] * tiles_in[j] for j in range(16)]
                )
            high = stats.astype(bf16).astype(f32)
            rest_of = stats - high
            mid = rest_of.astype(bf16).astype(f32)
            low = rest_of - mid
            packed = jnp.where(lane < 32, high, jnp.where(lane < 64, mid, low))
            out_ref[slot, 0:128] = mix.reshape(128, HD).astype(bf16)
            out_ref[slot, 128:144] = jnp.concatenate(
                [packed, jnp.zeros((ROWS, HD), f32)], axis=0
            ).astype(bf16)


def decode_parts(cache_lengths, decode_queries, kv_cache, after, theirs):
    def heads(c):
        side = lax.axis_index("side")
        return (0, 0, 0, 2 * (1 - side if theirs is None else side) + c)

    operands = [in_hbm(cache_lengths), in_hbm(decode_queries), in_hbm(kv_cache), after]
    in_specs = [
        whole(cache_lengths.shape),
        pl.BlockSpec((1, STEPS, ROWS, 2048), heads),
        pl.BlockSpec((1, ROWS - 1, CACHE_BLOCK, 512), heads),
        pl.BlockSpec(memory_space=pl.ANY),
    ]
    if theirs is not None:
        operands.append(theirs)
        in_specs.append(pl.BlockSpec((4, PART_ROWS, HD), lambda c: (c, 0, 0)))
    return pl.pallas_call(
        decode_kernel,
        out_shape=jax.ShapeDtypeStruct((8, PART_ROWS, HD), bf16),
        grid=(2,),
        in_specs=in_specs,
        out_specs=pl.BlockSpec((4, PART_ROWS, HD), lambda c: (c, 0, 0)),
        compiler_params=params(16),
        cost_estimate=pl.CostEstimate(
            flops=1000000000, bytes_accessed=2400000, transcendentals=150000
        ),
        name="decode_parts",
    )(*operands)


def norms_kernel(prefix_ref, own_ref, other_ref, after_ref, longest_ref):
    def norm(ref):
        k = ref[0, :, :HD].astype(f32)
        return jnp.max(jnp.sum(k * k, axis=-1, keepdims=True), axis=0, keepdims=True)

    longest = jnp.maximum(norm(prefix_ref), jnp.maximum(norm(own_ref), norm(other_ref)))
    longest_ref[...] = jnp.broadcast_to(longest, longest_ref.shape)


def norms(prefix, own, other, after):
    return pl.pallas_call(
        norms_kernel,
        out_shape=jax.ShapeDtypeStruct((ROWS, HD), f32),
        grid=(1,),
        in_specs=[
            whole(prefix.shape),
            whole(own.shape),
            whole(other.shape),
            pl.BlockSpec(memory_space=pl.ANY),
        ],
        out_specs=whole((ROWS, HD)),
        compiler_params=params(8),
        cost_estimate=pl.CostEstimate(flops=2000000, bytes_accessed=1000000, transcendentals=0),
        name="norms",
    )(prefix, own, other, after)


def prompt_kernel(
    pieces, ctrl_ref, q_ref, prefix_ref, own_ref, other_ref, longest_ref, after_ref, prior, out_hbm, mixed, least, done, sems
):
    side = lax.axis_index("side")
    tokens = 256
    scale = FACTOR * LOG2E
    longest = longest_ref[0:1, 0:1]
    pos = lax.broadcasted_iota(jnp.int32, (PREFIX, HD), 0).astype(f32)
    kept = jnp.where(pos < ctrl_ref[START : START + 1, :], 1.0, 0.0)
    mixed[SEG_HALF : SEG_HALF + PREFIX, :HD] = (prefix_ref[0, :, HD:].astype(f32) * kept).astype(bf16)
    mixed[SEG_HALF : SEG_HALF + PREFIX, HD:] = kept.astype(bf16)
    ones = jnp.ones((SEG_HALF, HD), bf16)
    mixed[:SEG_HALF] = jnp.concatenate([other_ref[0, :, HD:], ones], axis=1)
    mixed[SEG_HALF + PREFIX :] = jnp.concatenate([own_ref[0, :, HD:], ones], axis=1)
    causal = lax.broadcasted_iota(jnp.int32, (tokens, tokens), 1) <= lax.broadcasted_iota(
        jnp.int32, (tokens, tokens), 0
    )

    def key_parts(half, later):
        parts = []
        if later:
            parts += [(other_ref, n) for n in range(0, SEG_HALF, 256)]
        parts += [(prefix_ref, n) for n in range(0, PREFIX, 256)]
        parts += [(own_ref, n) for n in range(0, (half + 1) * tokens, 256)]
        return parts

    def mix(weights, half, later):
        first = 0 if later else SEG_HALF
        last = SEG_HALF + PREFIX + (half + 1) * tokens
        return dot(jnp.concatenate(weights, axis=1), mixed[first:last])

    def lanes(start, size):
        return pl.ds(start if isinstance(start, int) else pl.multiple_of(start, size), size)

    def queries(half, head):
        cols = lanes(head * HD, HD)
        return q_ref[0, half * tokens : (half + 1) * tokens, cols]

    def block(half, head, later):
        q = queries(half, head)
        wide_q = q.astype(f32)
        norms = jnp.sum(wide_q * wide_q, axis=-1, keepdims=True)
        bound = jnp.sqrt(norms * longest) * scale
        parts = key_parts(half, later)
        weights = []
        for number, (ref, n) in enumerate(parts):
            w = jnp.exp2(dot_t(q, ref[0, n : n + 256, :HD]) * scale - bound)
            if number == len(parts) - 1:
                w = jnp.where(causal, w, 0.0)
            weights.append(w.astype(bf16))
        total = mix(weights, half, later)
        sums = total[:, HD:]
        least[...] = jnp.minimum(least[...], sums)
        return (total[:, :HD] / sums).astype(bf16)

    def block_exact(half, head, later):
        q = queries(half, head)
        parts = key_parts(half, later)
        scores = []
        for number, (ref, n) in enumerate(parts):
            s = dot_t(q, ref[0, n : n + 256, :HD])
            if ref is prefix_ref:
                at = n + lax.broadcasted_iota(jnp.int32, s.shape, 1)
                s = jnp.where(at.astype(f32) < ctrl_ref[START : START + 1, 0:1], s, NEG_FILL)
            if number == len(parts) - 1:
                s = jnp.where(causal, s, NEG_FILL)
            scores.append(s)
        peak = functools.reduce(
            jnp.maximum, [jnp.max(s, axis=-1, keepdims=True) for s in scores]
        )
        weights = [jnp.exp2((s - peak) * scale).astype(bf16) for s in scores]
        total = mix(weights, half, later)
        return (total[:, :HD] / total[:, HD:]).astype(bf16)

    def result_copy(pair, half, slot):
        rows = pl.ds(half * tokens, tokens)
        cols = lanes(pair * 2 * HD, 2 * HD)
        return pltpu.make_async_copy(done.at[slot], out_hbm.at[0, rows, cols], sems.at[slot])

    def piece(one, pair, half, slot, later):
        for head in range(2):
            done[slot, :, head * HD : (head + 1) * HD] = one(half, pair * 2 + head, later)
        result_copy(pair, half, slot).start()

    least[...] = jnp.ones(least.shape, f32)
    for later in (False, True):

        @pl.when(side == int(later))
        def _(later=later):
            for slot, (pair, half) in enumerate(pieces):
                piece(block, pair, half, slot, later)
            loose = jnp.min(least[...]) < 1e-27
            for slot, (pair, half) in enumerate(pieces):
                result_copy(pair, half, slot).wait()

            @pl.when(loose)
            def _():
                for half in range(2):
                    pairs = [pair for pair, h in pieces if h == half]

                    @pl.loop(pairs[0], pairs[-1] + 1)
                    def _(pair):
                        piece(block_exact, pair, half, 0, later)
                        result_copy(pair, half, 0).wait()


def prompt(pieces, ctrl, queries, prefix, own, other, longest, after, prior):
    operands = [ctrl, queries, prefix, own, other, longest, after]
    units = sum(6 + half for _, half in pieces) * 2 if prior is not None else 0
    anywhere = pl.BlockSpec(memory_space=pl.ANY)
    return pl.pallas_call(
        functools.partial(prompt_kernel, pieces),
        out_shape=jax.ShapeDtypeStruct(queries.shape, bf16),
        grid=(1,),
        in_specs=[whole(x.shape) for x in operands[:-1]]
        + [anywhere, pl.BlockSpec(memory_space=pltpu.HBM) if prior is not None else anywhere],
        out_specs=pl.BlockSpec(memory_space=pltpu.HBM),
        scratch_shapes=[
            pltpu.VMEM((2 * SEG_HALF + PREFIX, 2 * HD), bf16),
            pltpu.VMEM((256, HD), f32),
            pltpu.VMEM((len(pieces), 256, 2 * HD), bf16),
            pltpu.SemaphoreType.DMA((len(pieces),)),
        ],
        input_output_aliases={7: 0} if prior is not None else {},
        compiler_params=params(24),
        cost_estimate=pl.CostEstimate(
            flops=units * 256 * 256 * 128 * 6 + 1000, bytes_accessed=1000, transcendentals=0
        ),
        name="prompt",
    )(*operands, after if prior is None else in_hbm(prior))


def first_row_kernel(ctrl_ref, got_ref, prefix_ref, own_ref, other_ref, after_ref, out_ref):
    asked = got_ref[number_of(ctrl_ref, ASKED)].astype(f32)
    q = asked[0:16].astype(bf16)
    fresh = asked[16:24]
    pad = jnp.zeros((12, HD), f32)
    fresh_k = jnp.concatenate([fresh[:4], pad], axis=0).astype(bf16)
    fresh_v = jnp.concatenate([fresh[4:], pad], axis=0).astype(bf16)
    s0 = dot_t(q, prefix_ref[0, :, :HD])
    pos = lax.broadcasted_iota(jnp.int32, s0.shape, 1)
    s0 = jnp.where(pos.astype(f32) < ctrl_ref[START : START + 1, 0:1], s0, NEG_FILL)
    s1 = dot_t(q, own_ref[0, :, :HD])
    s2 = dot_t(q, other_ref[0, :, :HD])
    s3 = dot_t(q, fresh_k)
    step = lax.broadcasted_iota(jnp.int32, s3.shape, 0) // 4
    pos = lax.broadcasted_iota(jnp.int32, s3.shape, 1)
    s3 = jnp.where(pos <= step, s3, NEG_FILL)
    scores = (s0, s1, s2, s3)
    values = (prefix_ref[0, :, HD:], own_ref[0, :, HD:], other_ref[0, :, HD:], fresh_v)
    peak = functools.reduce(jnp.maximum, [jnp.max(s, axis=-1, keepdims=True) for s in scores])
    mix = jnp.zeros((16, HD), f32)
    totals = jnp.zeros((16, 1), f32)
    for s, v in zip(scores, values):
        w = jnp.exp2((s - peak) * (FACTOR * LOG2E))
        totals += jnp.sum(w, axis=-1, keepdims=True)
        mix += dot(w.astype(bf16), v)
    out = (mix / totals).astype(bf16)
    for p in range(GROUPS):
        out_ref[p] = out


def first_row(ctrl, got, prefix, own, other, after):
    shape = (GROUPS, 16, HD)
    return pl.pallas_call(
        first_row_kernel,
        out_shape=jax.ShapeDtypeStruct(shape, bf16),
        grid=(1,),
        in_specs=[
            whole(ctrl.shape),
            whole(got.shape),
            whole(prefix.shape),
            whole(own.shape),
            whole(other.shape),
            pl.BlockSpec(memory_space=pl.ANY),
        ],
        out_specs=whole(shape),
        compiler_params=params(8),
        cost_estimate=pl.CostEstimate(
            flops=20000000, bytes_accessed=1300000, transcendentals=33000
        ),
        name="first_row",
    )(ctrl, got, prefix, own, other, after)


def merge_kernel(ctrl_ref, parts_ref, first_ref, q_ref, kv_ref, out_ref):
    block = lax.axis_index("side") * 8 + lax.axis_index("tp")
    q = q_ref[0, :, :, pl.ds(pl.multiple_of(block * 512, 512), 512)].astype(f32)
    kv = kv_ref[0, :, :, pl.ds(pl.multiple_of((block // 2) * 256, 256), 256)].astype(f32)
    sub = lax.broadcasted_iota(jnp.int32, (ROWS, HD), 0)
    lane = lax.broadcasted_iota(jnp.int32, (ROWS, HD), 1)

    peaks, totals = [], []
    for b in range(8):
        x = parts_ref[b, 128:144].astype(f32)[:ROWS]
        x = x + pltpu.roll(x, HD - 32, 1) + pltpu.roll(x, HD - 64, 1)
        peaks.append(x)
        totals.append(pltpu.roll(x, HD - 16, 1))
    top = functools.reduce(jnp.maximum, peaks)
    fresh = {}
    fresh_top = jnp.full((ROWS, HD), NEG_FILL, f32)
    for t in range(STEPS):
        for h in range(4):
            j = t * 4 + h
            qt = q[t, :, h * HD : (h + 1) * HD]
            for u in range(t + 1):
                s = jnp.sum(qt * kv[u, :, :HD], axis=-1, keepdims=True) * FACTOR
                fresh[j, u] = s
                fresh_top = jnp.where(lane == j, jnp.maximum(fresh_top, s), fresh_top)
    top = jnp.maximum(top, fresh_top)
    scales = [jnp.exp(p - top) for p in peaks]
    total = functools.reduce(jnp.add, [s * t for s, t in zip(scales, totals)])
    first = first_ref[number_of(ctrl_ref, HOLDER)].astype(f32)
    for t in range(STEPS):
        for h in range(4):
            j = t * 4 + h
            acc = jnp.zeros((ROWS, HD), f32)
            for b in range(8):
                tile = parts_ref[b, (j // 2) * 16 : (j // 2) * 16 + 16].astype(f32)
                acc += scales[b][:, j : j + 1] * tile[(j % 2) * 8 : (j % 2) * 8 + 8]
            denom = total[:, j : j + 1]
            for u in range(t + 1):
                w = jnp.exp(fresh[j, u] - top[:, j : j + 1])
                acc += w * kv[u, :, HD:]
                denom = denom + w
            out = acc / denom
            out = jnp.where(sub == 0, first[j : j + 1], out)
            out_ref[0, t, :, h * HD : (h + 1) * HD] = out.astype(bf16)


def merge(ctrl, parts, first, decode_queries, decode_kv):
    shape = (1, STEPS, ROWS, 512)
    return pl.pallas_call(
        merge_kernel,
        out_shape=jax.ShapeDtypeStruct(shape, bf16),
        grid=(1,),
        in_specs=[whole(x.shape) for x in (ctrl, parts, first, decode_queries, decode_kv)],
        out_specs=whole(shape),
        compiler_params=params(8),
        cost_estimate=pl.CostEstimate(flops=3000000, bytes_accessed=1300000, transcendentals=60000),
        name="merge",
    )(ctrl, parts, first, decode_queries, decode_kv)


def exchange(x, axis):
    return lax.all_to_all(x, axis, split_axis=0, concat_axis=0, tiled=True)


def local(
    segment_queries,
    segment_kv,
    prefix_kv,
    kv_cache,
    decode_queries,
    decode_kv,
    matching,
    segment_starts,
    cache_lengths,
):
    other_kv = lax.ppermute(segment_kv, "side", [(0, 1), (1, 0)])
    sent, ctrl = prep(matching, segment_starts, decode_queries, decode_kv)
    sent, other_kv, prefix, own, queries = lax.optimization_barrier(
        (sent, other_kv, prefix_kv, segment_kv, segment_queries)
    )
    keys = (prefix, own, other_kv)
    cache = (cache_lengths, decode_queries, kv_cache)
    given = decode_parts(*cache, sent, None)
    longest = norms(*keys, given)
    moved, given = lax.optimization_barrier((exchange(sent, "pair"), given))
    first = first_row(ctrl, moved, *keys, longest)
    first, given = lax.optimization_barrier((first, given))
    theirs = lax.ppermute(given, "side", [(0, 1), (1, 0)])
    parts = decode_parts(*cache, first, theirs)
    tokens = (ctrl, queries, *keys, longest)
    out = prompt(PIECES[:EARLY], *tokens, parts, None)
    answered, parts, out = lax.optimization_barrier((exchange(first, "pair"), parts, out))
    answered = lax.ppermute(
        answered, ("side", "tp"), [(s * 8 + c, 2 * c + s) for s in range(2) for c in range(8)]
    )
    out = prompt(PIECES[EARLY:], *tokens, parts, out)
    parts = exchange(parts, "tp")
    decode_out = merge(ctrl, parts, answered, decode_queries, decode_kv)
    return (out, decode_out)


def solution(mesh):
    in_specs = (
        P("pair", "side", "tp"),
        P("pair", "side", "tp"),
        P("pair", None, "tp"),
        P("pair", None, ("side", "tp"), None),
        P("pair", None, None, None),
        P("pair", None, None, None),
        P(),
        P(),
        P("pair", None),
    )
    out_specs = (P("pair", "side", "tp"), P("pair", None, None, ("side", "tp")))
    return jax.shard_map(local, mesh=mesh, in_specs=in_specs, out_specs=out_specs, check_vma=False)
```

```python
import functools
import math

import jax
import jax.numpy as jnp
from jax import lax
from jax.experimental import pallas as pl
from jax.experimental.pallas import tpu as pltpu
from jax.sharding import PartitionSpec as P

H = 64
KVH = 8
HD = 128
STEPS = 4
ROWS = 8
GROUPS = 16
PIECES = [(pair, half) for pair in range(4) for half in range(2)]
EARLY = 2
LATE = 6
SEG_HALF = 512
PREFIX = 1024
CACHE_BLOCK = 128

FACTOR = 1.0 / math.sqrt(HD)
LOG2E = 1.4426950408889634
NEG_FILL = -1e30
PART_ROWS = 144

f32 = jnp.float32
bf16 = jnp.bfloat16


def params(mib):
    return pltpu.CompilerParams(vmem_limit_bytes=mib * 1024 * 1024)


def in_hbm(x):
    return pltpu.with_memory_space_constraint(x, pltpu.HBM)


def whole(shape):
    return pl.BlockSpec(shape, lambda *_: (0,) * len(shape))


def dot_t(a, b):
    return lax.dot_general(a, b, (((1,), (1,)), ((), ())), preferred_element_type=f32)


def dot(a, b):
    return jnp.dot(a, b, preferred_element_type=f32)


ASKED = 0
HOLDER = 1
START = 2


def prep_kernel(match_hbm, start_hbm, q_hbm, kv_hbm, out_ref, ctrl_ref, match, starts, q_ref, kv_ref, sems):
    side = lax.axis_index("side")
    tp = lax.axis_index("tp")
    group = lax.axis_index("pair")
    q_col = pl.multiple_of((2 * tp + side) * 512, 512)
    kv_col = pl.multiple_of(tp * 256, 256)
    copies = [
        pltpu.make_async_copy(match_hbm, match, sems.at[0]),
        pltpu.make_async_copy(start_hbm, starts, sems.at[1]),
        pltpu.make_async_copy(q_hbm.at[0, :, :, pl.ds(q_col, 512)], q_ref, sems.at[2]),
        pltpu.make_async_copy(kv_hbm.at[0, :, :, pl.ds(kv_col, 256)], kv_ref, sems.at[3]),
    ]
    for copy in copies:
        copy.start()
    for copy in copies:
        copy.wait()
    q = q_ref[...].astype(f32)
    kv = kv_ref[...].astype(f32)
    rows = [q[t, 0:1, h * HD : (h + 1) * HD] for t in range(STEPS) for h in range(4)]
    rows += [kv[u, 0:1, :HD] for u in range(STEPS)]
    rows += [kv[u, 0:1, HD:] for u in range(STEPS)]
    sent = jnp.concatenate(rows, axis=0).astype(bf16)
    for p in range(GROUPS):
        out_ref[p] = sent

    holder = jnp.int32(0)
    for p in range(GROUPS):
        holder = jnp.where(match[p] == group, p, holder)
    numbers = [match[group], holder, starts[group]]
    sub = lax.broadcasted_iota(jnp.int32, ctrl_ref.shape, 0)
    ctrl = jnp.zeros(ctrl_ref.shape, f32)
    for k, number in enumerate(numbers):
        ctrl = jnp.where(sub == k, number.astype(f32), ctrl)
    ctrl_ref[...] = ctrl


def prep(matching, starts, decode_queries, decode_kv):
    shape = (GROUPS, 24, HD)
    hbm = pl.BlockSpec(memory_space=pltpu.HBM)
    return pl.pallas_call(
        prep_kernel,
        out_shape=(
            jax.ShapeDtypeStruct(shape, bf16),
            jax.ShapeDtypeStruct((ROWS, HD), f32),
        ),
        grid=(1,),
        in_specs=[hbm] * 4,
        out_specs=(whole(shape), whole((ROWS, HD))),
        scratch_shapes=[
            pltpu.SMEM((GROUPS,), jnp.int32),
            pltpu.SMEM((GROUPS,), jnp.int32),
            pltpu.VMEM((STEPS, ROWS, 512), bf16),
            pltpu.VMEM((STEPS, ROWS, 256), bf16),
            pltpu.SemaphoreType.DMA((4,)),
        ],
        compiler_params=params(4),
        cost_estimate=pl.CostEstimate(flops=10000, bytes_accessed=200000, transcendentals=0),
        name="prep",
    )(in_hbm(matching), in_hbm(starts), in_hbm(decode_queries), in_hbm(decode_kv))


def number_of(ctrl_ref, row):
    return jnp.max(ctrl_ref[row : row + 1, :]).astype(jnp.int32)


def decode_kernel(len_ref, q_ref, cache_ref, after_ref, *rest):
    theirs_ref, out_ref = rest if len(rest) == 2 else (None, rest[0])
    block = lax.axis_index("side") * 8 + lax.axis_index("tp")
    sub = lax.broadcasted_iota(jnp.int32, (ROWS, HD), 0)
    lane = lax.broadcasted_iota(jnp.int32, (ROWS, HD), 1)
    lens = jnp.zeros((ROWS, HD), jnp.int32)
    for k in range(ROWS - 1):
        lens = jnp.where(sub == k + 1, len_ref[0:1, k : k + 1], lens)
    allowed = (block * CACHE_BLOCK + lane < lens)[None]
    tiles = STEPS * 8
    small = lane % 32
    row_of = lax.broadcasted_iota(jnp.int32, (tiles * ROWS, HD), 0) % ROWS
    keep = [jnp.where(row_of == k + 1, 1.0, 0.0).astype(bf16) for k in range(ROWS - 1)]

    def spread(x):
        return jnp.concatenate([x * k for k in keep], axis=1)

    scores = []
    for head in range(2):
        q = jnp.concatenate(
            [
                q_ref[0, t, :, (head * 8 + g) * HD : (head * 8 + g + 1) * HD].astype(f32)
                for t in range(STEPS)
                for g in range(8)
            ],
            axis=0,
        ).astype(bf16)
        keys = jnp.concatenate(
            [cache_ref[0, k, :, head * 256 : head * 256 + HD] for k in range(ROWS - 1)], axis=1
        )
        scores.append(dot_t(spread(q), keys).reshape(tiles, ROWS, HD))
    for head in range(2):
        s = jnp.where(allowed, scores[head] * FACTOR, NEG_FILL)
        peak = jnp.max(s, axis=-1, keepdims=True)
        weights = jnp.where(allowed, jnp.exp(s - peak), 0.0)
        values = cache_ref[0, :, :, head * 256 + HD : head * 256 + 256].reshape(-1, HD)
        values = jnp.concatenate([values, jnp.ones_like(values)], axis=1)
        both = dot(spread(weights.reshape(tiles * ROWS, HD).astype(bf16)), values)
        both = both.reshape(STEPS, 8, ROWS, 2 * HD)
        peak = peak.reshape(STEPS, 8, ROWS, 1)
        for half in range(2):
            stats = jnp.zeros((ROWS, HD), f32)
            for t in range(STEPS):
                for h in range(4):
                    j = t * 4 + h
                    stats = jnp.where(small == j, peak[t, half * 4 + h], stats)
                    stats = jnp.where(small == 16 + j, both[t, half * 4 + h, :, HD:], stats)
            slot = head * 2 + half
            mix = both[:, half * 4 : half * 4 + 4, :, :HD].reshape(16, ROWS, HD)
            if theirs_ref is not None:
                other = theirs_ref[slot, 128:144].astype(f32)[:ROWS]
                other = other + pltpu.roll(other, HD - 32, 1) + pltpu.roll(other, HD - 64, 1)
                top = jnp.maximum(stats, other)
                mine, its = jnp.exp(stats - top), jnp.exp(other - top)
                total = mine * pltpu.roll(stats, HD - 16, 1) + its * pltpu.roll(other, HD - 16, 1)
                joined = jnp.where(lane < 16, top, jnp.where(lane < 32, pltpu.roll(total, 16, 1), 0.0))
                stats = joined + pltpu.roll(joined, 32, 1) + pltpu.roll(joined, 64, 1)
                tiles_in = theirs_ref[slot, 0:128].astype(f32).reshape(16, ROWS, HD)
                mix = jnp.stack(
                    [mine[:, j : j + 1] * mix[j] + its[:, j : j + 1] * tiles_in[j] for j in range(16)]
                )
            high = stats.astype(bf16).astype(f32)
            rest_of = stats - high
            mid = rest_of.astype(bf16).astype(f32)
            low = rest_of - mid
            packed = jnp.where(lane < 32, high, jnp.where(lane < 64, mid, low))
            out_ref[slot, 0:128] = mix.reshape(128, HD).astype(bf16)
            out_ref[slot, 128:144] = jnp.concatenate(
                [packed, jnp.zeros((ROWS, HD), f32)], axis=0
            ).astype(bf16)


def decode_parts(cache_lengths, decode_queries, kv_cache, after, theirs):
    def heads(c):
        side = lax.axis_index("side")
        return (0, 0, 0, 2 * (1 - side if theirs is None else side) + c)

    operands = [in_hbm(cache_lengths), in_hbm(decode_queries), in_hbm(kv_cache), after]
    in_specs = [
        whole(cache_lengths.shape),
        pl.BlockSpec((1, STEPS, ROWS, 2048), heads),
        pl.BlockSpec((1, ROWS - 1, CACHE_BLOCK, 512), heads),
        pl.BlockSpec(memory_space=pl.ANY),
    ]
    if theirs is not None:
        operands.append(theirs)
        in_specs.append(pl.BlockSpec((4, PART_ROWS, HD), lambda c: (c, 0, 0)))
    return pl.pallas_call(
        decode_kernel,
        out_shape=jax.ShapeDtypeStruct((8, PART_ROWS, HD), bf16),
        grid=(2,),
        in_specs=in_specs,
        out_specs=pl.BlockSpec((4, PART_ROWS, HD), lambda c: (c, 0, 0)),
        compiler_params=params(16),
        cost_estimate=pl.CostEstimate(
            flops=1000000000, bytes_accessed=2400000, transcendentals=150000
        ),
        name="decode_parts",
    )(*operands)


def norms_kernel(prefix_ref, own_ref, other_ref, after_ref, longest_ref):
    def norm(ref):
        k = ref[0, :, :HD].astype(f32)
        return jnp.max(jnp.sum(k * k, axis=-1, keepdims=True), axis=0, keepdims=True)

    longest = jnp.maximum(norm(prefix_ref), jnp.maximum(norm(own_ref), norm(other_ref)))
    longest_ref[...] = jnp.broadcast_to(longest, longest_ref.shape)


def norms(prefix, own, other, after):
    return pl.pallas_call(
        norms_kernel,
        out_shape=jax.ShapeDtypeStruct((ROWS, HD), f32),
        grid=(1,),
        in_specs=[
            whole(prefix.shape),
            whole(own.shape),
            whole(other.shape),
            pl.BlockSpec(memory_space=pl.ANY),
        ],
        out_specs=whole((ROWS, HD)),
        compiler_params=params(8),
        cost_estimate=pl.CostEstimate(flops=2000000, bytes_accessed=1000000, transcendentals=0),
        name="norms",
    )(prefix, own, other, after)


def prompt_kernel(
    pieces, ctrl_ref, q_ref, prefix_ref, own_ref, other_ref, longest_ref, after_ref, prior, out_hbm, mixed, least, done, sems
):
    side = lax.axis_index("side")
    tokens = 256
    scale = FACTOR * LOG2E
    longest = longest_ref[0:1, 0:1]
    pos = lax.broadcasted_iota(jnp.int32, (PREFIX, HD), 0).astype(f32)
    kept = jnp.where(pos < ctrl_ref[START : START + 1, :], 1.0, 0.0)
    mixed[SEG_HALF : SEG_HALF + PREFIX, :HD] = (prefix_ref[0, :, HD:].astype(f32) * kept).astype(bf16)
    mixed[SEG_HALF : SEG_HALF + PREFIX, HD:] = kept.astype(bf16)
    ones = jnp.ones((SEG_HALF, HD), bf16)
    mixed[:SEG_HALF] = jnp.concatenate([other_ref[0, :, HD:], ones], axis=1)
    mixed[SEG_HALF + PREFIX :] = jnp.concatenate([own_ref[0, :, HD:], ones], axis=1)
    causal = lax.broadcasted_iota(jnp.int32, (tokens, tokens), 1) <= lax.broadcasted_iota(
        jnp.int32, (tokens, tokens), 0
    )

    def key_parts(half, later):
        parts = []
        if later:
            parts += [(other_ref, n) for n in range(0, SEG_HALF, 256)]
        parts += [(prefix_ref, n) for n in range(0, PREFIX, 256)]
        parts += [(own_ref, n) for n in range(0, (half + 1) * tokens, 256)]
        return parts

    def mix(weights, half, later):
        first = 0 if later else SEG_HALF
        last = SEG_HALF + PREFIX + (half + 1) * tokens
        return dot(jnp.concatenate(weights, axis=1), mixed[first:last])

    def lanes(start, size):
        return pl.ds(start if isinstance(start, int) else pl.multiple_of(start, size), size)

    def queries(half, head):
        cols = lanes(head * HD, HD)
        return q_ref[0, half * tokens : (half + 1) * tokens, cols]

    def block(half, head, later):
        q = queries(half, head)
        wide_q = q.astype(f32)
        norms = jnp.sum(wide_q * wide_q, axis=-1, keepdims=True)
        bound = jnp.sqrt(norms * longest) * scale
        parts = key_parts(half, later)
        weights = []
        for number, (ref, n) in enumerate(parts):
            w = jnp.exp2(dot_t(q, ref[0, n : n + 256, :HD]) * scale - bound)
            if number == len(parts) - 1:
                w = jnp.where(causal, w, 0.0)
            weights.append(w.astype(bf16))
        total = mix(weights, half, later)
        sums = total[:, HD:]
        least[...] = jnp.minimum(least[...], sums)
        return (total[:, :HD] / sums).astype(bf16)

    def block_exact(half, head, later):
        q = queries(half, head)
        parts = key_parts(half, later)
        scores = []
        for number, (ref, n) in enumerate(parts):
            s = dot_t(q, ref[0, n : n + 256, :HD])
            if ref is prefix_ref:
                at = n + lax.broadcasted_iota(jnp.int32, s.shape, 1)
                s = jnp.where(at.astype(f32) < ctrl_ref[START : START + 1, 0:1], s, NEG_FILL)
            if number == len(parts) - 1:
                s = jnp.where(causal, s, NEG_FILL)
            scores.append(s)
        peak = functools.reduce(
            jnp.maximum, [jnp.max(s, axis=-1, keepdims=True) for s in scores]
        )
        weights = [jnp.exp2((s - peak) * scale).astype(bf16) for s in scores]
        total = mix(weights, half, later)
        return (total[:, :HD] / total[:, HD:]).astype(bf16)

    def result_copy(pair, half, slot):
        rows = pl.ds(half * tokens, tokens)
        cols = lanes(pair * 2 * HD, 2 * HD)
        return pltpu.make_async_copy(done.at[slot], out_hbm.at[0, rows, cols], sems.at[slot])

    def piece(one, pair, half, slot, later):
        for head in range(2):
            done[slot, :, head * HD : (head + 1) * HD] = one(half, pair * 2 + head, later)
        result_copy(pair, half, slot).start()

    least[...] = jnp.ones(least.shape, f32)
    for later in (False, True):

        @pl.when(side == int(later))
        def _(later=later):
            for slot, (pair, half) in enumerate(pieces):
                piece(block, pair, half, slot, later)
            loose = jnp.min(least[...]) < 1e-27
            for slot, (pair, half) in enumerate(pieces):
                result_copy(pair, half, slot).wait()

            @pl.when(loose)
            def _():
                for half in range(2):
                    pairs = [pair for pair, h in pieces if h == half]

                    @pl.loop(pairs[0], pairs[-1] + 1)
                    def _(pair):
                        piece(block_exact, pair, half, 0, later)
                        result_copy(pair, half, 0).wait()


def prompt(pieces, ctrl, queries, prefix, own, other, longest, after, prior):
    operands = [ctrl, queries, prefix, own, other, longest, after]
    units = sum(6 + half for _, half in pieces) * 2 if prior is not None else 0
    anywhere = pl.BlockSpec(memory_space=pl.ANY)
    return pl.pallas_call(
        functools.partial(prompt_kernel, pieces),
        out_shape=jax.ShapeDtypeStruct(queries.shape, bf16),
        grid=(1,),
        in_specs=[whole(x.shape) for x in operands[:-1]]
        + [anywhere, pl.BlockSpec(memory_space=pltpu.HBM) if prior is not None else anywhere],
        out_specs=pl.BlockSpec(memory_space=pltpu.HBM),
        scratch_shapes=[
            pltpu.VMEM((2 * SEG_HALF + PREFIX, 2 * HD), bf16),
            pltpu.VMEM((256, HD), f32),
            pltpu.VMEM((len(pieces), 256, 2 * HD), bf16),
            pltpu.SemaphoreType.DMA((len(pieces),)),
        ],
        input_output_aliases={7: 0} if prior is not None else {},
        compiler_params=params(24),
        cost_estimate=pl.CostEstimate(
            flops=units * 256 * 256 * 128 * 6 + 1000, bytes_accessed=1000, transcendentals=0
        ),
        name="prompt",
    )(*operands, after if prior is None else in_hbm(prior))


def first_row_kernel(ctrl_ref, got_ref, prefix_ref, own_ref, other_ref, after_ref, out_ref):
    asked = got_ref[number_of(ctrl_ref, ASKED)].astype(f32)
    q = asked[0:16].astype(bf16)
    fresh = asked[16:24]
    pad = jnp.zeros((12, HD), f32)
    fresh_k = jnp.concatenate([fresh[:4], pad], axis=0).astype(bf16)
    fresh_v = jnp.concatenate([fresh[4:], pad], axis=0).astype(bf16)
    s0 = dot_t(q, prefix_ref[0, :, :HD])
    pos = lax.broadcasted_iota(jnp.int32, s0.shape, 1)
    s0 = jnp.where(pos.astype(f32) < ctrl_ref[START : START + 1, 0:1], s0, NEG_FILL)
    s1 = dot_t(q, own_ref[0, :, :HD])
    s2 = dot_t(q, other_ref[0, :, :HD])
    s3 = dot_t(q, fresh_k)
    step = lax.broadcasted_iota(jnp.int32, s3.shape, 0) // 4
    pos = lax.broadcasted_iota(jnp.int32, s3.shape, 1)
    s3 = jnp.where(pos <= step, s3, NEG_FILL)
    scores = (s0, s1, s2, s3)
    values = (prefix_ref[0, :, HD:], own_ref[0, :, HD:], other_ref[0, :, HD:], fresh_v)
    peak = functools.reduce(jnp.maximum, [jnp.max(s, axis=-1, keepdims=True) for s in scores])
    mix = jnp.zeros((16, HD), f32)
    totals = jnp.zeros((16, 1), f32)
    for s, v in zip(scores, values):
        w = jnp.exp2((s - peak) * (FACTOR * LOG2E))
        totals += jnp.sum(w, axis=-1, keepdims=True)
        mix += dot(w.astype(bf16), v)
    out = (mix / totals).astype(bf16)
    for p in range(GROUPS):
        out_ref[p] = out


def first_row(ctrl, got, prefix, own, other, after):
    shape = (GROUPS, 16, HD)
    return pl.pallas_call(
        first_row_kernel,
        out_shape=jax.ShapeDtypeStruct(shape, bf16),
        grid=(1,),
        in_specs=[
            whole(ctrl.shape),
            whole(got.shape),
            whole(prefix.shape),
            whole(own.shape),
            whole(other.shape),
            pl.BlockSpec(memory_space=pl.ANY),
        ],
        out_specs=whole(shape),
        compiler_params=params(8),
        cost_estimate=pl.CostEstimate(
            flops=20000000, bytes_accessed=1300000, transcendentals=33000
        ),
        name="first_row",
    )(ctrl, got, prefix, own, other, after)


def merge_kernel(ctrl_ref, parts_ref, first_ref, q_ref, kv_ref, out_ref):
    block = lax.axis_index("side") * 8 + lax.axis_index("tp")
    q = q_ref[0, :, :, pl.ds(pl.multiple_of(block * 512, 512), 512)].astype(f32)
    kv = kv_ref[0, :, :, pl.ds(pl.multiple_of((block // 2) * 256, 256), 256)].astype(f32)
    sub = lax.broadcasted_iota(jnp.int32, (ROWS, HD), 0)
    lane = lax.broadcasted_iota(jnp.int32, (ROWS, HD), 1)

    peaks, totals = [], []
    for b in range(8):
        x = parts_ref[b, 128:144].astype(f32)[:ROWS]
        x = x + pltpu.roll(x, HD - 32, 1) + pltpu.roll(x, HD - 64, 1)
        peaks.append(x)
        totals.append(pltpu.roll(x, HD - 16, 1))
    top = functools.reduce(jnp.maximum, peaks)
    fresh = {}
    fresh_top = jnp.full((ROWS, HD), NEG_FILL, f32)
    for t in range(STEPS):
        for h in range(4):
            j = t * 4 + h
            qt = q[t, :, h * HD : (h + 1) * HD]
            for u in range(t + 1):
                s = jnp.sum(qt * kv[u, :, :HD], axis=-1, keepdims=True) * FACTOR
                fresh[j, u] = s
                fresh_top = jnp.where(lane == j, jnp.maximum(fresh_top, s), fresh_top)
    top = jnp.maximum(top, fresh_top)
    scales = [jnp.exp(p - top) for p in peaks]
    total = functools.reduce(jnp.add, [s * t for s, t in zip(scales, totals)])
    first = first_ref[number_of(ctrl_ref, HOLDER)].astype(f32)
    for t in range(STEPS):
        for h in range(4):
            j = t * 4 + h
            acc = jnp.zeros((ROWS, HD), f32)
            for b in range(8):
                tile = parts_ref[b, (j // 2) * 16 : (j // 2) * 16 + 16].astype(f32)
                acc += scales[b][:, j : j + 1] * tile[(j % 2) * 8 : (j % 2) * 8 + 8]
            denom = total[:, j : j + 1]
            for u in range(t + 1):
                w = jnp.exp(fresh[j, u] - top[:, j : j + 1])
                acc += w * kv[u, :, HD:]
                denom = denom + w
            out = acc / denom
            out = jnp.where(sub == 0, first[j : j + 1], out)
            out_ref[0, t, :, h * HD : (h + 1) * HD] = out.astype(bf16)


def merge(ctrl, parts, first, decode_queries, decode_kv):
    shape = (1, STEPS, ROWS, 512)
    return pl.pallas_call(
        merge_kernel,
        out_shape=jax.ShapeDtypeStruct(shape, bf16),
        grid=(1,),
        in_specs=[whole(x.shape) for x in (ctrl, parts, first, decode_queries, decode_kv)],
        out_specs=whole(shape),
        compiler_params=params(8),
        cost_estimate=pl.CostEstimate(flops=3000000, bytes_accessed=1300000, transcendentals=60000),
        name="merge",
    )(ctrl, parts, first, decode_queries, decode_kv)


def exchange(x, axis):
    return lax.all_to_all(x, axis, split_axis=0, concat_axis=0, tiled=True)


def local(
    segment_queries,
    segment_kv,
    prefix_kv,
    kv_cache,
    decode_queries,
    decode_kv,
    matching,
    segment_starts,
    cache_lengths,
):
    other_kv = lax.ppermute(segment_kv, "side", [(0, 1), (1, 0)])
    sent, ctrl = prep(matching, segment_starts, decode_queries, decode_kv)
    sent, other_kv, prefix, own, queries = lax.optimization_barrier(
        (sent, other_kv, prefix_kv, segment_kv, segment_queries)
    )
    keys = (prefix, own, other_kv)
    cache = (cache_lengths, decode_queries, kv_cache)
    given = decode_parts(*cache, sent, None)
    longest = norms(*keys, given)
    moved, given = lax.optimization_barrier((exchange(sent, "pair"), given))
    first = first_row(ctrl, moved, *keys, longest)
    first, given = lax.optimization_barrier((first, given))
    theirs = lax.ppermute(given, "side", [(0, 1), (1, 0)])
    parts = decode_parts(*cache, first, theirs)
    tokens = (ctrl, queries, *keys, longest)
    out = prompt(PIECES[:EARLY], *tokens, parts, None)
    answered, parts, out = lax.optimization_barrier((exchange(first, "pair"), parts, out))
    out = prompt(PIECES[EARLY:LATE], *tokens, parts, out)
    answered, out = lax.optimization_barrier((answered, out))
    answered = lax.ppermute(
        answered, ("side", "tp"), [(s * 8 + c, 2 * c + s) for s in range(2) for c in range(8)]
    )
    out = prompt(PIECES[LATE:], *tokens, parts, out)
    parts = exchange(parts, "tp")
    decode_out = merge(ctrl, parts, answered, decode_queries, decode_kv)
    return (out, decode_out)


def solution(mesh):
    in_specs = (
        P("pair", "side", "tp"),
        P("pair", "side", "tp"),
        P("pair", None, "tp"),
        P("pair", None, ("side", "tp"), None),
        P("pair", None, None, None),
        P("pair", None, None, None),
        P(),
        P(),
        P("pair", None),
    )
    out_specs = (P("pair", "side", "tp"), P("pair", None, None, ("side", "tp")))
    return jax.shard_map(local, mesh=mesh, in_specs=in_specs, out_specs=out_specs, check_vma=False)
```
